32 devices in a mesh: groups: 2 (over x), ep: 16 (over z, y, core).
Axes of the slice: x: 2, y: 2, z: 4, core: 2. Of those that a mesh axis runs over, the one named last changes fastest.
Arguments:
- queries: bfloat16 [256, 4096], P('groups', 'ep'), parts along dimension 0, may hold values from -35 to 35
- key_values: bfloat16 [256, 256, 512], P(('groups', 'ep')), parts along dimension 0, may hold values from -12 to 12
- lengths: int32 [256], P(('groups', 'ep')), parts along dimension 0, may hold values from 2 to 256
- residual: bfloat16 [256, 3584], P(('groups', 'ep')), parts along dimension 0, may hold values from -25 to 25
- routes: int32 [256, 3], P(('groups', 'ep')), parts along dimension 0, may hold values from 0 to 7, as said below
- gate_weights: bfloat16 [256, 3], P(('groups', 'ep')), parts along dimension 0, may hold values from 0.19921875 to 1
- output_weight: bfloat16 [4096, 3584], P('ep'), may hold values from -0.09375 to 0.09375
- norm_gain: float32 [3584], replicated, may hold values from 0.1 to 1.9
- gate_weight: bfloat16 [24576, 3584], P('ep'), may hold values from -0.09375 to 0.09375
- up_weight: bfloat16 [24576, 3584], P('ep'), may hold values from -0.09375 to 0.09375
- down_weight: bfloat16 [24576, 3584], P('ep'), may hold values from -0.109375 to 0.109375
Outputs:
- layer_output: bfloat16 [256, 3584], P(('groups', 'ep')), parts along dimension 0
The draws below stay inside these ranges and needn't reach their ends.
There are 2 independent parts, one for each index of `groups`. The reference program is written for one: setup_inputs(seed, part) draws one part's arguments, and reference() takes and returns one part's arrays. A program takes and returns all parts, laid end to end along the dimension named above; an argument that names none is the same for every part. Nothing has to cross between parts.
Inputs may be any that keep to these rules, and one draw needn't show every extreme that they name: `routes`: each row names 3 different experts. Among the rows of one index of ep no expert is named by more than 6 rows; one expert, the same for every index, is named by exactly 6 rows of each index, and there the other experts' counts differ by at most one.
All inputs are finite; a program needn't handle non-finite values.
Results may differ from the reference program's by a relative error of at most 0.0056.
Values may be sent and summed in bfloat16 or wider, within the bound.
No kernel may reach another device: no remote copies, remote signals or barrier semaphores. Data moves between devices by JAX's collectives and lax.ppermute only.
A program may use at most 128 MiB of HBM per device.

```python
import jax
import jax.numpy as jnp
from jax import lax

D = 3584
HD = 256
FF = 3072
EXPERTS = 8
TOP = 3
TOK_DEV = 8
CTX = 256
HEADS = 16
ROWS = 128
HID = 1536
CAP = 6
N_EP = 16


def cache_fields(key, align_share):
    seed_keys, seed_values, seed_queries, seed_rows, seed_heads, seed_power = jax.random.split(key, 6)
    key_shape = (ROWS, CTX, HD)
    query_shape = (ROWS, HEADS, HD)
    cached = jnp.clip(jax.random.normal(seed_keys, key_shape), -6.0, 6.0)
    values = 2.0 * jnp.clip(jax.random.normal(seed_values, key_shape), -6.0, 6.0)
    query_field = jnp.clip(jax.random.normal(seed_queries, query_shape), -6.0, 6.0)
    row_flag = jax.random.bernoulli(seed_rows, 0.125, (ROWS,)) & (align_share > 0.5)
    head_flag = jax.random.bernoulli(seed_heads, 0.125, (ROWS, HEADS)) & row_flag[:, None]
    strength = 8.0 + 4.0 * jax.random.randint(seed_power, (ROWS,), 0, 4).astype(jnp.float32)
    leading = cached[:, 0, :]
    second = leading * (1.0 + 2.0 / (strength * HD ** 0.5))[:, None]
    cached = cached.at[:, 1, :].set(jnp.where(row_flag[:, None], second, cached[:, 1, :]))
    query_field = jnp.where(head_flag[:, :, None], strength[:, None, None] * leading[:, None, :], query_field)
    return (jnp.concatenate([cached, values], axis=2), query_field.reshape(ROWS, HEADS * HD))


def draw_key_values(key, part):
    fields = cache_fields(key, 0.0)
    return fields[0].astype(jnp.bfloat16)


def draw_queries(key, part):
    fields = cache_fields(key, 0.0)
    return fields[1].astype(jnp.bfloat16)


def draw_residual(key, part):
    key = jax.random.fold_in(key, 3)
    seed_base = jax.random.fold_in(key, 0)
    drawn = jnp.clip(jax.random.normal(seed_base, (ROWS, D)), -6.0, 6.0)
    return drawn.astype(jnp.bfloat16)


def draw_lengths(key, part):
    key = jax.random.fold_in(key, 5)
    seed_length, seed_pick = jax.random.split(key)
    uniform_int = jax.random.randint(seed_length, (ROWS,), 0, 4096)
    cubed = uniform_int * uniform_int // 4096 * uniform_int // 4096
    drawn = 2 + (CTX - 2) * cubed // 4095
    picked = jax.random.randint(seed_pick, (), 0, ROWS)
    drawn = jnp.where(jnp.arange(ROWS, dtype=jnp.int32) == picked, CTX, drawn)
    return drawn.astype(jnp.int32)


def draw_routes(key, part):
    key = jax.random.fold_in(key, 7)
    seed_hot, seed_blocks = jax.random.split(key)
    hot_expert = jax.random.randint(seed_hot, (), 0, EXPERTS)
    block_keys = jax.random.split(seed_blocks, ROWS // TOK_DEV)

    def one_block(block_key):
        seed_pick, seed_order, seed_offset = jax.random.split(block_key, 3)
        shuffled = jax.random.permutation(seed_pick, TOK_DEV)
        hot_row = (shuffled < CAP).astype(jnp.int32)
        others = (hot_expert + 1 + jax.random.permutation(seed_order, EXPERTS - 1)) % EXPERTS
        offset = jax.random.randint(seed_offset, (), 0, EXPERTS - 1)
        needed = TOP - hot_row
        starts = offset + jnp.cumsum(needed) - needed
        slot_index = jnp.arange(TOP, dtype=jnp.int32)
        position = (starts[:, None] + slot_index[None, :] - hot_row[:, None]) % (EXPERTS - 1)
        chosen = others[position]
        return jnp.where((slot_index[None, :] == 0) & (hot_row[:, None] == 1), hot_expert, chosen)
    return jax.vmap(one_block)(block_keys).reshape(ROWS, TOP).astype(jnp.int32)


def levels(key, dims, shards, least, top_value):
    factor_of = 1.0
    for axis_at, parts in shards:
        steps = jax.random.uniform(jax.random.fold_in(jax.random.fold_in(key, 6), axis_at), (parts,), jnp.float32, least / len(shards), top_value / len(shards))
        factor_of = factor_of * jnp.repeat(jnp.exp(steps), dims[axis_at] // parts).reshape((-1,) + (1,) * (len(dims) - 1 - axis_at))
    return factor_of


def scatter_about(stream_key, extent, width, reach, shards=(), held_as=jnp.bfloat16):
    array = jax.random.normal(stream_key, extent, jnp.float32) * width
    if len(shards) > 0:
        array = levels(stream_key, extent, shards, -0.22, 0.18) * array
    return jnp.clip(array, min=-reach, max=reach).astype(held_as)


def setup_inputs(seed: int = 0, part: int = 0) -> dict:
    key_list = jax.random.split(jax.random.key(seed), 12)
    part_keys = jax.random.split(jax.random.fold_in(key_list[11], part), 12)
    queries = draw_queries(jax.random.fold_in(jax.random.fold_in(key_list[11], part), 71), part)
    key_values = draw_key_values(jax.random.fold_in(jax.random.fold_in(key_list[11], part), 71), part)
    lengths = draw_lengths(jax.random.fold_in(jax.random.fold_in(key_list[11], part), 71), part)
    residual = draw_residual(jax.random.fold_in(jax.random.fold_in(key_list[11], part), 71), part)
    routes = draw_routes(jax.random.fold_in(jax.random.fold_in(key_list[11], part), 71), part)
    gate_weights = jnp.clip(0.19921875 + 0.80078125 * jax.random.uniform(part_keys[5], (ROWS, TOP), jnp.float32) ** levels(part_keys[5], (ROWS, TOP), ((0, 16),), -0.2, 0.2), 0.19921875, 1.0).astype(jnp.bfloat16)
    output_weight = scatter_about(key_list[6], (HEADS * HD, D), (HEADS * HD) ** -0.5, 0.09375, ((0, 16),))
    norm_gain = jnp.clip(1.0 + 0.18 * jax.random.normal(key_list[7], (D,), jnp.float32), 0.1, 1.9)
    gate_weight = scatter_about(key_list[8], (EXPERTS * FF, D), D ** -0.5, 0.09375, ((0, 16),))
    up_weight = scatter_about(key_list[9], (EXPERTS * FF, D), D ** -0.5, 0.09375, ((0, 16),))
    down_weight = scatter_about(key_list[10], (EXPERTS * FF, D), FF ** -0.5, 0.109375, ((0, 16),))
    return {"queries": queries, "key_values": key_values, "lengths": lengths, "residual": residual, "routes": routes, "gate_weights": gate_weights, "output_weight": output_weight, "norm_gain": norm_gain, "gate_weight": gate_weight, "up_weight": up_weight, "down_weight": down_weight}


EPSILON = 1e-05

def reference(queries, key_values, lengths, residual, routes, gate_weights, output_weight, norm_gain, gate_weight, up_weight, down_weight):
    query_heads = queries.reshape(ROWS, HEADS, HD).astype(jnp.float32)
    key_rows = key_values[:, :, :HD].astype(jnp.float32)
    value_rows = key_values[:, :, HD:].astype(jnp.float32)
    scores = jnp.einsum('rhd,rtd->rht', query_heads, key_rows) * HD ** (-0.5)
    live_mask = jnp.arange(CTX, dtype=jnp.int32)[None, None, :] < lengths[:, None, None]
    scores = jnp.where(live_mask, scores, -1e+30)
    row_max = lax.optimization_barrier(jnp.max(scores, axis=2, keepdims=True))
    weights = jnp.exp(scores - row_max)
    prob_rows = (weights / lax.optimization_barrier(jnp.sum(weights, axis=2, keepdims=True))).astype(jnp.bfloat16)
    prob_wide = lax.optimization_barrier(prob_rows).astype(jnp.float32)
    attended = jnp.einsum('rht,rtd->rhd', prob_wide, value_rows).astype(jnp.bfloat16).reshape(ROWS, HEADS * HD)
    middle = residual.astype(jnp.float32) + jnp.dot(attended, output_weight, preferred_element_type=jnp.float32)
    inverse_root = lax.rsqrt(lax.optimization_barrier(jnp.mean(middle * middle, axis=1, keepdims=True)) + EPSILON)
    normed = (middle * inverse_root * norm_gain).astype(jnp.bfloat16)
    expert_span = N_EP // EXPERTS
    gate_wide = gate_weights.astype(jnp.float32)
    combined = jnp.zeros((ROWS, D), jnp.float32)
    for expert in range(EXPERTS):
        first_unit = expert * FF
        gate_rows = gate_weight[first_unit:first_unit + FF]
        up_rows = up_weight[first_unit:first_unit + FF]
        down_rows = down_weight[first_unit:first_unit + FF]
        gate_pre = jnp.dot(normed, gate_rows.T, preferred_element_type=jnp.float32)
        up_pre = jnp.dot(normed, up_rows.T, preferred_element_type=jnp.float32)
        hidden = (jax.nn.silu(gate_pre) * up_pre).astype(jnp.bfloat16)
        hidden_wide = lax.optimization_barrier(hidden).astype(jnp.float32).reshape(ROWS, expert_span, HID)
        down_blocks = down_rows.astype(jnp.float32).reshape(expert_span, HID, D)
        blocks = jnp.einsum('rjh,jhd->rjd', hidden_wide, down_blocks)
        rounded = lax.optimization_barrier(blocks.astype(jnp.bfloat16)).astype(jnp.float32)
        part_sum = lax.optimization_barrier(jnp.sum(rounded, axis=1))
        gate_of = lax.optimization_barrier(jnp.sum(jnp.where(routes == expert, gate_wide, 0.0), axis=1))
        combined = combined + gate_of[:, None] * part_sum
    return (middle + combined).astype(jnp.bfloat16)
```

```python
import jax
import jax.numpy as jnp
from jax import lax
from jax.sharding import PartitionSpec as P

EXPERTS = 8
EPSILON = 1e-05
F32 = jnp.float32
BF16 = jnp.bfloat16


def attend(query_rows, key_values, lengths):
    row_count, context, width = key_values.shape
    head_dim = width // 2
    key_rows = key_values[:, :, :head_dim]
    value_rows = key_values[:, :, head_dim:]
    scores = jnp.einsum(
        "hrd,rtd->rht", query_rows, key_rows, preferred_element_type=F32
    ) * head_dim ** (-0.5)
    positions = lax.broadcasted_iota(jnp.int32, (row_count, 1, context), 2)
    scores = jnp.where(positions < lengths[:, None, None], scores, -1e30)
    row_max = jnp.max(scores, axis=2, keepdims=True)
    weights = jnp.exp(scores - row_max)
    prob_rows = (weights / jnp.sum(weights, axis=2, keepdims=True)).astype(BF16)
    attended = jnp.einsum("rht,rtd->hrd", prob_rows, value_rows, preferred_element_type=F32)
    return attended.astype(BF16)


def swap(x, bit, size):
    return lax.ppermute(x, "ep", [(i, i ^ bit) for i in range(size)])


def rank_bits(size):
    bits, bit = [], 1
    while bit < size:
        bits.append(bit)
        bit *= 2
    return bits


def order_of(bits):
    order = [0]
    for bit in reversed(bits):
        order = order + [o ^ bit for o in order]
    return order


def scatter_sum(parts, bits, size):
    for bit in bits:
        half = parts.shape[0] // 2
        sent = parts[half:].astype(BF16)
        parts = parts[:half].astype(F32) + swap(sent, bit, size).astype(F32)
    return parts[0]


def gather_rows(rows, bits, size):
    gathered = rows[None]
    for bit in reversed(bits):
        gathered = jnp.concatenate([gathered, swap(gathered, bit, size)], axis=0)
    return gathered


def local(
    queries,
    key_values,
    lengths,
    residual,
    routes,
    gate_weights,
    output_weight,
    norm_gain,
    gate_weight,
    up_weight,
    down_weight,
):
    tok = key_values.shape[0]
    head_dim = key_values.shape[2] // 2
    size = lax.axis_size("ep")
    me = lax.axis_index("ep")
    bits = rank_bits(size)
    order = jnp.array(order_of(bits), jnp.int32)
    span = size // EXPERTS
    feature = residual.shape[1]

    expert_ids = jnp.arange(size, dtype=jnp.int32) // span
    matches = routes[:, :, None] == expert_ids[None, None, :]
    gate_by_device = jnp.sum(
        jnp.where(matches, gate_weights.astype(F32)[:, :, None], 0.0), axis=1
    ).astype(BF16)
    gate_payload = jnp.broadcast_to(gate_by_device.T[:, :, None], (size, tok, 128))

    query_rows = lax.all_to_all(
        queries.reshape(size, tok, head_dim), "ep", split_axis=0, concat_axis=0, tiled=True
    )
    attended = attend(query_rows, key_values, lengths)
    head_rows = lax.all_to_all(
        jnp.concatenate([attended, gate_payload], axis=2),
        "ep", split_axis=0, concat_axis=0, tiled=True,
    )
    head_rows = jnp.take(head_rows, me ^ order, axis=0)
    gates = head_rows[:, :, head_dim].reshape(size * tok, 1).astype(F32)
    head_rows = head_rows[:, :, :head_dim].reshape(size * tok, head_dim)
    terms = jnp.dot(head_rows, output_weight, preferred_element_type=F32)
    arrived = scatter_sum(terms.reshape(size, tok, feature), bits, size)
    middle = residual.astype(F32) + arrived
    inverse_root = lax.rsqrt(jnp.mean(middle * middle, axis=1, keepdims=True) + EPSILON)
    normed = (middle * inverse_root * norm_gain).astype(BF16)
    rows = gather_rows(normed, bits, size).reshape(size * tok, feature)
    contract = (((1,), (1,)), ((), ()))
    gate_pre = lax.dot_general(rows, gate_weight, contract, preferred_element_type=F32)
    up_pre = lax.dot_general(rows, up_weight, contract, preferred_element_type=F32)
    hidden = (jax.nn.silu(gate_pre) * up_pre * gates).astype(BF16)
    partial_value = jnp.dot(hidden, down_weight, preferred_element_type=F32)
    combined = scatter_sum(partial_value.reshape(size, tok, feature), bits, size)
    return (middle + combined).astype(BF16)


def solution(mesh):
    in_specs = (
        P("groups", "ep"),
        P(("groups", "ep"), None, None),
        P(("groups", "ep")),
        P(("groups", "ep"), None),
        P(("groups", "ep"), None),
        P(("groups", "ep"), None),
        P("ep", None),
        P(),
        P("ep", None),
        P("ep", None),
        P("ep", None),
    )
    out_specs = P(("groups", "ep"), None)
    return jax.shard_map(local, mesh=mesh, in_specs=in_specs, out_specs=out_specs, check_vma=False)
```

```python
import functools

import jax
import jax.numpy as jnp
from jax import lax
from jax.experimental import pallas as pl
from jax.experimental.pallas import tpu as pltpu
from jax.sharding import PartitionSpec as P

EXPERTS = 8
EPSILON = 1e-05
LANES = 128
F32 = jnp.float32
BF16 = jnp.bfloat16
VMEM_SPEC = pl.BlockSpec(memory_space=pltpu.VMEM)
HBM_SPEC = pl.BlockSpec(memory_space=pltpu.HBM)
SMEM_SPEC = pl.BlockSpec(memory_space=pltpu.SMEM)


def tile_of(extent, most):
    return max(t for t in range(LANES, most + 1, LANES) if extent % t == 0)


def attend_kernel(lengths_ref, routes_ref, shares_ref, query_ref, source_ref, out_ref, cache_ref, sems):
    heads, tok, head_dim = query_ref.shape
    context = cache_ref.shape[1]
    span = heads // EXPERTS
    copies = [
        pltpu.make_async_copy(source_ref.at[row], cache_ref.at[row], sems.at[row])
        for row in range(tok)
    ]
    for copy in copies:
        copy.start()
    rows = heads * tok
    turned = query_ref[...].reshape(rows, head_dim).T
    lane_row = lax.broadcasted_iota(jnp.int32, (context, rows), 1) % tok
    position = lax.broadcasted_iota(jnp.int32, (context, rows), 0)
    scores = jnp.zeros((context, rows), F32)
    live = jnp.zeros((context, rows), jnp.int32)
    for row in range(tok):
        copies[row].wait()
        found = jnp.dot(cache_ref[row, :, :head_dim], turned, preferred_element_type=F32)
        scores = jnp.where(lane_row == row, found, scores)
        live = jnp.where(lane_row == row, lengths_ref[row], live)
    scores = jnp.where(position < live, scores * head_dim ** (-0.5), -1e30)
    weights = jnp.exp(scores - jnp.max(scores, axis=0, keepdims=True))
    prob = (weights / jnp.sum(weights, axis=0, keepdims=True)).T.astype(BF16)
    out_row = lax.broadcasted_iota(jnp.int32, (rows, head_dim), 0) % tok
    attended = jnp.zeros((rows, head_dim), F32)
    for row in range(tok):
        found = jnp.dot(prob, cache_ref[row, :, head_dim:], preferred_element_type=F32)
        attended = jnp.where(out_row == row, found, attended)
    out_ref[:, :, :head_dim] = attended.astype(BF16).reshape(heads, tok, head_dim)
    place = lax.broadcasted_iota(jnp.int32, (rows, LANES), 0)
    expert = place // (tok * span)
    gates = jnp.zeros((rows, LANES), F32)
    for row in range(tok):
        for k in range(routes_ref.shape[1]):
            named = (place % tok == row) & (expert == routes_ref[row, k])
            gates = gates + jnp.where(named, shares_ref[row, k], 0.0)
    out_ref[:, :, head_dim:] = gates.astype(BF16).reshape(heads, tok, LANES)


def attend(lengths, routes, shares, query_rows, cache):
    heads, tok, head_dim = query_rows.shape
    return pl.pallas_call(
        attend_kernel,
        out_shape=jax.ShapeDtypeStruct((heads, tok, head_dim + LANES), BF16),
        in_specs=[SMEM_SPEC] * 3 + [VMEM_SPEC, HBM_SPEC],
        out_specs=VMEM_SPEC,
        scratch_shapes=[
            pltpu.VMEM(cache.shape, cache.dtype),
            pltpu.SemaphoreType.DMA((tok,)),
        ],
        compiler_params=pltpu.CompilerParams(vmem_limit_bytes=8 << 20),
    )(lengths, routes, shares, query_rows, pltpu.with_memory_space_constraint(cache, pltpu.HBM))


def project_kernel(core_ref, rows_ref, weight_ref, kept_ref, sent_ref, gates_ref):
    chips, _, tok, _ = rows_ref.shape
    head_dim = weight_ref.shape[0]
    half = chips * tok
    mine = core_ref[0]
    for place, core, out_ref in ((1, 1 - mine, sent_ref), (0, mine, kept_ref)):
        block = rows_ref[:, pl.ds(core, 1)].reshape(half, head_dim + LANES)
        out_ref[...] = jnp.dot(
            block[:, :head_dim], weight_ref[...], preferred_element_type=F32
        ).astype(out_ref.dtype)
        gates_ref[pl.ds(place * half, half), :] = block[:, head_dim:]


def project(core, rows, weight):
    chips, _, tok, _ = rows.shape
    half = chips * tok
    feature = weight.shape[1]
    return pl.pallas_call(
        project_kernel,
        out_shape=(
            jax.ShapeDtypeStruct((half, feature), F32),
            jax.ShapeDtypeStruct((half, feature), BF16),
            jax.ShapeDtypeStruct((2 * half, LANES), BF16),
        ),
        in_specs=[SMEM_SPEC, VMEM_SPEC, VMEM_SPEC],
        out_specs=(VMEM_SPEC, VMEM_SPEC, VMEM_SPEC),
        compiler_params=pltpu.CompilerParams(vmem_limit_bytes=8 << 20),
    )(core, rows, weight)


def expert_kernel(
    own_ref, other_ref, gates_ref, gate_source, up_source, down_source, kept_ref, sent_ref,
    turned, hidden, gate_ref, up_ref, down_ref, sems,
):
    half = own_ref.shape[0]
    units, feature = gate_ref.shape
    step = tile_of(units, 384)
    wide = tile_of(feature, 896)

    def unit_copies(at):
        rows = pl.ds(at, step)
        return [
            pltpu.make_async_copy(source.at[rows], target.at[rows], sems.at[which, at // step])
            for which, (source, target) in enumerate(((gate_source, gate_ref), (up_source, up_ref)))
        ]

    def down_copy(at):
        columns = pl.ds(at, wide)
        return pltpu.make_async_copy(
            down_source.at[:, columns], down_ref.at[:, columns], sems.at[2, at // wide]
        )

    for at in range(0, units, step):
        for copy in unit_copies(at):
            copy.start()
    for at in range(0, feature, wide):
        down_copy(at).start()
    turned[:, :half] = own_ref[...].T
    turned[:, half:] = other_ref[...].T
    gates = gates_ref[:, :1].astype(F32)
    for at in range(0, units, step):
        for copy in unit_copies(at):
            copy.wait()
        rows = pl.ds(at, step)
        gate_pre = jnp.dot(gate_ref[rows, :], turned[...], preferred_element_type=F32)
        up_pre = jnp.dot(up_ref[rows, :], turned[...], preferred_element_type=F32)
        product = gate_pre / (1.0 + jnp.exp(-gate_pre)) * up_pre
        hidden[:, rows] = (product.T * gates).astype(BF16)
    for at in range(0, feature, wide):
        down_copy(at).wait()
        columns = pl.ds(at, wide)
        part = jnp.dot(hidden[...], down_ref[:, columns], preferred_element_type=F32)
        kept_ref[:, columns] = part[:half]
        sent_ref[:, columns] = part[half:].astype(BF16)


def experts(own, other, gates, gate_weight, up_weight, down_weight):
    half, feature = own.shape
    units = gate_weight.shape[0]
    weights = (gate_weight, up_weight, down_weight)
    return pl.pallas_call(
        expert_kernel,
        out_shape=(
            jax.ShapeDtypeStruct((half, feature), F32),
            jax.ShapeDtypeStruct((half, feature), BF16),
        ),
        in_specs=[VMEM_SPEC] * 3 + [HBM_SPEC] * 3,
        out_specs=(VMEM_SPEC, VMEM_SPEC),
        scratch_shapes=[
            pltpu.VMEM((feature, 2 * half), BF16),
            pltpu.VMEM((2 * half, units), BF16),
        ]
        + [pltpu.VMEM((units, feature), BF16)] * 3
        + [pltpu.SemaphoreType.DMA((3, 8))],
        compiler_params=pltpu.CompilerParams(vmem_limit_bytes=44 << 20),
        cost_estimate=pl.CostEstimate(
            flops=12 * half * feature * units,
            bytes_accessed=6 * units * feature,
            transcendentals=2 * half * units,
        ),
    )(own, other, gates, *[pltpu.with_memory_space_constraint(w, pltpu.HBM) for w in weights])


def local(
    queries,
    key_values,
    lengths,
    residual,
    routes,
    gate_weights,
    output_weight,
    norm_gain,
    gate_weight,
    up_weight,
    down_weight,
):
    tok = key_values.shape[0]
    head_dim = key_values.shape[2] // 2
    size = lax.axis_size("ep")
    chips = size // 2
    core = lax.rem(lax.axis_index("ep"), 2).astype(jnp.int32).reshape(1)
    same_core = [[2 * chip + c for chip in range(chips)] for c in range(2)]
    feature = residual.shape[1]

    def swap_cores(x):
        return lax.ppermute(x, "ep", [(i, i ^ 1) for i in range(size)])

    def sum_over_chips(kept, arrived):
        summed = (kept + arrived.astype(F32)).astype(BF16).reshape(chips, tok, feature)
        blocks = lax.all_to_all(
            summed, "ep", split_axis=0, concat_axis=0, tiled=True, axis_index_groups=same_core
        )
        return jnp.sum(blocks.astype(F32), axis=0)

    query_rows = lax.all_to_all(
        queries.reshape(size, tok, head_dim), "ep", split_axis=0, concat_axis=0, tiled=True
    )
    attended = attend(lengths, routes, gate_weights.astype(F32), query_rows, key_values)
    head_rows = lax.all_to_all(attended, "ep", split_axis=0, concat_axis=0, tiled=True)
    kept, sent, gates = project(
        core, head_rows.reshape(chips, 2, tok, head_dim + LANES), output_weight
    )
    middle = residual.astype(F32) + sum_over_chips(kept, swap_cores(sent))
    inverse_root = lax.rsqrt(jnp.mean(middle * middle, axis=1, keepdims=True) + EPSILON)
    normed = (middle * inverse_root * norm_gain).astype(BF16)
    own = lax.all_to_all(
        jnp.broadcast_to(normed[None], (chips, tok, feature)),
        "ep", split_axis=0, concat_axis=0, tiled=True, axis_index_groups=same_core,
    ).reshape(chips * tok, feature)
    kept, sent = experts(own, swap_cores(own), gates, gate_weight, up_weight, down_weight)
    combined = sum_over_chips(kept, swap_cores(sent))
    return (middle + combined).astype(BF16)


def solution(mesh):
    in_specs = (
        P("groups", "ep"),
        P(("groups", "ep"), None, None),
        P(("groups", "ep")),
        P(("groups", "ep"), None),
        P(("groups", "ep"), None),
        P(("groups", "ep"), None),
        P("ep", None),
        P(),
        P("ep", None),
        P("ep", None),
        P("ep", None),
    )
    out_specs = P(("groups", "ep"), None)
    return jax.shard_map(local, mesh=mesh, in_specs=in_specs, out_specs=out_specs, check_vma=False)
```

```python
import functools

import jax
import jax.numpy as jnp
from jax import lax
from jax.experimental import pallas as pl
from jax.experimental.pallas import tpu as pltpu
from jax.sharding import PartitionSpec as P

EXPERTS = 8
EPSILON = 1e-05
LANES = 128
F32 = jnp.float32
BF16 = jnp.bfloat16
VMEM_SPEC = pl.BlockSpec(memory_space=pltpu.VMEM)
HBM_SPEC = pl.BlockSpec(memory_space=pltpu.HBM)
SMEM_SPEC = pl.BlockSpec(memory_space=pltpu.SMEM)


def tile_of(extent, most):
    return max(t for t in range(LANES, most + 1, LANES) if extent % t == 0)


def fetch_kernel(count, *refs):
    sources, held, sems = refs[:count], refs[-count - 1 : -1], refs[-1]
    copies = [
        pltpu.make_async_copy(source, target, sems.at[at])
        for at, (source, target) in enumerate(zip(sources, held))
    ]
    for copy in copies:
        copy.start()
    for copy in copies:
        copy.wait()


def fetch(*arrays, after=()):
    count = len(arrays)
    return pl.pallas_call(
        functools.partial(fetch_kernel, count),
        out_shape=tuple(pltpu.VMEM(a.shape, a.dtype) for a in arrays),
        in_specs=[HBM_SPEC] * count + [pl.BlockSpec(memory_space=pl.ANY)] * len(after),
        out_specs=(VMEM_SPEC,) * count,
        scratch_shapes=[pltpu.SemaphoreType.DMA((count,))],
        compiler_params=pltpu.CompilerParams(vmem_limit_bytes=1 << 20),
        cost_estimate=pl.CostEstimate(
            flops=0, bytes_accessed=sum(2 * a.size for a in arrays), transcendentals=0
        ),
    )(*[pltpu.with_memory_space_constraint(a, pltpu.HBM) for a in arrays], *after)


def attend_kernel(meta_ref, shares_ref, query_ref, cache_ref, out_ref):
    heads, tok, head_dim = query_ref.shape
    context = cache_ref.shape[1]
    span = heads // EXPERTS
    rows = heads * tok
    turned = query_ref[...].reshape(rows, head_dim).T
    lane_row = lax.rem(lax.broadcasted_iota(jnp.int32, (1, rows), 1), tok)
    position = lax.broadcasted_iota(jnp.int32, (context, rows), 0)
    scores = jnp.zeros((context, rows), F32)
    live = jnp.zeros((1, rows), jnp.int32)
    for row in range(tok):
        found = jnp.dot(cache_ref[row, :, :head_dim], turned, preferred_element_type=F32)
        scores = jnp.where(lane_row == row, found, scores)
        live = jnp.where(lane_row == row, meta_ref[row, 0], live)
    scores = jnp.where(position < live, scores * head_dim ** (-0.5), -1e30)
    weights = jnp.exp(scores - jnp.max(scores, axis=0, keepdims=True))
    prob = (weights / jnp.sum(weights, axis=0, keepdims=True)).T.astype(BF16)
    place = lax.broadcasted_iota(jnp.int32, (rows, 1), 0)
    place_row = lax.rem(place, tok)
    attended = jnp.zeros((rows, head_dim), F32)
    for row in range(tok):
        found = jnp.dot(prob, cache_ref[row, :, head_dim:], preferred_element_type=F32)
        attended = jnp.where(place_row == row, found, attended)
    out_ref[:, :, :head_dim] = attended.astype(BF16).reshape(heads, tok, head_dim)
    expert = place // (tok * span)
    gates = jnp.zeros((rows, 1), F32)
    for row in range(tok):
        for k in range(shares_ref.shape[1]):
            named = (place_row == row) & (expert == meta_ref[row, 1 + k])
            gates = gates + jnp.where(named, shares_ref[row, k], 0.0)
    out_ref[:, :, head_dim:] = (
        jnp.broadcast_to(gates, (rows, LANES)).astype(BF16).reshape(heads, tok, LANES)
    )


def attend(meta, shares, query_rows, cache):
    heads, tok, head_dim = query_rows.shape
    return pl.pallas_call(
        attend_kernel,
        out_shape=jax.ShapeDtypeStruct((heads, tok, head_dim + LANES), BF16),
        in_specs=[SMEM_SPEC] * 2 + [VMEM_SPEC] * 2,
        out_specs=VMEM_SPEC,
        compiler_params=pltpu.CompilerParams(vmem_limit_bytes=8 << 20),
    )(meta, shares, query_rows, cache)


def relative_order(chips):
    order, bit = [0], chips // 2
    while bit:
        order = order + [o ^ bit for o in order]
        bit //= 2
    return order


def project_kernel(place_ref, rows_ref, weight_ref, kept_ref, sent_ref, gates_ref, ordered):
    chips, _, tok, _ = rows_ref.shape
    head_dim = weight_ref.shape[0]
    half = chips * tok
    mine, core = place_ref[0], place_ref[1]
    for part, core_at, out_ref in ((1, 1 - core, sent_ref), (0, core, kept_ref)):
        for at, bits in enumerate(relative_order(chips)):
            ordered[at] = rows_ref[mine ^ bits, core_at]
        block = ordered[...].reshape(half, head_dim + LANES)
        out_ref[...] = jnp.dot(
            block[:, :head_dim], weight_ref[...], preferred_element_type=F32
        ).astype(out_ref.dtype)
        gates_ref[pl.ds(part * half, half), :] = block[:, head_dim:]


def project(place, rows, weight):
    chips, _, tok, width = rows.shape
    half = chips * tok
    feature = weight.shape[1]
    return pl.pallas_call(
        project_kernel,
        out_shape=(
            jax.ShapeDtypeStruct((half, feature), F32),
            jax.ShapeDtypeStruct((half, feature), BF16),
            jax.ShapeDtypeStruct((2 * half, LANES), BF16),
        ),
        in_specs=[SMEM_SPEC, VMEM_SPEC, VMEM_SPEC],
        out_specs=(VMEM_SPEC, VMEM_SPEC, VMEM_SPEC),
        scratch_shapes=[pltpu.VMEM((chips, tok, width), BF16)],
        compiler_params=pltpu.CompilerParams(vmem_limit_bytes=8 << 20),
    )(place, rows, weight)


def norm_kernel(kept_ref, arrived_ref, gain_ref, middle_ref, normed_ref):
    tok = kept_ref.shape[0] // 2
    for block in range(2):
        mine = pl.ds(block * tok, tok)
        total = kept_ref[mine, :].astype(F32) + arrived_ref[1 - block].astype(F32)
        if block == 0:
            middle_ref[...] = total
        scale = lax.rsqrt(jnp.mean(total * total, axis=1, keepdims=True) + EPSILON)
        normed_ref[block] = (total * scale * gain_ref[...]).astype(BF16)


def norm(kept, arrived, gain):
    rows, feature = kept.shape
    tok = rows // 2
    return pl.pallas_call(
        norm_kernel,
        out_shape=(
            jax.ShapeDtypeStruct((tok, feature), F32),
            jax.ShapeDtypeStruct((2, tok, feature), BF16),
        ),
        in_specs=[VMEM_SPEC] * 3,
        out_specs=(VMEM_SPEC, VMEM_SPEC),
        compiler_params=pltpu.CompilerParams(vmem_limit_bytes=4 << 20),
    )(kept, arrived.reshape(2, tok, feature), gain)


def expert_kernel(
    place_ref, own_ref, other_ref, gates_ref, gate_source, up_source, down_source, kept_ref, sent_ref,
    turned, hidden, gate_ref, up_ref, down_ref, sems,
):
    half = own_ref.shape[0]
    units, feature = gate_ref.shape
    step = tile_of(units, 384)
    wide = tile_of(feature, 896)

    def unit_copies(at):
        rows = pl.ds(at, step)
        return [
            pltpu.make_async_copy(source.at[rows], target.at[rows], sems.at[which, at // step])
            for which, (source, target) in enumerate(((gate_source, gate_ref), (up_source, up_ref)))
        ]

    def down_copy(at):
        columns = pl.ds(at, wide)
        return pltpu.make_async_copy(
            down_source.at[:, columns], down_ref.at[:, columns], sems.at[2, at // wide]
        )

    for at in range(0, units, step):
        for copy in unit_copies(at):
            copy.start()
    for at in range(0, feature, wide):
        down_copy(at).start()
    turned[:, :half] = own_ref[...].T
    turned[:, half:] = other_ref[...].T
    gates = gates_ref[:, :1].astype(F32)
    for at in range(0, units, step):
        for copy in unit_copies(at):
            copy.wait()
        rows = pl.ds(at, step)
        gate_pre = jnp.dot(gate_ref[rows, :], turned[...], preferred_element_type=F32)
        up_pre = jnp.dot(up_ref[rows, :], turned[...], preferred_element_type=F32)
        product = gate_pre / (1.0 + jnp.exp(-gate_pre)) * up_pre
        hidden[:, rows] = (product.T * gates).astype(BF16)
    for at in range(0, feature, wide):
        down_copy(at).wait()
        columns = pl.ds(at, wide)
        part = jnp.dot(hidden[...], down_ref[:, columns], preferred_element_type=F32)
        chips, tok, _ = kept_ref.shape
        for at_block, bits in enumerate(relative_order(chips)):
            chip, low = place_ref[0] ^ bits, at_block * tok
            kept_ref[chip, :, columns] = part[low : low + tok]
            sent_ref[chip, :, columns] = part[half + low : half + low + tok].astype(BF16)


def experts(place, chips, own, other, gates, gate_weight, up_weight, down_weight):
    half, feature = own.shape
    units = gate_weight.shape[0]
    weights = (gate_weight, up_weight, down_weight)
    return pl.pallas_call(
        expert_kernel,
        out_shape=(
            jax.ShapeDtypeStruct((chips, half // chips, feature), F32),
            jax.ShapeDtypeStruct((chips, half // chips, feature), BF16),
        ),
        in_specs=[SMEM_SPEC] + [VMEM_SPEC] * 3 + [HBM_SPEC] * 3,
        out_specs=(VMEM_SPEC, VMEM_SPEC),
        scratch_shapes=[
            pltpu.VMEM((feature, 2 * half), BF16),
            pltpu.VMEM((2 * half, units), BF16),
        ]
        + [pltpu.VMEM((units, feature), BF16)] * 3
        + [pltpu.SemaphoreType.DMA((3, 8))],
        compiler_params=pltpu.CompilerParams(vmem_limit_bytes=44 << 20),
        cost_estimate=pl.CostEstimate(
            flops=12 * half * feature * units,
            bytes_accessed=6 * units * feature,
            transcendentals=2 * half * units,
        ),
    )(place, own, other, gates, *[pltpu.with_memory_space_constraint(w, pltpu.HBM) for w in weights])


def local(
    queries,
    key_values,
    lengths,
    residual,
    routes,
    gate_weights,
    output_weight,
    norm_gain,
    gate_weight,
    up_weight,
    down_weight,
):
    tok = key_values.shape[0]
    head_dim = key_values.shape[2] // 2
    size = lax.axis_size("ep")
    chips = size // 2
    me = lax.axis_index("ep").astype(jnp.int32)
    place = jnp.stack([me // 2, me % 2])
    same_core = [[2 * chip + c for chip in range(chips)] for c in range(2)]
    feature = residual.shape[1]

    def swap(x, bit):
        return lax.ppermute(x, "ep", [(i, i ^ bit) for i in range(size)])

    meta = jnp.concatenate([lengths[:, None], routes], axis=1)
    cache, residual_held, gain_held = fetch(
        key_values, residual, norm_gain.reshape(1, feature)
    )
    query_rows = lax.all_to_all(
        queries.reshape(size, tok, head_dim), "ep", split_axis=0, concat_axis=0, tiled=True
    )
    attended = attend(meta, gate_weights.astype(F32), query_rows, cache)
    (output_held,) = fetch(output_weight, after=(attended,))
    head_rows = lax.all_to_all(attended, "ep", split_axis=0, concat_axis=0, tiled=True)
    kept, sent, gates = project(
        place, head_rows.reshape(chips, 2, tok, head_dim + LANES), output_held
    )
    arrived = swap(sent, 1)
    bit = 2
    while bit < chips:
        half = kept.shape[0] // 2
        sent = (kept[half:] + arrived[half:].astype(F32)).astype(BF16)
        kept = kept[:half] + arrived[:half].astype(F32)
        arrived = swap(sent, bit)
        bit *= 2
    summed = kept + arrived.astype(F32)
    summed = summed.at[:tok].add(residual_held.astype(F32)).astype(BF16)
    middle, own = norm(summed, swap(summed, bit), gain_held)
    own = own.reshape(2 * tok, feature)
    bit //= 2
    while bit > 1:
        own = jnp.concatenate([own, swap(own, bit)], axis=0)
        bit //= 2
    kept, sent = experts(
        place, chips, own, swap(own, 1), gates, gate_weight, up_weight, down_weight
    )
    summed = (kept + swap(sent, 1).astype(F32)).astype(BF16)
    blocks = lax.all_to_all(
        summed, "ep", split_axis=0, concat_axis=0, tiled=True, axis_index_groups=same_core
    )
    return (middle + jnp.sum(blocks.astype(F32), axis=0)).astype(BF16)


def solution(mesh):
    in_specs = (
        P("groups", "ep"),
        P(("groups", "ep"), None, None),
        P(("groups", "ep")),
        P(("groups", "ep"), None),
        P(("groups", "ep"), None),
        P(("groups", "ep"), None),
        P("ep", None),
        P(),
        P("ep", None),
        P("ep", None),
        P("ep", None),
    )
    out_specs = P(("groups", "ep"), None)
    return jax.shard_map(local, mesh=mesh, in_specs=in_specs, out_specs=out_specs, check_vma=False)
```

```python
import functools

import jax
import jax.numpy as jnp
from jax import lax
from jax.experimental import pallas as pl
from jax.experimental.pallas import tpu as pltpu
from jax.sharding import PartitionSpec as P

EXPERTS = 8
EPSILON = 1e-05
LANES = 128
F32 = jnp.float32
BF16 = jnp.bfloat16
VMEM_SPEC = pl.BlockSpec(memory_space=pltpu.VMEM)
HBM_SPEC = pl.BlockSpec(memory_space=pltpu.HBM)
SMEM_SPEC = pl.BlockSpec(memory_space=pltpu.SMEM)


def tile_of(extent, most):
    return max(t for t in range(LANES, most + 1, LANES) if extent % t == 0)


def fetch_kernel(count, carried, *refs):
    sources, held, sems = refs[:count], refs[-count - 1 - carried : -1 - carried], refs[-1]
    copies = [
        pltpu.make_async_copy(source, target, sems.at[at])
        for at, (source, target) in enumerate(zip(sources, held))
    ]
    for copy in copies:
        copy.start()
    if carried:
        refs[-2][...] = refs[count][...]
    for copy in copies:
        copy.wait()


def fetch(*arrays, after=(), carry=None):
    count, carried = len(arrays), int(carry is not None)
    carries = (carry,) * carried
    return pl.pallas_call(
        functools.partial(fetch_kernel, count, carried),
        out_shape=tuple(pltpu.VMEM(a.shape, a.dtype) for a in arrays)
        + tuple(jax.ShapeDtypeStruct(c.shape, c.dtype) for c in carries),
        in_specs=[HBM_SPEC] * count
        + [VMEM_SPEC] * carried
        + [pl.BlockSpec(memory_space=pl.ANY)] * len(after),
        out_specs=(VMEM_SPEC,) * (count + carried),
        scratch_shapes=[pltpu.SemaphoreType.DMA((count,))],
        compiler_params=pltpu.CompilerParams(vmem_limit_bytes=4 << 20),
        cost_estimate=pl.CostEstimate(
            flops=0, bytes_accessed=sum(2 * a.size for a in arrays), transcendentals=0
        ),
    )(*[pltpu.with_memory_space_constraint(a, pltpu.HBM) for a in arrays], *carries, *after)


def attend_kernel(lengths_ref, routes_ref, shares_ref, query_ref, cache_ref, out_ref):
    heads, tok, head_dim = query_ref.shape
    context = cache_ref.shape[1]
    span = heads // EXPERTS
    rows = heads * tok
    turned = query_ref[...].reshape(rows, head_dim).T
    lane_row = lax.rem(lax.broadcasted_iota(jnp.int32, (1, rows), 1), tok)
    position = lax.broadcasted_iota(jnp.int32, (context, rows), 0)
    scores = jnp.zeros((context, rows), F32)
    live = jnp.zeros((1, rows), jnp.int32)
    for row in range(tok):
        found = jnp.dot(cache_ref[row, :, :head_dim], turned, preferred_element_type=F32)
        scores = jnp.where(lane_row == row, found, scores)
        live = jnp.where(lane_row == row, lengths_ref[row], live)
    scores = jnp.where(position < live, scores * head_dim ** (-0.5), -1e30)
    weights = jnp.exp(scores - jnp.max(scores, axis=0, keepdims=True))
    prob = (weights / jnp.sum(weights, axis=0, keepdims=True)).T.astype(BF16)
    place = lax.broadcasted_iota(jnp.int32, (rows, 1), 0)
    place_row = lax.rem(place, tok)
    attended = jnp.zeros((rows, head_dim), F32)
    for row in range(tok):
        found = jnp.dot(prob, cache_ref[row, :, head_dim:], preferred_element_type=F32)
        attended = jnp.where(place_row == row, found, attended)
    out_ref[:, :, :head_dim] = attended.astype(BF16).reshape(heads, tok, head_dim)
    expert = place // (tok * span)
    gates = jnp.zeros((rows, 1), F32)
    for row in range(tok):
        for k in range(shares_ref.shape[0]):
            named = (place_row == row) & (expert == routes_ref[k, row])
            gates = gates + jnp.where(named, shares_ref[k, row], 0.0)
    out_ref[:, :, head_dim:] = (
        jnp.broadcast_to(gates, (rows, LANES)).astype(BF16).reshape(heads, tok, LANES)
    )


def attend(lengths, routes, shares, query_rows, cache):
    heads, tok, head_dim = query_rows.shape
    return pl.pallas_call(
        attend_kernel,
        out_shape=jax.ShapeDtypeStruct((heads, tok, head_dim + LANES), BF16),
        in_specs=[SMEM_SPEC] * 3 + [VMEM_SPEC] * 2,
        out_specs=VMEM_SPEC,
        compiler_params=pltpu.CompilerParams(vmem_limit_bytes=8 << 20),
    )(lengths, routes, shares, query_rows, cache)


def relative_order(chips):
    order, bit = [0], chips // 2
    while bit:
        order = order + [o ^ bit for o in order]
        bit //= 2
    return order


def project_kernel(place_ref, rows_ref, weight_ref, kept_ref, sent_ref, gates_ref, ordered):
    chips, _, tok, _ = rows_ref.shape
    head_dim = weight_ref.shape[0]
    half = chips * tok
    mine, core = place_ref[0], place_ref[1]
    for part, core_at, out_ref in ((1, 1 - core, sent_ref), (0, core, kept_ref)):
        for at, bits in enumerate(relative_order(chips)):
            ordered[at] = rows_ref[mine ^ bits, core_at]
        block = ordered[...].reshape(half, head_dim + LANES)
        out_ref[...] = jnp.dot(
            block[:, :head_dim], weight_ref[...], preferred_element_type=F32
        ).astype(out_ref.dtype)
        gates_ref[pl.ds(part * half, half), :] = block[:, head_dim:]


def project(place, rows, weight):
    chips, _, tok, width = rows.shape
    half = chips * tok
    feature = weight.shape[1]
    return pl.pallas_call(
        project_kernel,
        out_shape=(
            jax.ShapeDtypeStruct((half, feature), F32),
            jax.ShapeDtypeStruct((half, feature), BF16),
            jax.ShapeDtypeStruct((2 * half, LANES), BF16),
        ),
        in_specs=[SMEM_SPEC, VMEM_SPEC, VMEM_SPEC],
        out_specs=(VMEM_SPEC, VMEM_SPEC, VMEM_SPEC),
        scratch_shapes=[pltpu.VMEM((chips, tok, width), BF16)],
        compiler_params=pltpu.CompilerParams(vmem_limit_bytes=8 << 20),
    )(place, rows, weight)


def norm_kernel(kept_ref, arrived_ref, gain_ref, middle_ref, normed_ref):
    tok = kept_ref.shape[0] // 2
    for block in range(2):
        mine = pl.ds(block * tok, tok)
        total = kept_ref[mine, :].astype(F32) + arrived_ref[1 - block].astype(F32)
        if block == 0:
            middle_ref[...] = total
        scale = lax.rsqrt(jnp.mean(total * total, axis=1, keepdims=True) + EPSILON)
        normed_ref[block] = (total * scale * gain_ref[...].reshape(1, -1)).astype(BF16)


def norm(kept, arrived, gain):
    rows, feature = kept.shape
    tok = rows // 2
    return pl.pallas_call(
        norm_kernel,
        out_shape=(
            jax.ShapeDtypeStruct((tok, feature), F32),
            jax.ShapeDtypeStruct((2, tok, feature), BF16),
        ),
        in_specs=[VMEM_SPEC] * 3,
        out_specs=(VMEM_SPEC, VMEM_SPEC),
        compiler_params=pltpu.CompilerParams(vmem_limit_bytes=4 << 20),
    )(kept, arrived.reshape(2, tok, feature), gain)


def expert_kernel(
    place_ref, near_ref, far_ref, near_other_ref, far_other_ref, gates_ref, gate_ref, up_source, down_source,
    kept_ref, sent_ref, turned, hidden, up_ref, down_ref, sems,
):
    half = 2 * near_ref.shape[0]
    units, feature = gate_ref.shape
    step = tile_of(units, 384)
    wide = tile_of(feature, 896)

    def up_copy(at):
        rows = pl.ds(at, step)
        return pltpu.make_async_copy(up_source.at[rows], up_ref.at[rows], sems.at[0, at // step])

    def down_copy(at):
        columns = pl.ds(at, wide)
        return pltpu.make_async_copy(
            down_source.at[:, columns], down_ref.at[:, columns], sems.at[1, at // wide]
        )

    for at in range(0, units, step):
        up_copy(at).start()
    for at in range(0, feature, wide):
        down_copy(at).start()
    pieces = (near_ref, far_ref, near_other_ref, far_other_ref)
    turned[...] = jnp.concatenate([piece[...] for piece in pieces], axis=0).T
    gates = gates_ref[:, :1].astype(F32)
    for at in range(0, units, step):
        rows = pl.ds(at, step)
        gate_pre = jnp.dot(gate_ref[rows, :], turned[...], preferred_element_type=F32)
        up_copy(at).wait()
        up_pre = jnp.dot(up_ref[rows, :], turned[...], preferred_element_type=F32)
        product = gate_pre / (1.0 + jnp.exp(-gate_pre)) * up_pre
        hidden[:, rows] = (product.T * gates).astype(BF16)
    for at in range(0, feature, wide):
        down_copy(at).wait()
        columns = pl.ds(at, wide)
        part = jnp.dot(hidden[...], down_ref[:, columns], preferred_element_type=F32)
        chips, tok, _ = kept_ref.shape
        for at_block, bits in enumerate(relative_order(chips)):
            chip, low = place_ref[0] ^ bits, at_block * tok
            kept_ref[chip, :, columns] = part[low : low + tok]
            sent_ref[chip, :, columns] = part[half + low : half + low + tok].astype(BF16)


def experts(place, chips, pieces, gates, gate_weight, up_weight, down_weight):
    half, feature = 2 * pieces[0].shape[0], pieces[0].shape[1]
    units = gate_weight.shape[0]
    weights = (up_weight, down_weight)
    return pl.pallas_call(
        expert_kernel,
        out_shape=(
            jax.ShapeDtypeStruct((chips, half // chips, feature), F32),
            jax.ShapeDtypeStruct((chips, half // chips, feature), BF16),
        ),
        in_specs=[SMEM_SPEC] + [VMEM_SPEC] * 6 + [HBM_SPEC] * 2,
        out_specs=(VMEM_SPEC, VMEM_SPEC),
        scratch_shapes=[
            pltpu.VMEM((feature, 2 * half), BF16),
            pltpu.VMEM((2 * half, units), BF16),
        ]
        + [pltpu.VMEM((units, feature), BF16)] * 2
        + [pltpu.SemaphoreType.DMA((2, 8))],
        compiler_params=pltpu.CompilerParams(vmem_limit_bytes=32 << 20),
        cost_estimate=pl.CostEstimate(
            flops=12 * half * feature * units,
            bytes_accessed=6 * units * feature,
            transcendentals=2 * half * units,
        ),
    )(place, *pieces, gates, gate_weight, *[pltpu.with_memory_space_constraint(w, pltpu.HBM) for w in weights])


def local(
    queries,
    key_values,
    lengths,
    residual,
    routes,
    gate_weights,
    output_weight,
    norm_gain,
    gate_weight,
    up_weight,
    down_weight,
):
    tok = key_values.shape[0]
    head_dim = key_values.shape[2] // 2
    size = lax.axis_size("ep")
    chips = size // 2
    me = lax.axis_index("ep").astype(jnp.int32)
    place = jnp.stack([me // 2, me % 2])
    same_core = [[2 * chip + c for chip in range(chips)] for c in range(2)]

    def swap(x, bit):
        return lax.ppermute(x, "ep", [(i, i ^ bit) for i in range(size)])

    cache, residual_held, gain_held, lengths_held, routes_held = fetch(
        key_values, residual, norm_gain, lengths, routes.T
    )
    query_rows = lax.all_to_all(
        queries.reshape(size, tok, head_dim), "ep", split_axis=0, concat_axis=0, tiled=True
    )
    attended = attend(lengths_held, routes_held, gate_weights.astype(F32).T, query_rows, cache)
    (output_held,) = fetch(output_weight, after=(attended,))
    head_rows = lax.all_to_all(attended, "ep", split_axis=0, concat_axis=0, tiled=True)
    kept, sent, gates = project(
        place, head_rows.reshape(chips, 2, tok, head_dim + LANES), output_held
    )
    arrived = swap(sent, 1)
    bit = 2
    while bit < chips:
        half = kept.shape[0] // 2
        sent = (kept[half:] + arrived[half:].astype(F32)).astype(BF16)
        kept = kept[:half] + arrived[:half].astype(F32)
        arrived = swap(sent, bit)
        bit *= 2
    summed = kept + arrived.astype(F32)
    summed = summed.at[:tok].add(residual_held.astype(F32)).astype(BF16)
    middle, own = norm(summed, swap(summed, bit), gain_held)
    own = own.reshape(2 * tok, -1)
    bit //= 2
    while bit > 2:
        own = jnp.concatenate([own, swap(own, bit)], axis=0)
        bit //= 2
    far = swap(own, bit)
    gate_held, near = fetch(gate_weight, carry=own)
    pieces = (near, far, swap(near, 1), swap(far, 1))
    kept, sent = experts(place, chips, pieces, gates, gate_held, up_weight, down_weight)
    summed = (kept + swap(sent, 1).astype(F32)).astype(BF16)
    blocks = lax.all_to_all(
        summed, "ep", split_axis=0, concat_axis=0, tiled=True, axis_index_groups=same_core
    )
    return (middle + jnp.sum(blocks.astype(F32), axis=0)).astype(BF16)


def solution(mesh):
    in_specs = (
        P("groups", "ep"),
        P(("groups", "ep"), None, None),
        P(("groups", "ep")),
        P(("groups", "ep"), None),
        P(("groups", "ep"), None),
        P(("groups", "ep"), None),
        P("ep", None),
        P(),
        P("ep", None),
        P("ep", None),
        P("ep", None),
    )
    out_specs = P(("groups", "ep"), None)
    return jax.shard_map(local, mesh=mesh, in_specs=in_specs, out_specs=out_specs, check_vma=False)
```

```python
import functools

import jax
import jax.numpy as jnp
from jax import lax
from jax.experimental import pallas as pl
from jax.experimental.pallas import tpu as pltpu
from jax.sharding import PartitionSpec as P

EXPERTS = 8
EPSILON = 1e-05
LANES = 128
F32 = jnp.float32
BF16 = jnp.bfloat16
VMEM_SPEC = pl.BlockSpec(memory_space=pltpu.VMEM)
HBM_SPEC = pl.BlockSpec(memory_space=pltpu.HBM)
SMEM_SPEC = pl.BlockSpec(memory_space=pltpu.SMEM)


def tile_of(extent, most):
    return max(t for t in range(LANES, most + 1, LANES) if extent % t == 0)


def fetch_kernel(count, carried, *refs):
    sources, held, sems = refs[:count], refs[-count - 1 - carried : -1 - carried], refs[-1]
    copies = [
        pltpu.make_async_copy(source, target, sems.at[at])
        for at, (source, target) in enumerate(zip(sources, held))
    ]
    for copy in copies:
        copy.start()
    if carried:
        refs[-2][...] = refs[count][...]
    for copy in copies:
        copy.wait()


def fetch(*arrays, after=(), carry=None):
    count, carried = len(arrays), int(carry is not None)
    carries = (carry,) * carried
    return pl.pallas_call(
        functools.partial(fetch_kernel, count, carried),
        out_shape=tuple(pltpu.VMEM(a.shape, a.dtype) for a in arrays)
        + tuple(jax.ShapeDtypeStruct(c.shape, c.dtype) for c in carries),
        in_specs=[HBM_SPEC] * count
        + [VMEM_SPEC] * carried
        + [pl.BlockSpec(memory_space=pl.ANY)] * len(after),
        out_specs=(VMEM_SPEC,) * (count + carried),
        scratch_shapes=[pltpu.SemaphoreType.DMA((count,))],
        compiler_params=pltpu.CompilerParams(vmem_limit_bytes=4 << 20),
        cost_estimate=pl.CostEstimate(
            flops=0, bytes_accessed=sum(2 * a.size for a in arrays), transcendentals=0
        ),
    )(*[pltpu.with_memory_space_constraint(a, pltpu.HBM) for a in arrays], *carries, *after)


def attend_kernel(lengths_ref, routes_ref, shares_ref, query_ref, cache_ref, out_ref):
    heads, tok, head_dim = query_ref.shape
    context = cache_ref.shape[1]
    span = heads // EXPERTS
    rows = heads * tok
    turned = query_ref[...].reshape(rows, head_dim).T
    lane_row = lax.rem(lax.broadcasted_iota(jnp.int32, (1, rows), 1), tok)
    position = lax.broadcasted_iota(jnp.int32, (context, rows), 0)
    scores = jnp.zeros((context, rows), F32)
    live = jnp.zeros((1, rows), jnp.int32)
    for row in range(tok):
        found = jnp.dot(cache_ref[row, :, :head_dim], turned, preferred_element_type=F32)
        scores = jnp.where(lane_row == row, found, scores)
        live = jnp.where(lane_row == row, lengths_ref[row], live)
    scores = jnp.where(position < live, scores * head_dim ** (-0.5), -1e30)
    weights = jnp.exp(scores - jnp.max(scores, axis=0, keepdims=True))
    prob = (weights / jnp.sum(weights, axis=0, keepdims=True)).T.astype(BF16)
    place = lax.broadcasted_iota(jnp.int32, (rows, 1), 0)
    place_row = lax.rem(place, tok)
    attended = jnp.zeros((rows, head_dim), F32)
    for row in range(tok):
        found = jnp.dot(prob, cache_ref[row, :, head_dim:], preferred_element_type=F32)
        attended = jnp.where(place_row == row, found, attended)
    out_ref[:, :, :head_dim] = attended.astype(BF16).reshape(heads, tok, head_dim)
    expert = place // (tok * span)
    gates = jnp.zeros((rows, 1), F32)
    for row in range(tok):
        for k in range(shares_ref.shape[0]):
            named = (place_row == row) & (expert == routes_ref[k, row])
            gates = gates + jnp.where(named, shares_ref[k, row], 0.0)
    out_ref[:, :, head_dim:] = (
        jnp.broadcast_to(gates, (rows, LANES)).astype(BF16).reshape(heads, tok, LANES)
    )


def attend(lengths, routes, shares, query_rows, cache):
    heads, tok, head_dim = query_rows.shape
    return pl.pallas_call(
        attend_kernel,
        out_shape=jax.ShapeDtypeStruct((heads, tok, head_dim + LANES), BF16),
        in_specs=[SMEM_SPEC] * 3 + [VMEM_SPEC] * 2,
        out_specs=VMEM_SPEC,
        compiler_params=pltpu.CompilerParams(vmem_limit_bytes=8 << 20),
    )(lengths, routes, shares, query_rows, cache)


def relative_order(chips):
    order, bit = [0], chips // 2
    while bit:
        order = order + [o ^ bit for o in order]
        bit //= 2
    return order


def project_kernel(place_ref, rows_ref, weight_ref, kept_ref, sent_ref, gates_ref, ordered):
    chips, _, tok, _ = rows_ref.shape
    head_dim = weight_ref.shape[0]
    half = chips * tok
    mine, core = place_ref[0], place_ref[1]
    for part, core_at, out_ref in ((1, 1 - core, sent_ref), (0, core, kept_ref)):
        for at, bits in enumerate(relative_order(chips)):
            ordered[at] = rows_ref[mine ^ bits, core_at]
        block = ordered[...].reshape(half, head_dim + LANES)
        out_ref[...] = jnp.dot(
            block[:, :head_dim], weight_ref[...], preferred_element_type=F32
        ).astype(out_ref.dtype)
        gates_ref[pl.ds(part * half, half), :] = block[:, head_dim:]


def project(place, rows, weight):
    chips, _, tok, width = rows.shape
    half = chips * tok
    feature = weight.shape[1]
    return pl.pallas_call(
        project_kernel,
        out_shape=(
            jax.ShapeDtypeStruct((half, feature), F32),
            jax.ShapeDtypeStruct((half, feature), BF16),
            jax.ShapeDtypeStruct((2 * half, LANES), BF16),
        ),
        in_specs=[SMEM_SPEC, VMEM_SPEC, VMEM_SPEC],
        out_specs=(VMEM_SPEC, VMEM_SPEC, VMEM_SPEC),
        scratch_shapes=[pltpu.VMEM((chips, tok, width), BF16)],
        compiler_params=pltpu.CompilerParams(vmem_limit_bytes=8 << 20),
    )(place, rows, weight)


def norm_kernel(kept_ref, arrived_ref, gain_ref, middle_ref, normed_ref):
    tok = kept_ref.shape[0] // 2
    for block in range(2):
        mine = pl.ds(block * tok, tok)
        total = kept_ref[mine, :].astype(F32) + arrived_ref[1 - block].astype(F32)
        if block == 0:
            middle_ref[...] = total
        scale = lax.rsqrt(jnp.mean(total * total, axis=1, keepdims=True) + EPSILON)
        normed_ref[block] = (total * scale * gain_ref[...].reshape(1, -1)).astype(BF16)


def norm(kept, arrived, gain):
    rows, feature = kept.shape
    tok = rows // 2
    return pl.pallas_call(
        norm_kernel,
        out_shape=(
            jax.ShapeDtypeStruct((tok, feature), F32),
            jax.ShapeDtypeStruct((2, tok, feature), BF16),
        ),
        in_specs=[VMEM_SPEC] * 3,
        out_specs=(VMEM_SPEC, VMEM_SPEC),
        compiler_params=pltpu.CompilerParams(vmem_limit_bytes=4 << 20),
    )(kept, arrived.reshape(2, tok, feature), gain)


def expert_kernel(
    place_ref, gates_ref, gate_ref, up_source, down_source, *refs
):
    pieces, (kept_ref, sent_ref, turned, hidden, up_ref, down_ref, sems) = refs[:-7], refs[-7:]
    half = turned.shape[1] // 2
    units, feature = gate_ref.shape
    step = tile_of(units, 384)
    wide = tile_of(feature, 896)

    def up_copy(at):
        rows = pl.ds(at, step)
        return pltpu.make_async_copy(up_source.at[rows], up_ref.at[rows], sems.at[0, at // step])

    def down_copy(at):
        columns = pl.ds(at, wide)
        return pltpu.make_async_copy(
            down_source.at[:, columns], down_ref.at[:, columns], sems.at[1, at // wide]
        )

    for at in range(0, units, step):
        up_copy(at).start()
    for at in range(0, feature, wide):
        down_copy(at).start()
    turned[...] = jnp.concatenate([piece[...] for piece in pieces], axis=0).T
    gates = gates_ref[:, :1].astype(F32)
    for at in range(0, units, step):
        rows = pl.ds(at, step)
        gate_pre = jnp.dot(gate_ref[rows, :], turned[...], preferred_element_type=F32)
        up_copy(at).wait()
        up_pre = jnp.dot(up_ref[rows, :], turned[...], preferred_element_type=F32)
        product = gate_pre / (1.0 + jnp.exp(-gate_pre)) * up_pre
        hidden[:, rows] = (product.T * gates).astype(BF16)
    for at in range(0, feature, wide):
        down_copy(at).wait()
        columns = pl.ds(at, wide)
        part = jnp.dot(hidden[...], down_ref[:, columns], preferred_element_type=F32)
        chips, tok, _ = kept_ref.shape
        for at_block, bits in enumerate(relative_order(chips)):
            chip, low = place_ref[0] ^ bits, at_block * tok
            kept_ref[chip, :, columns] = part[low : low + tok]
            sent_ref[chip, :, columns] = part[half + low : half + low + tok].astype(BF16)


def experts(place, chips, pieces, gates, gate_weight, up_weight, down_weight):
    half = sum(piece.shape[0] for piece in pieces) // 2
    feature = gate_weight.shape[1]
    units = gate_weight.shape[0]
    weights = (up_weight, down_weight)
    return pl.pallas_call(
        expert_kernel,
        out_shape=(
            jax.ShapeDtypeStruct((chips, half // chips, feature), F32),
            jax.ShapeDtypeStruct((chips, half // chips, feature), BF16),
        ),
        in_specs=[SMEM_SPEC, VMEM_SPEC, VMEM_SPEC, HBM_SPEC, HBM_SPEC]
        + [VMEM_SPEC] * len(pieces),
        out_specs=(VMEM_SPEC, VMEM_SPEC),
        scratch_shapes=[
            pltpu.VMEM((feature, 2 * half), BF16),
            pltpu.VMEM((2 * half, units), BF16),
        ]
        + [pltpu.VMEM((units, feature), BF16)] * 2
        + [pltpu.SemaphoreType.DMA((2, 8))],
        compiler_params=pltpu.CompilerParams(vmem_limit_bytes=32 << 20),
        cost_estimate=pl.CostEstimate(
            flops=12 * half * feature * units,
            bytes_accessed=6 * units * feature,
            transcendentals=2 * half * units,
        ),
    )(
        place,
        gates,
        gate_weight,
        *[pltpu.with_memory_space_constraint(w, pltpu.HBM) for w in weights],
        *pieces,
    )


def local(
    queries,
    key_values,
    lengths,
    residual,
    routes,
    gate_weights,
    output_weight,
    norm_gain,
    gate_weight,
    up_weight,
    down_weight,
):
    tok = key_values.shape[0]
    head_dim = key_values.shape[2] // 2
    size = lax.axis_size("ep")
    chips = size // 2
    me = lax.axis_index("ep").astype(jnp.int32)
    place = jnp.stack([me // 2, me % 2])
    same_core = [[2 * chip + c for chip in range(chips)] for c in range(2)]

    def swap(x, bit):
        return lax.ppermute(x, "ep", [(i, i ^ bit) for i in range(size)])

    cache, residual_held, gain_held, lengths_held, routes_held = fetch(
        key_values, residual, norm_gain, lengths, routes.T
    )
    query_rows = lax.all_to_all(
        queries.reshape(size, tok, head_dim), "ep", split_axis=0, concat_axis=0, tiled=True
    )
    attended = attend(lengths_held, routes_held, gate_weights.astype(F32).T, query_rows, cache)
    (output_held,) = fetch(output_weight, after=(attended,))
    head_rows = lax.all_to_all(attended, "ep", split_axis=0, concat_axis=0, tiled=True)
    kept, sent, gates = project(
        place, head_rows.reshape(chips, 2, tok, head_dim + LANES), output_held
    )
    arrived = swap(sent, 1)
    quarter = kept.shape[0] // 4
    parts = [
        kept[at : at + quarter] + arrived[at : at + quarter].astype(F32)
        for at in range(0, 4 * quarter, quarter)
    ]
    kept = parts[0]
    for bits, part in ((6, parts[3]), (2, parts[2]), (4, parts[1])):
        kept = kept + swap(part.astype(BF16), bits).astype(F32)
    bit = 8
    while bit < chips:
        half = kept.shape[0] // 2
        sent = kept[half:].astype(BF16)
        kept = kept[:half] + swap(sent, bit).astype(F32)
        bit *= 2
    summed = kept.at[:tok].add(residual_held.astype(F32)).astype(BF16)
    middle, own = norm(summed, swap(summed, bit), gain_held)
    own = own.reshape(2 * tok, -1)
    bit //= 2
    while bit > 4:
        own = jnp.concatenate([own, swap(own, bit)], axis=0)
        bit //= 2
    others = [swap(own, bits) for bits in (4, 2, 6)]
    gate_held, own = fetch(gate_weight, carry=own)
    pieces = [own] + others
    pieces = pieces + [swap(piece, 1) for piece in pieces]
    kept, sent = experts(place, chips, pieces, gates, gate_held, up_weight, down_weight)
    summed = (kept + swap(sent, 1).astype(F32)).astype(BF16)
    blocks = lax.all_to_all(
        summed, "ep", split_axis=0, concat_axis=0, tiled=True, axis_index_groups=same_core
    )
    return (middle + jnp.sum(blocks.astype(F32), axis=0)).astype(BF16)


def solution(mesh):
    in_specs = (
        P("groups", "ep"),
        P(("groups", "ep"), None, None),
        P(("groups", "ep")),
        P(("groups", "ep"), None),
        P(("groups", "ep"), None),
        P(("groups", "ep"), None),
        P("ep", None),
        P(),
        P("ep", None),
        P("ep", None),
        P("ep", None),
    )
    out_specs = P(("groups", "ep"), None)
    return jax.shard_map(local, mesh=mesh, in_specs=in_specs, out_specs=out_specs, check_vma=False)
```

```python
import functools

import jax
import jax.numpy as jnp
from jax import lax
from jax.experimental import pallas as pl
from jax.experimental.pallas import tpu as pltpu
from jax.sharding import PartitionSpec as P

EXPERTS = 8
EPSILON = 1e-05
LANES = 128
F32 = jnp.float32
BF16 = jnp.bfloat16
VMEM_SPEC = pl.BlockSpec(memory_space=pltpu.VMEM)
HBM_SPEC = pl.BlockSpec(memory_space=pltpu.HBM)
SMEM_SPEC = pl.BlockSpec(memory_space=pltpu.SMEM)


def tile_of(extent, most):
    return max(t for t in range(LANES, most + 1, LANES) if extent % t == 0)


def fetch_kernel(count, carried, *refs):
    sources, held, sems = refs[:count], refs[-count - 1 - carried : -1 - carried], refs[-1]
    copies = [
        pltpu.make_async_copy(source, target, sems.at[at])
        for at, (source, target) in enumerate(zip(sources, held))
    ]
    for copy in copies:
        copy.start()
    if carried:
        refs[-2][...] = refs[count][...]
    for copy in copies:
        copy.wait()


def fetch(*arrays, after=(), carry=None):
    count, carried = len(arrays), int(carry is not None)
    carries = (carry,) * carried
    return pl.pallas_call(
        functools.partial(fetch_kernel, count, carried),
        out_shape=tuple(pltpu.VMEM(a.shape, a.dtype) for a in arrays)
        + tuple(jax.ShapeDtypeStruct(c.shape, c.dtype) for c in carries),
        in_specs=[HBM_SPEC] * count
        + [VMEM_SPEC] * carried
        + [pl.BlockSpec(memory_space=pl.ANY)] * len(after),
        out_specs=(VMEM_SPEC,) * (count + carried),
        scratch_shapes=[pltpu.SemaphoreType.DMA((count,))],
        compiler_params=pltpu.CompilerParams(vmem_limit_bytes=4 << 20),
        cost_estimate=pl.CostEstimate(
            flops=0, bytes_accessed=sum(2 * a.size for a in arrays), transcendentals=0
        ),
    )(*[pltpu.with_memory_space_constraint(a, pltpu.HBM) for a in arrays], *carries, *after)


def attend_kernel(lengths_ref, routes_ref, shares_ref, query_ref, cache_ref, out_ref):
    heads, tok, head_dim = query_ref.shape
    context = cache_ref.shape[1]
    span = heads // EXPERTS
    rows = heads * tok
    turned = query_ref[...].reshape(rows, head_dim).T
    lane_row = lax.rem(lax.broadcasted_iota(jnp.int32, (1, rows), 1), tok)
    position = lax.broadcasted_iota(jnp.int32, (context, rows), 0)
    scores = jnp.zeros((context, rows), F32)
    live = jnp.zeros((1, rows), jnp.int32)
    for row in range(tok):
        found = jnp.dot(cache_ref[row, :, :head_dim], turned, preferred_element_type=F32)
        scores = jnp.where(lane_row == row, found, scores)
        live = jnp.where(lane_row == row, lengths_ref[row], live)
    scores = jnp.where(position < live, scores * head_dim ** (-0.5), -1e30)
    weights = jnp.exp(scores - jnp.max(scores, axis=0, keepdims=True))
    prob = (weights / jnp.sum(weights, axis=0, keepdims=True)).T.astype(BF16)
    place = lax.broadcasted_iota(jnp.int32, (rows, 1), 0)
    place_row = lax.rem(place, tok)
    attended = jnp.zeros((rows, head_dim), F32)
    for row in range(tok):
        found = jnp.dot(prob, cache_ref[row, :, head_dim:], preferred_element_type=F32)
        attended = jnp.where(place_row == row, found, attended)
    out_ref[:, :, :head_dim] = attended.astype(BF16).reshape(heads, tok, head_dim)
    expert = place // (tok * span)
    gates = jnp.zeros((rows, 1), F32)
    for row in range(tok):
        for k in range(shares_ref.shape[0]):
            named = (place_row == row) & (expert == routes_ref[k, row])
            gates = gates + jnp.where(named, shares_ref[k, row], 0.0)
    out_ref[:, :, head_dim:] = (
        jnp.broadcast_to(gates, (rows, LANES)).astype(BF16).reshape(heads, tok, LANES)
    )


def attend(lengths, routes, shares, query_rows, cache):
    heads, tok, head_dim = query_rows.shape
    return pl.pallas_call(
        attend_kernel,
        out_shape=jax.ShapeDtypeStruct((heads, tok, head_dim + LANES), BF16),
        in_specs=[SMEM_SPEC] * 3 + [VMEM_SPEC] * 2,
        out_specs=VMEM_SPEC,
        compiler_params=pltpu.CompilerParams(vmem_limit_bytes=8 << 20),
    )(lengths, routes, shares, query_rows, cache)


def relative_order(chips):
    order, bit = [0], chips // 2
    while bit:
        order = order + [o ^ bit for o in order]
        bit //= 2
    return order


def project_kernel(place_ref, rows_ref, weight_ref, kept_ref, sent_ref, gates_ref, ordered):
    chips, _, tok, _ = rows_ref.shape
    head_dim = weight_ref.shape[0]
    half = chips * tok
    mine, core = place_ref[0], place_ref[1]
    for part, core_at, out_ref in ((1, 1 - core, sent_ref), (0, core, kept_ref)):
        for at, bits in enumerate(relative_order(chips)):
            ordered[at] = rows_ref[mine ^ bits, core_at]
        block = ordered[...].reshape(half, head_dim + LANES)
        out_ref[...] = jnp.dot(
            block[:, :head_dim], weight_ref[...], preferred_element_type=F32
        ).astype(out_ref.dtype)
        gates_ref[pl.ds(part * half, half), :] = block[:, head_dim:]


def project(place, rows, weight):
    chips, _, tok, width = rows.shape
    half = chips * tok
    feature = weight.shape[1]
    return pl.pallas_call(
        project_kernel,
        out_shape=(
            jax.ShapeDtypeStruct((half, feature), F32),
            jax.ShapeDtypeStruct((half, feature), BF16),
            jax.ShapeDtypeStruct((2 * half, LANES), BF16),
        ),
        in_specs=[SMEM_SPEC, VMEM_SPEC, VMEM_SPEC],
        out_specs=(VMEM_SPEC, VMEM_SPEC, VMEM_SPEC),
        scratch_shapes=[pltpu.VMEM((chips, tok, width), BF16)],
        compiler_params=pltpu.CompilerParams(vmem_limit_bytes=8 << 20),
    )(place, rows, weight)


def norm_kernel(kept_ref, arrived_ref, gain_ref, middle_ref, normed_ref):
    tok = kept_ref.shape[0] // 2
    for block in range(2):
        mine = pl.ds(block * tok, tok)
        total = kept_ref[mine, :].astype(F32) + arrived_ref[1 - block].astype(F32)
        if block == 0:
            middle_ref[...] = total
        scale = lax.rsqrt(jnp.mean(total * total, axis=1, keepdims=True) + EPSILON)
        normed_ref[block] = (total * scale * gain_ref[...].reshape(1, -1)).astype(BF16)


def norm(kept, arrived, gain):
    rows, feature = kept.shape
    tok = rows // 2
    return pl.pallas_call(
        norm_kernel,
        out_shape=(
            jax.ShapeDtypeStruct((tok, feature), F32),
            jax.ShapeDtypeStruct((2, tok, feature), BF16),
        ),
        in_specs=[VMEM_SPEC] * 3,
        out_specs=(VMEM_SPEC, VMEM_SPEC),
        compiler_params=pltpu.CompilerParams(vmem_limit_bytes=4 << 20),
    )(kept, arrived.reshape(2, tok, feature), gain)


def expert_kernel(
    gates_ref, gate_ref, up_ref, down_source, *refs
):
    pieces, (kept_ref, sent_ref, turned, hidden, down_ref, sems) = refs[:-6], refs[-6:]
    half = turned.shape[1] // 2
    units, feature = gate_ref.shape
    step = tile_of(units, 384)
    wide = tile_of(feature, 896)

    def down_copy(at):
        columns = pl.ds(at, wide)
        return pltpu.make_async_copy(
            down_source.at[:, columns], down_ref.at[:, columns], sems.at[at // wide]
        )

    for at in range(0, feature, wide):
        down_copy(at).start()
    turned[...] = jnp.concatenate([piece[...] for piece in pieces], axis=0).T
    gates = gates_ref[:, :1].astype(F32)
    for at in range(0, units, step):
        rows = pl.ds(at, step)
        gate_pre = jnp.dot(gate_ref[rows, :], turned[...], preferred_element_type=F32)
        up_pre = jnp.dot(up_ref[rows, :], turned[...], preferred_element_type=F32)
        product = gate_pre / (1.0 + jnp.exp(-gate_pre)) * up_pre
        hidden[:, rows] = (product.T * gates).astype(BF16)
    for at in range(0, feature, wide):
        down_copy(at).wait()
        columns = pl.ds(at, wide)
        part = jnp.dot(hidden[...], down_ref[:, columns], preferred_element_type=F32)
        kept_ref[:, columns] = part[:half]
        sent_ref[:, columns] = part[half:].astype(BF16)


def experts(pieces, gates, gate_weight, up_weight, down_weight):
    half = sum(piece.shape[0] for piece in pieces) // 2
    feature = gate_weight.shape[1]
    units = gate_weight.shape[0]
    return pl.pallas_call(
        expert_kernel,
        out_shape=(
            jax.ShapeDtypeStruct((half, feature), F32),
            jax.ShapeDtypeStruct((half, feature), BF16),
        ),
        in_specs=[VMEM_SPEC] * 3 + [HBM_SPEC] + [VMEM_SPEC] * len(pieces),
        out_specs=(VMEM_SPEC, VMEM_SPEC),
        scratch_shapes=[
            pltpu.VMEM((feature, 2 * half), BF16),
            pltpu.VMEM((2 * half, units), BF16),
            pltpu.VMEM((units, feature), BF16),
            pltpu.SemaphoreType.DMA((8,)),
        ],
        compiler_params=pltpu.CompilerParams(vmem_limit_bytes=22 << 20),
        cost_estimate=pl.CostEstimate(
            flops=12 * half * feature * units,
            bytes_accessed=6 * units * feature,
            transcendentals=2 * half * units,
        ),
    )(
        gates,
        gate_weight,
        up_weight,
        pltpu.with_memory_space_constraint(down_weight, pltpu.HBM),
        *pieces,
    )


def local(
    queries,
    key_values,
    lengths,
    residual,
    routes,
    gate_weights,
    output_weight,
    norm_gain,
    gate_weight,
    up_weight,
    down_weight,
):
    tok = key_values.shape[0]
    head_dim = key_values.shape[2] // 2
    size = lax.axis_size("ep")
    chips = size // 2
    me = lax.axis_index("ep").astype(jnp.int32)
    place = jnp.stack([me // 2, me % 2])

    def swap(x, bit):
        return lax.ppermute(x, "ep", [(i, i ^ bit) for i in range(size)])

    def sum_nearest(kept, arrived):
        quarter = kept.shape[0] // 4
        parts = [
            kept[at : at + quarter] + arrived[at : at + quarter].astype(F32)
            for at in range(0, 4 * quarter, quarter)
        ]
        kept = parts[0]
        for bits, part in ((6, parts[3]), (2, parts[2]), (4, parts[1])):
            kept = kept + swap(part.astype(BF16), bits).astype(F32)
        bit = 8
        while bit < chips:
            half = kept.shape[0] // 2
            kept = kept[:half] + swap(kept[half:].astype(BF16), bit).astype(F32)
            bit *= 2
        return kept

    cache, residual_held, gain_held, lengths_held, routes_held = fetch(
        key_values, residual, norm_gain, lengths, routes.T
    )
    query_rows = lax.all_to_all(
        queries.reshape(size, tok, head_dim), "ep", split_axis=0, concat_axis=0, tiled=True
    )
    attended = attend(lengths_held, routes_held, gate_weights.astype(F32).T, query_rows, cache)
    (output_held,) = fetch(output_weight, after=(attended,))
    head_rows = lax.all_to_all(attended, "ep", split_axis=0, concat_axis=0, tiled=True)
    kept, sent, gates = project(
        place, head_rows.reshape(chips, 2, tok, head_dim + LANES), output_held
    )
    kept = sum_nearest(kept, swap(sent, 1))
    summed = kept.at[:tok].add(residual_held.astype(F32)).astype(BF16)
    bit = chips
    up_held, gain_held = fetch(up_weight, after=(summed,), carry=gain_held)
    middle, own = norm(summed, swap(summed, bit), gain_held)
    own = own.reshape(2 * tok, -1)
    bit //= 2
    while bit > 4:
        own = jnp.concatenate([own, swap(own, bit)], axis=0)
        bit //= 2
    others = [swap(own, bits) for bits in (4, 2, 6)]
    gate_held, own = fetch(gate_weight, carry=own)
    pieces = [own] + others
    pieces = pieces + [swap(piece, 1) for piece in pieces]
    kept, sent = experts(pieces, gates, gate_held, up_held, down_weight)
    kept = sum_nearest(kept, swap(sent, 1))
    combined = kept[:tok] + swap(kept[tok:].astype(BF16), chips).astype(F32)
    return (middle + combined).astype(BF16)


def solution(mesh):
    in_specs = (
        P("groups", "ep"),
        P(("groups", "ep"), None, None),
        P(("groups", "ep")),
        P(("groups", "ep"), None),
        P(("groups", "ep"), None),
        P(("groups", "ep"), None),
        P("ep", None),
        P(),
        P("ep", None),
        P("ep", None),
        P("ep", None),
    )
    out_specs = P(("groups", "ep"), None)
    return jax.shard_map(local, mesh=mesh, in_specs=in_specs, out_specs=out_specs, check_vma=False)
```

```python
import functools
import math

import jax
import jax.numpy as jnp
from jax import lax
from jax.experimental import pallas as pl
from jax.experimental.pallas import tpu as pltpu
from jax.sharding import PartitionSpec as P

EXPERTS = 8
EPSILON = 1e-05
LANES = 128
F32 = jnp.float32
BF16 = jnp.bfloat16
VMEM_SPEC = pl.BlockSpec(memory_space=pltpu.VMEM)
HBM_SPEC = pl.BlockSpec(memory_space=pltpu.HBM)
SMEM_SPEC = pl.BlockSpec(memory_space=pltpu.SMEM)


def tile_of(extent, most):
    return max(t for t in range(LANES, most + 1, LANES) if extent % t == 0)


def fetch_kernel(count, carried, ranges, *refs):
    sources, held, sems = refs[:count], refs[-count - 1 - carried : -1 - carried], refs[-1]
    copies = [
        pltpu.make_async_copy(source if rows is None else source.at[pl.ds(*rows)], target, sems.at[at])
        for at, (source, target, rows) in enumerate(zip(sources, held, ranges))
    ]
    for copy in copies:
        copy.start()
    if carried:
        refs[-2][...] = refs[count][...]
    for copy in copies:
        copy.wait()


def fetch(*arrays, after=(), carry=None):
    count, carried = len(arrays), int(carry is not None)
    carries = (carry,) * carried
    ranges = [a[1:] if isinstance(a, tuple) else None for a in arrays]
    arrays = [a[0] if isinstance(a, tuple) else a for a in arrays]
    shapes = [
        a.shape if rows is None else (rows[1],) + a.shape[1:] for a, rows in zip(arrays, ranges)
    ]
    return pl.pallas_call(
        functools.partial(fetch_kernel, count, carried, ranges),
        out_shape=tuple(pltpu.VMEM(s, a.dtype) for s, a in zip(shapes, arrays))
        + tuple(jax.ShapeDtypeStruct(c.shape, c.dtype) for c in carries),
        in_specs=[HBM_SPEC] * count
        + [VMEM_SPEC] * carried
        + [pl.BlockSpec(memory_space=pl.ANY)] * len(after),
        out_specs=(VMEM_SPEC,) * (count + carried),
        scratch_shapes=[pltpu.SemaphoreType.DMA((count,))],
        compiler_params=pltpu.CompilerParams(vmem_limit_bytes=4 << 20),
        cost_estimate=pl.CostEstimate(
            flops=0, bytes_accessed=sum(2 * a.size for a in arrays), transcendentals=0
        ),
    )(*[pltpu.with_memory_space_constraint(a, pltpu.HBM) for a in arrays], *carries, *after)


def attend_kernel(lengths_ref, routes_ref, shares_ref, query_ref, cache_ref, out_ref):
    heads, tok, head_dim = query_ref.shape
    context = cache_ref.shape[1]
    span = heads // EXPERTS
    rows = heads * tok
    turned = query_ref[...].reshape(rows, head_dim).T
    lane_row = lax.rem(lax.broadcasted_iota(jnp.int32, (1, rows), 1), tok)
    position = lax.broadcasted_iota(jnp.int32, (context, rows), 0)
    scores = jnp.zeros((context, rows), F32)
    live = jnp.zeros((1, rows), jnp.int32)
    for row in range(tok):
        found = jnp.dot(cache_ref[row, :, :head_dim], turned, preferred_element_type=F32)
        scores = jnp.where(lane_row == row, found, scores)
        live = jnp.where(lane_row == row, lengths_ref[row], live)
    scores = jnp.where(position < live, scores * head_dim ** (-0.5), -1e30)
    weights = jnp.exp(scores - jnp.max(scores, axis=0, keepdims=True))
    prob = (weights / jnp.sum(weights, axis=0, keepdims=True)).T.astype(BF16)
    place = lax.broadcasted_iota(jnp.int32, (rows, 1), 0)
    place_row = lax.rem(place, tok)
    attended = jnp.zeros((rows, head_dim), F32)
    for row in range(tok):
        found = jnp.dot(prob, cache_ref[row, :, head_dim:], preferred_element_type=F32)
        attended = jnp.where(place_row == row, found, attended)
    out_ref[:, :, :head_dim] = attended.astype(BF16).reshape(heads, tok, head_dim)
    expert = place // (tok * span)
    gates = jnp.zeros((rows, 1), F32)
    for row in range(tok):
        for k in range(shares_ref.shape[0]):
            named = (place_row == row) & (expert == routes_ref[k, row])
            gates = gates + jnp.where(named, shares_ref[k, row], 0.0)
    out_ref[:, :, head_dim:] = (
        jnp.broadcast_to(gates, (rows, LANES)).astype(BF16).reshape(heads, tok, LANES)
    )


def attend(lengths, routes, shares, query_rows, cache):
    heads, tok, head_dim = query_rows.shape
    return pl.pallas_call(
        attend_kernel,
        out_shape=jax.ShapeDtypeStruct((heads, tok, head_dim + LANES), BF16),
        in_specs=[SMEM_SPEC] * 3 + [VMEM_SPEC] * 2,
        out_specs=VMEM_SPEC,
        compiler_params=pltpu.CompilerParams(vmem_limit_bytes=8 << 20),
    )(lengths, routes, shares, query_rows, cache)


def relative_order(chips):
    order, bit = [0], chips // 2
    while bit:
        order = order + [o ^ bit for o in order]
        bit //= 2
    return order


def project_kernel(place_ref, rows_ref, weight_ref, terms_ref, gates_ref, ordered):
    chips, _, tok, _ = rows_ref.shape
    head_dim = weight_ref.shape[0]
    for at, bits in enumerate(relative_order(chips)):
        ordered[at] = rows_ref[place_ref[0] ^ bits, place_ref[1]]
    block = ordered[...].reshape(chips * tok, head_dim + LANES)
    terms_ref[...] = jnp.dot(
        block[:, :head_dim], weight_ref[...], preferred_element_type=F32
    ).astype(terms_ref.dtype)
    gates_ref[...] = block[:, head_dim:]


def project(place, rows, weight, dtype):
    chips, _, tok, width = rows.shape
    half = chips * tok
    feature = weight.shape[1]
    return pl.pallas_call(
        project_kernel,
        out_shape=(
            jax.ShapeDtypeStruct((half, feature), dtype),
            jax.ShapeDtypeStruct((half, LANES), BF16),
        ),
        in_specs=[SMEM_SPEC, VMEM_SPEC, VMEM_SPEC],
        out_specs=(VMEM_SPEC, VMEM_SPEC),
        scratch_shapes=[pltpu.VMEM((chips, tok, width), BF16)],
        compiler_params=pltpu.CompilerParams(vmem_limit_bytes=8 << 20),
        cost_estimate=pl.CostEstimate(
            flops=2 * half * feature * weight.shape[0],
            bytes_accessed=2 * weight.size,
            transcendentals=0,
        ),
    )(place, rows, weight)


def norm_kernel(kept_ref, arrived_ref, gain_ref, middle_ref, normed_ref):
    tok = kept_ref.shape[0] // 2
    for block in range(2):
        mine = pl.ds(block * tok, tok)
        total = kept_ref[mine, :].astype(F32) + arrived_ref[1 - block].astype(F32)
        if block == 0:
            middle_ref[...] = total
        scale = lax.rsqrt(jnp.mean(total * total, axis=1, keepdims=True) + EPSILON)
        normed_ref[block] = (total * scale * gain_ref[...].reshape(1, -1)).astype(BF16)


def norm(kept, arrived, gain):
    rows, feature = kept.shape
    tok = rows // 2
    return pl.pallas_call(
        norm_kernel,
        out_shape=(
            jax.ShapeDtypeStruct((tok, feature), F32),
            jax.ShapeDtypeStruct((2, tok, feature), BF16),
        ),
        in_specs=[VMEM_SPEC] * 3,
        out_specs=(VMEM_SPEC, VMEM_SPEC),
        compiler_params=pltpu.CompilerParams(vmem_limit_bytes=4 << 20),
    )(kept, arrived.reshape(2, tok, feature), gain)


def expert_kernel(own_gates_ref, other_gates_ref, first_ref, second_ref, up_ref, down_source, *refs):
    pieces, (kept_ref, sent_ref, turned, hidden, down_ref, sems) = refs[:-6], refs[-6:]
    half = turned.shape[1] // 2
    units, feature = up_ref.shape
    wide = tile_of(feature, 896)

    def down_copy(at):
        columns = pl.ds(at, wide)
        return pltpu.make_async_copy(
            down_source.at[:, columns], down_ref.at[:, columns], sems.at[at // wide]
        )

    for at in range(0, feature, wide):
        down_copy(at).start()
    turned[...] = jnp.concatenate([piece[...] for piece in pieces], axis=0).T
    gates = jnp.concatenate([own_gates_ref[...], other_gates_ref[...]], axis=0)
    gates = gates.astype(F32).T[:1]
    part = first_ref.shape[0]
    step = tile_of(math.gcd(part, units - part), 384)
    for at in range(0, units, step):
        gate_ref, low = (first_ref, at) if at < part else (second_ref, at - part)
        rows = pl.ds(at, step)
        gate_pre = jnp.dot(
            gate_ref[pl.ds(low, step), :], turned[...], preferred_element_type=F32
        )
        up_pre = jnp.dot(up_ref[rows, :], turned[...], preferred_element_type=F32)
        product = gate_pre / (1.0 + jnp.exp(-gate_pre)) * up_pre * gates
        hidden[:, rows] = product.astype(BF16).T
    for at in range(0, feature, wide):
        down_copy(at).wait()
        columns = pl.ds(at, wide)
        part = jnp.dot(hidden[...], down_ref[:, columns], preferred_element_type=F32)
        kept_ref[:, columns] = part[:half]
        sent_ref[:, columns] = part[half:].astype(BF16)


def experts(pieces, own_gates, other_gates, first_gate, second_gate, up_weight, down_weight):
    half = own_gates.shape[0]
    units, feature = up_weight.shape
    return pl.pallas_call(
        expert_kernel,
        out_shape=(
            jax.ShapeDtypeStruct((half, feature), F32),
            jax.ShapeDtypeStruct((half, feature), BF16),
        ),
        in_specs=[VMEM_SPEC] * 5 + [HBM_SPEC] + [VMEM_SPEC] * len(pieces),
        out_specs=(VMEM_SPEC, VMEM_SPEC),
        scratch_shapes=[
            pltpu.VMEM((feature, 2 * half), BF16),
            pltpu.VMEM((2 * half, units), BF16),
            pltpu.VMEM((units, feature), BF16),
            pltpu.SemaphoreType.DMA((8,)),
        ],
        compiler_params=pltpu.CompilerParams(vmem_limit_bytes=22 << 20),
        cost_estimate=pl.CostEstimate(
            flops=12 * half * feature * units,
            bytes_accessed=6 * units * feature,
            transcendentals=2 * half * units,
        ),
    )(
        own_gates,
        other_gates,
        first_gate,
        second_gate,
        up_weight,
        pltpu.with_memory_space_constraint(down_weight, pltpu.HBM),
        *pieces,
    )


def local(
    queries,
    key_values,
    lengths,
    residual,
    routes,
    gate_weights,
    output_weight,
    norm_gain,
    gate_weight,
    up_weight,
    down_weight,
):
    tok = key_values.shape[0]
    head_dim = key_values.shape[2] // 2
    size = lax.axis_size("ep")
    chips = size // 2
    me = lax.axis_index("ep").astype(jnp.int32)
    place = jnp.stack([me // 2, me % 2])
    other_place = jnp.stack([me // 2, 1 - me % 2])

    def swap(x, bit):
        return lax.ppermute(x, "ep", [(i, i ^ bit) for i in range(size)])

    def sum_nearest(kept, arrived):
        quarter = kept.shape[0] // 4
        parts = [
            kept[at : at + quarter] + arrived[at : at + quarter].astype(F32)
            for at in range(0, 4 * quarter, quarter)
        ]
        kept = parts[0]
        for bits, part in ((6, parts[3]), (2, parts[2]), (4, parts[1])):
            kept = kept + swap(part.astype(BF16), bits).astype(F32)
        bit = 8
        while bit < chips:
            half = kept.shape[0] // 2
            kept = kept[:half] + swap(kept[half:].astype(BF16), bit).astype(F32)
            bit *= 2
        return kept

    cache, residual_held, gain_held, lengths_held, routes_held = fetch(
        key_values, residual, norm_gain, lengths, routes.T
    )
    query_rows = lax.all_to_all(
        queries.reshape(size, tok, head_dim), "ep", split_axis=0, concat_axis=0, tiled=True
    )
    attended = attend(lengths_held, routes_held, gate_weights.astype(F32).T, query_rows, cache)
    (output_held,) = fetch(output_weight, after=(attended,))
    head_rows = lax.all_to_all(attended, "ep", split_axis=0, concat_axis=0, tiled=True)
    head_rows = head_rows.reshape(chips, 2, tok, head_dim + LANES)
    sent, other_gates = project(other_place, head_rows, output_held, BF16)
    arrived = swap(sent, 1)
    kept, own_gates = project(place, head_rows, output_held, F32)
    kept = sum_nearest(kept, arrived)
    summed = kept.at[:tok].add(residual_held.astype(F32)).astype(BF16)
    bit = chips
    units = gate_weight.shape[0]
    part = units // LANES // 2 * LANES
    up_held, first_held, gain_held = fetch(
        up_weight, (gate_weight, 0, part), after=(summed,), carry=gain_held
    )
    middle, own = norm(summed, swap(summed, bit), gain_held)
    own = own.reshape(2 * tok, -1)
    bit //= 2
    while bit > 4:
        own = jnp.concatenate([own, swap(own, bit)], axis=0)
        bit //= 2
    others = [swap(own, bits) for bits in (4, 2, 6)]
    second_held, own = fetch((gate_weight, part, units - part), carry=own)
    pieces = [own] + others
    pieces = pieces + [swap(piece, 1) for piece in pieces]
    kept, sent = experts(
        pieces, own_gates, other_gates, first_held, second_held, up_held, down_weight
    )
    kept = sum_nearest(kept, swap(sent, 1))
    combined = kept[:tok] + swap(kept[tok:].astype(BF16), chips).astype(F32)
    return (middle + combined).astype(BF16)


def solution(mesh):
    in_specs = (
        P("groups", "ep"),
        P(("groups", "ep"), None, None),
        P(("groups", "ep")),
        P(("groups", "ep"), None),
        P(("groups", "ep"), None),
        P(("groups", "ep"), None),
        P("ep", None),
        P(),
        P("ep", None),
        P("ep", None),
        P("ep", None),
    )
    out_specs = P(("groups", "ep"), None)
    return jax.shard_map(local, mesh=mesh, in_specs=in_specs, out_specs=out_specs, check_vma=False)
```

```python
import functools
import math

import jax
import jax.numpy as jnp
from jax import lax
from jax.experimental import pallas as pl
from jax.experimental.pallas import tpu as pltpu
from jax.sharding import PartitionSpec as P

EXPERTS = 8
EPSILON = 1e-05
LANES = 128
F32 = jnp.float32
BF16 = jnp.bfloat16
VMEM_SPEC = pl.BlockSpec(memory_space=pltpu.VMEM)
HBM_SPEC = pl.BlockSpec(memory_space=pltpu.HBM)
SMEM_SPEC = pl.BlockSpec(memory_space=pltpu.SMEM)


def tile_of(extent, most):
    return max(t for t in range(LANES, most + 1, LANES) if extent % t == 0)


def fetch_kernel(count, carried, ranges, *refs):
    sources, held, sems = refs[:count], refs[-count - 1 - carried : -1 - carried], refs[-1]
    copies = [
        pltpu.make_async_copy(source if rows is None else source.at[pl.ds(*rows)], target, sems.at[at])
        for at, (source, target, rows) in enumerate(zip(sources, held, ranges))
    ]
    for copy in copies:
        copy.start()
    if carried:
        refs[-2][...] = refs[count][...]
    for copy in copies:
        copy.wait()


def fetch(*arrays, after=(), carry=None):
    count, carried = len(arrays), int(carry is not None)
    carries = (carry,) * carried
    ranges = [a[1:] if isinstance(a, tuple) else None for a in arrays]
    arrays = [a[0] if isinstance(a, tuple) else a for a in arrays]
    shapes = [
        a.shape if rows is None else (rows[1],) + a.shape[1:] for a, rows in zip(arrays, ranges)
    ]
    return pl.pallas_call(
        functools.partial(fetch_kernel, count, carried, ranges),
        out_shape=tuple(pltpu.VMEM(s, a.dtype) for s, a in zip(shapes, arrays))
        + tuple(jax.ShapeDtypeStruct(c.shape, c.dtype) for c in carries),
        in_specs=[HBM_SPEC] * count
        + [VMEM_SPEC] * carried
        + [pl.BlockSpec(memory_space=pl.ANY)] * len(after),
        out_specs=(VMEM_SPEC,) * (count + carried),
        scratch_shapes=[pltpu.SemaphoreType.DMA((count,))],
        compiler_params=pltpu.CompilerParams(vmem_limit_bytes=4 << 20),
        cost_estimate=pl.CostEstimate(
            flops=0, bytes_accessed=sum(2 * a.size for a in arrays), transcendentals=0
        ),
    )(*[pltpu.with_memory_space_constraint(a, pltpu.HBM) for a in arrays], *carries, *after)


def attend_kernel(lengths_ref, routes_ref, shares_ref, query_ref, cache_ref, out_ref):
    heads, tok, head_dim = query_ref.shape
    context = cache_ref.shape[1]
    span = heads // EXPERTS
    rows = heads * tok
    turned = query_ref[...].reshape(rows, head_dim).T
    lane_row = lax.rem(lax.broadcasted_iota(jnp.int32, (1, rows), 1), tok)
    position = lax.broadcasted_iota(jnp.int32, (context, rows), 0)
    scores = jnp.zeros((context, rows), F32)
    live = jnp.zeros((1, rows), jnp.int32)
    for row in range(tok):
        found = jnp.dot(cache_ref[row, :, :head_dim], turned, preferred_element_type=F32)
        scores = jnp.where(lane_row == row, found, scores)
        live = jnp.where(lane_row == row, lengths_ref[row], live)
    scores = jnp.where(position < live, scores * head_dim ** (-0.5), -1e30)
    weights = jnp.exp(scores - jnp.max(scores, axis=0, keepdims=True))
    prob = (weights / jnp.sum(weights, axis=0, keepdims=True)).T.astype(BF16)
    place = lax.broadcasted_iota(jnp.int32, (rows, 1), 0)
    place_row = lax.rem(place, tok)
    attended = jnp.zeros((rows, head_dim), F32)
    for row in range(tok):
        found = jnp.dot(prob, cache_ref[row, :, head_dim:], preferred_element_type=F32)
        attended = jnp.where(place_row == row, found, attended)
    out_ref[:, :, :head_dim] = attended.astype(BF16).reshape(heads, tok, head_dim)
    expert = place // (tok * span)
    gates = jnp.zeros((rows, 1), F32)
    for row in range(tok):
        for k in range(shares_ref.shape[0]):
            named = (place_row == row) & (expert == routes_ref[k, row])
            gates = gates + jnp.where(named, shares_ref[k, row], 0.0)
    out_ref[:, :, head_dim:] = (
        jnp.broadcast_to(gates, (rows, LANES)).astype(BF16).reshape(heads, tok, LANES)
    )


def attend(lengths, routes, shares, query_rows, cache):
    heads, tok, head_dim = query_rows.shape
    return pl.pallas_call(
        attend_kernel,
        out_shape=jax.ShapeDtypeStruct((heads, tok, head_dim + LANES), BF16),
        in_specs=[SMEM_SPEC] * 3 + [VMEM_SPEC] * 2,
        out_specs=VMEM_SPEC,
        compiler_params=pltpu.CompilerParams(vmem_limit_bytes=8 << 20),
    )(lengths, routes, shares, query_rows, cache)


def relative_order(chips):
    order, bit = [0], chips // 2
    while bit:
        order = order + [o ^ bit for o in order]
        bit //= 2
    return order


def project_kernel(place_ref, rows_ref, weight_ref, terms_ref, gates_ref, ordered):
    chips, _, tok, _ = rows_ref.shape
    head_dim = weight_ref.shape[0]
    for at, bits in enumerate(relative_order(chips)):
        ordered[at] = rows_ref[place_ref[0] ^ bits, place_ref[1]]
    block = ordered[...].reshape(chips * tok, head_dim + LANES)
    terms_ref[...] = jnp.dot(
        block[:, :head_dim], weight_ref[...], preferred_element_type=F32
    ).astype(terms_ref.dtype)
    gates_ref[...] = block[:, head_dim:]


def project(place, rows, weight, dtype):
    chips, _, tok, width = rows.shape
    half = chips * tok
    feature = weight.shape[1]
    return pl.pallas_call(
        project_kernel,
        out_shape=(
            jax.ShapeDtypeStruct((half, feature), dtype),
            jax.ShapeDtypeStruct((half, LANES), BF16),
        ),
        in_specs=[SMEM_SPEC, VMEM_SPEC, VMEM_SPEC],
        out_specs=(VMEM_SPEC, VMEM_SPEC),
        scratch_shapes=[pltpu.VMEM((chips, tok, width), BF16)],
        compiler_params=pltpu.CompilerParams(vmem_limit_bytes=8 << 20),
        cost_estimate=pl.CostEstimate(
            flops=2 * half * feature * weight.shape[0],
            bytes_accessed=2 * weight.size,
            transcendentals=0,
        ),
    )(place, rows, weight)


def norm_kernel(kept_ref, arrived_ref, gain_ref, middle_ref, normed_ref):
    tok = kept_ref.shape[0] // 2
    for block in range(2):
        mine = pl.ds(block * tok, tok)
        total = kept_ref[mine, :].astype(F32) + arrived_ref[1 - block].astype(F32)
        if block == 0:
            middle_ref[...] = total
        scale = lax.rsqrt(jnp.mean(total * total, axis=1, keepdims=True) + EPSILON)
        normed_ref[block] = (total * scale * gain_ref[...].reshape(1, -1)).astype(BF16)


def norm(kept, arrived, gain):
    rows, feature = kept.shape
    tok = rows // 2
    return pl.pallas_call(
        norm_kernel,
        out_shape=(
            jax.ShapeDtypeStruct((tok, feature), F32),
            jax.ShapeDtypeStruct((2, tok, feature), BF16),
        ),
        in_specs=[VMEM_SPEC] * 3,
        out_specs=(VMEM_SPEC, VMEM_SPEC),
        compiler_params=pltpu.CompilerParams(vmem_limit_bytes=4 << 20),
    )(kept, arrived.reshape(2, tok, feature), gain)


def expert_kernel(own_gates_ref, other_gates_ref, first_ref, second_ref, up_ref, down_source, *refs):
    pieces, (kept_ref, sent_ref, turned, hidden, down_ref, sems) = refs[:-6], refs[-6:]
    half = turned.shape[1] // 2
    units, feature = up_ref.shape
    wide = tile_of(feature, 1792)

    deep = tile_of(units, 384)
    copies = [
        pltpu.make_async_copy(
            down_source.at[pl.ds(at, deep)], down_ref.at[pl.ds(at, deep)], sems.at[at // deep]
        )
        for at in range(0, units, deep)
    ]
    for copy in copies:
        copy.start()
    turned[...] = jnp.concatenate([piece[...] for piece in pieces], axis=0).T
    gates = jnp.concatenate([own_gates_ref[...], other_gates_ref[...]], axis=0)
    gates = gates.astype(F32).T[:1]
    part = first_ref.shape[0]
    step = tile_of(math.gcd(part, units - part), 384)
    for at in range(0, units, step):
        gate_ref, low = (first_ref, at) if at < part else (second_ref, at - part)
        rows = pl.ds(at, step)
        gate_pre = jnp.dot(
            gate_ref[pl.ds(low, step), :], turned[...], preferred_element_type=F32
        )
        up_pre = jnp.dot(up_ref[rows, :], turned[...], preferred_element_type=F32)
        product = gate_pre / (1.0 + jnp.exp(-gate_pre)) * up_pre * gates
        hidden[:, rows] = product.astype(BF16).T
    for copy in copies:
        copy.wait()
    for at in range(0, feature, wide):
        columns = pl.ds(at, wide)
        part = jnp.dot(hidden[...], down_ref[:, columns], preferred_element_type=F32)
        kept_ref[:, columns] = part[:half]
        sent_ref[:, columns] = part[half:].astype(BF16)


def experts(pieces, own_gates, other_gates, first_gate, second_gate, up_weight, down_weight):
    half = own_gates.shape[0]
    units, feature = up_weight.shape
    return pl.pallas_call(
        expert_kernel,
        out_shape=(
            jax.ShapeDtypeStruct((half, feature), F32),
            jax.ShapeDtypeStruct((half, feature), BF16),
        ),
        in_specs=[VMEM_SPEC] * 5 + [HBM_SPEC] + [VMEM_SPEC] * len(pieces),
        out_specs=(VMEM_SPEC, VMEM_SPEC),
        scratch_shapes=[
            pltpu.VMEM((feature, 2 * half), BF16),
            pltpu.VMEM((2 * half, units), BF16),
            pltpu.VMEM((units, feature), BF16),
            pltpu.SemaphoreType.DMA((8,)),
        ],
        compiler_params=pltpu.CompilerParams(vmem_limit_bytes=22 << 20),
        cost_estimate=pl.CostEstimate(
            flops=12 * half * feature * units,
            bytes_accessed=6 * units * feature,
            transcendentals=2 * half * units,
        ),
    )(
        own_gates,
        other_gates,
        first_gate,
        second_gate,
        up_weight,
        pltpu.with_memory_space_constraint(down_weight, pltpu.HBM),
        *pieces,
    )


def local(
    queries,
    key_values,
    lengths,
    residual,
    routes,
    gate_weights,
    output_weight,
    norm_gain,
    gate_weight,
    up_weight,
    down_weight,
):
    tok = key_values.shape[0]
    head_dim = key_values.shape[2] // 2
    size = lax.axis_size("ep")
    chips = size // 2
    me = lax.axis_index("ep").astype(jnp.int32)
    place = jnp.stack([me // 2, me % 2])
    other_place = jnp.stack([me // 2, 1 - me % 2])

    def swap(x, bit):
        return lax.ppermute(x, "ep", [(i, i ^ bit) for i in range(size)])

    def sum_nearest(kept, arrived):
        quarter = kept.shape[0] // 4
        parts = [
            kept[at : at + quarter] + arrived[at : at + quarter].astype(F32)
            for at in range(0, 4 * quarter, quarter)
        ]
        kept = parts[0]
        for bits, part in ((6, parts[3]), (2, parts[2]), (4, parts[1])):
            kept = kept + swap(part.astype(BF16), bits).astype(F32)
        bit = 8
        while bit < chips:
            half = kept.shape[0] // 2
            kept = kept[:half] + swap(kept[half:].astype(BF16), bit).astype(F32)
            bit *= 2
        return kept

    cache, residual_held, gain_held, lengths_held, routes_held = fetch(
        key_values, residual, norm_gain, lengths, routes.T
    )
    query_rows = lax.all_to_all(
        queries.reshape(size, tok, head_dim), "ep", split_axis=0, concat_axis=0, tiled=True
    )
    attended = attend(lengths_held, routes_held, gate_weights.astype(F32).T, query_rows, cache)
    (output_held,) = fetch(output_weight, after=(attended,))
    head_rows = lax.all_to_all(attended, "ep", split_axis=0, concat_axis=0, tiled=True)
    head_rows = head_rows.reshape(chips, 2, tok, head_dim + LANES)
    sent, other_gates = project(other_place, head_rows, output_held, BF16)
    arrived = swap(sent, 1)
    kept, own_gates = project(place, head_rows, output_held, F32)
    kept = sum_nearest(kept, arrived)
    summed = kept.at[:tok].add(residual_held.astype(F32)).astype(BF16)
    bit = chips
    units = gate_weight.shape[0]
    part = units // LANES // 2 * LANES
    up_held, first_held, gain_held = fetch(
        up_weight, (gate_weight, 0, part), after=(summed,), carry=gain_held
    )
    middle, own = norm(summed, swap(summed, bit), gain_held)
    own = own.reshape(2 * tok, -1)
    bit //= 2
    while bit > 4:
        own = jnp.concatenate([own, swap(own, bit)], axis=0)
        bit //= 2
    others = [swap(own, bits) for bits in (4, 2, 6)]
    second_held, own = fetch((gate_weight, part, units - part), carry=own)
    pieces = [own] + others
    pieces = pieces + [swap(piece, 1) for piece in pieces]
    kept, sent = experts(
        pieces, own_gates, other_gates, first_held, second_held, up_held, down_weight
    )
    kept = sum_nearest(kept, swap(sent, 1))
    combined = kept[:tok] + swap(kept[tok:].astype(BF16), chips).astype(F32)
    return (middle + combined).astype(BF16)


def solution(mesh):
    in_specs = (
        P("groups", "ep"),
        P(("groups", "ep"), None, None),
        P(("groups", "ep")),
        P(("groups", "ep"), None),
        P(("groups", "ep"), None),
        P(("groups", "ep"), None),
        P("ep", None),
        P(),
        P("ep", None),
        P("ep", None),
        P("ep", None),
    )
    out_specs = P(("groups", "ep"), None)
    return jax.shard_map(local, mesh=mesh, in_specs=in_specs, out_specs=out_specs, check_vma=False)
```

```python
import functools
import math

import jax
import jax.numpy as jnp
from jax import lax
from jax.experimental import pallas as pl
from jax.experimental.pallas import tpu as pltpu
from jax.sharding import PartitionSpec as P

EXPERTS = 8
EPSILON = 1e-05
LANES = 128
F32 = jnp.float32
BF16 = jnp.bfloat16
VMEM_SPEC = pl.BlockSpec(memory_space=pltpu.VMEM)
HBM_SPEC = pl.BlockSpec(memory_space=pltpu.HBM)
SMEM_SPEC = pl.BlockSpec(memory_space=pltpu.SMEM)


def tile_of(extent, most):
    return max(t for t in range(LANES, most + 1, LANES) if extent % t == 0)


def fetch_kernel(count, carried, ranges, *refs):
    sources, held, sems = refs[:count], refs[-count - 1 - carried : -1 - carried], refs[-1]
    copies = [
        pltpu.make_async_copy(source if rows is None else source.at[pl.ds(*rows)], target, sems.at[at])
        for at, (source, target, rows) in enumerate(zip(sources, held, ranges))
    ]
    for copy in copies:
        copy.start()
    if carried:
        refs[-2][...] = refs[count][...]
    for copy in copies:
        copy.wait()


def fetch(*arrays, after=(), carry=None):
    count, carried = len(arrays), int(carry is not None)
    carries = (carry,) * carried
    ranges = [a[1:] if isinstance(a, tuple) else None for a in arrays]
    arrays = [a[0] if isinstance(a, tuple) else a for a in arrays]
    shapes = [
        a.shape if rows is None else (rows[1],) + a.shape[1:] for a, rows in zip(arrays, ranges)
    ]
    return pl.pallas_call(
        functools.partial(fetch_kernel, count, carried, ranges),
        out_shape=tuple(pltpu.VMEM(s, a.dtype) for s, a in zip(shapes, arrays))
        + tuple(jax.ShapeDtypeStruct(c.shape, c.dtype) for c in carries),
        in_specs=[HBM_SPEC] * count
        + [VMEM_SPEC] * carried
        + [pl.BlockSpec(memory_space=pl.ANY)] * len(after),
        out_specs=(VMEM_SPEC,) * (count + carried),
        scratch_shapes=[pltpu.SemaphoreType.DMA((count,))],
        compiler_params=pltpu.CompilerParams(vmem_limit_bytes=4 << 20),
        cost_estimate=pl.CostEstimate(
            flops=0, bytes_accessed=sum(2 * a.size for a in arrays), transcendentals=0
        ),
    )(*[pltpu.with_memory_space_constraint(a, pltpu.HBM) for a in arrays], *carries, *after)


def attend_kernel(lengths_ref, routes_ref, shares_ref, query_ref, cache_ref, out_ref):
    heads, tok, head_dim = query_ref.shape
    context = cache_ref.shape[1]
    span = heads // EXPERTS
    rows = heads * tok
    turned = query_ref[...].reshape(rows, head_dim).T
    lane_row = lax.rem(lax.broadcasted_iota(jnp.int32, (1, rows), 1), tok)
    position = lax.broadcasted_iota(jnp.int32, (context, rows), 0)
    scores = jnp.zeros((context, rows), F32)
    live = jnp.zeros((1, rows), jnp.int32)
    for row in range(tok):
        found = jnp.dot(cache_ref[row, :, :head_dim], turned, preferred_element_type=F32)
        scores = jnp.where(lane_row == row, found, scores)
        live = jnp.where(lane_row == row, lengths_ref[row], live)
    scores = jnp.where(position < live, scores * head_dim ** (-0.5), -1e30)
    weights = jnp.exp(scores - jnp.max(scores, axis=0, keepdims=True))
    prob = (weights / jnp.sum(weights, axis=0, keepdims=True)).T.astype(BF16)
    place = lax.broadcasted_iota(jnp.int32, (rows, 1), 0)
    place_row = lax.rem(place, tok)
    attended = jnp.zeros((rows, head_dim), F32)
    for row in range(tok):
        found = jnp.dot(prob, cache_ref[row, :, head_dim:], preferred_element_type=F32)
        attended = jnp.where(place_row == row, found, attended)
    out_ref[:, :, :head_dim] = attended.astype(BF16).reshape(heads, tok, head_dim)
    expert = place // (tok * span)
    gates = jnp.zeros((rows, 1), F32)
    for row in range(tok):
        for k in range(shares_ref.shape[0]):
            named = (place_row == row) & (expert == routes_ref[k, row])
            gates = gates + jnp.where(named, shares_ref[k, row], 0.0)
    out_ref[:, :, head_dim:] = (
        jnp.broadcast_to(gates, (rows, LANES)).astype(BF16).reshape(heads, tok, LANES)
    )


def attend(lengths, routes, shares, query_rows, cache):
    heads, tok, head_dim = query_rows.shape
    return pl.pallas_call(
        attend_kernel,
        out_shape=jax.ShapeDtypeStruct((heads, tok, head_dim + LANES), BF16),
        in_specs=[SMEM_SPEC] * 3 + [VMEM_SPEC] * 2,
        out_specs=VMEM_SPEC,
        compiler_params=pltpu.CompilerParams(vmem_limit_bytes=8 << 20),
    )(lengths, routes, shares, query_rows, cache)


def relative_order(chips):
    order, bit = [0], chips // 2
    while bit:
        order = order + [o ^ bit for o in order]
        bit //= 2
    return order


def project_kernel(place_ref, rows_ref, weight_ref, terms_ref, gates_ref, ordered):
    chips, _, tok, _ = rows_ref.shape
    head_dim = weight_ref.shape[0]
    for at, bits in enumerate(relative_order(chips)):
        ordered[at] = rows_ref[place_ref[0] ^ bits, place_ref[1]]
    block = ordered[...].reshape(chips * tok, head_dim + LANES)
    terms_ref[...] = jnp.dot(
        block[:, :head_dim], weight_ref[...], preferred_element_type=F32
    ).astype(terms_ref.dtype)
    gates_ref[...] = block[:, head_dim:]


def project(place, rows, weight, dtype):
    chips, _, tok, width = rows.shape
    half = chips * tok
    feature = weight.shape[1]
    return pl.pallas_call(
        project_kernel,
        out_shape=(
            jax.ShapeDtypeStruct((half, feature), dtype),
            jax.ShapeDtypeStruct((half, LANES), BF16),
        ),
        in_specs=[SMEM_SPEC, VMEM_SPEC, VMEM_SPEC],
        out_specs=(VMEM_SPEC, VMEM_SPEC),
        scratch_shapes=[pltpu.VMEM((chips, tok, width), BF16)],
        compiler_params=pltpu.CompilerParams(vmem_limit_bytes=8 << 20),
        cost_estimate=pl.CostEstimate(
            flops=2 * half * feature * weight.shape[0],
            bytes_accessed=2 * weight.size,
            transcendentals=0,
        ),
    )(place, rows, weight)


def norm_kernel(kept_ref, arrived_ref, gain_ref, middle_ref, normed_ref):
    tok = kept_ref.shape[0] // 2
    for block in range(2):
        mine = pl.ds(block * tok, tok)
        total = kept_ref[mine, :].astype(F32) + arrived_ref[1 - block].astype(F32)
        if block == 0:
            middle_ref[...] = total
        scale = lax.rsqrt(jnp.mean(total * total, axis=1, keepdims=True) + EPSILON)
        normed_ref[block] = (total * scale * gain_ref[...].reshape(1, -1)).astype(BF16)


def norm(kept, arrived, gain):
    rows, feature = kept.shape
    tok = rows // 2
    return pl.pallas_call(
        norm_kernel,
        out_shape=(
            jax.ShapeDtypeStruct((tok, feature), F32),
            jax.ShapeDtypeStruct((2, tok, feature), BF16),
        ),
        in_specs=[VMEM_SPEC] * 3,
        out_specs=(VMEM_SPEC, VMEM_SPEC),
        compiler_params=pltpu.CompilerParams(vmem_limit_bytes=4 << 20),
    )(kept, arrived.reshape(2, tok, feature), gain)


def expert_kernel(own_gates_ref, other_gates_ref, first_ref, second_ref, up_ref, low_ref, middle_ref, down_source, *refs):
    pieces, (kept_ref, sent_ref, turned, hidden, down_ref, sems) = refs[:-6], refs[-6:]
    half = turned.shape[1] // 2
    units, feature = up_ref.shape
    wide = tile_of(feature, 1792)

    first_unit = units - down_ref.shape[0]
    deep = tile_of(down_ref.shape[0], 128)
    copies = [
        pltpu.make_async_copy(
            down_source.at[pl.ds(first_unit + at, deep)], down_ref.at[pl.ds(at, deep)], sems.at[at // deep]
        )
        for at in range(0, down_ref.shape[0], deep)
    ]
    for copy in copies:
        copy.start()
    turned[...] = jnp.concatenate([piece[...] for piece in pieces], axis=0).T
    gates = jnp.concatenate([own_gates_ref[...], other_gates_ref[...]], axis=0)
    gates = gates.astype(F32).T[:1]
    part = first_ref.shape[0]
    step = tile_of(math.gcd(part, units - part), 384)
    for at in range(0, units, step):
        gate_ref, low = (first_ref, at) if at < part else (second_ref, at - part)
        rows = pl.ds(at, step)
        gate_pre = jnp.dot(
            gate_ref[pl.ds(low, step), :], turned[...], preferred_element_type=F32
        )
        up_pre = jnp.dot(up_ref[rows, :], turned[...], preferred_element_type=F32)
        product = gate_pre / (1.0 + jnp.exp(-gate_pre)) * up_pre * gates
        hidden[:, rows] = product.astype(BF16).T
    for copy in copies:
        copy.wait()
    for at in range(0, feature, wide):
        columns = pl.ds(at, wide)
        total, low = None, 0
        for ref in (low_ref, middle_ref, down_ref):
            units_here = pl.ds(low, ref.shape[0])
            term = jnp.dot(hidden[:, units_here], ref[:, columns], preferred_element_type=F32)
            total = term if total is None else total + term
            low += ref.shape[0]
        kept_ref[:, columns] = total[:half]
        sent_ref[:, columns] = total[half:].astype(BF16)


def experts(pieces, gates, held, down_weight):
    half = gates[0].shape[0]
    units, feature = down_weight.shape
    rest = units - held[3].shape[0] - held[4].shape[0]
    return pl.pallas_call(
        expert_kernel,
        out_shape=(
            jax.ShapeDtypeStruct((half, feature), F32),
            jax.ShapeDtypeStruct((half, feature), BF16),
        ),
        in_specs=[VMEM_SPEC] * 7 + [HBM_SPEC] + [VMEM_SPEC] * len(pieces),
        out_specs=(VMEM_SPEC, VMEM_SPEC),
        scratch_shapes=[
            pltpu.VMEM((feature, 2 * half), BF16),
            pltpu.VMEM((2 * half, units), BF16),
            pltpu.VMEM((rest, feature), BF16),
            pltpu.SemaphoreType.DMA((8,)),
        ],
        compiler_params=pltpu.CompilerParams(vmem_limit_bytes=16 << 20),
        cost_estimate=pl.CostEstimate(
            flops=12 * half * feature * units,
            bytes_accessed=6 * units * feature,
            transcendentals=2 * half * units,
        ),
    )(
        *gates,
        *held,
        pltpu.with_memory_space_constraint(down_weight, pltpu.HBM),
        *pieces,
    )


def local(
    queries,
    key_values,
    lengths,
    residual,
    routes,
    gate_weights,
    output_weight,
    norm_gain,
    gate_weight,
    up_weight,
    down_weight,
):
    tok = key_values.shape[0]
    head_dim = key_values.shape[2] // 2
    size = lax.axis_size("ep")
    chips = size // 2
    me = lax.axis_index("ep").astype(jnp.int32)
    place = jnp.stack([me // 2, me % 2])
    other_place = jnp.stack([me // 2, 1 - me % 2])

    def swap(x, bit):
        return lax.ppermute(x, "ep", [(i, i ^ bit) for i in range(size)])

    def sum_nearest(kept, arrived):
        quarter = kept.shape[0] // 4
        parts = [
            kept[at : at + quarter] + arrived[at : at + quarter].astype(F32)
            for at in range(0, 4 * quarter, quarter)
        ]
        kept = parts[0]
        for bits, part in ((6, parts[3]), (2, parts[2]), (4, parts[1])):
            kept = kept + swap(part.astype(BF16), bits).astype(F32)
        bit = 8
        while bit < chips:
            half = kept.shape[0] // 2
            kept = kept[:half] + swap(kept[half:].astype(BF16), bit).astype(F32)
            bit *= 2
        return kept

    cache, residual_held, gain_held, lengths_held, routes_held = fetch(
        key_values, residual, norm_gain, lengths, routes.T
    )
    query_rows = lax.all_to_all(
        queries.reshape(size, tok, head_dim), "ep", split_axis=0, concat_axis=0, tiled=True
    )
    attended = attend(lengths_held, routes_held, gate_weights.astype(F32).T, query_rows, cache)
    (output_held,) = fetch(output_weight, after=(attended,))
    head_rows = lax.all_to_all(attended, "ep", split_axis=0, concat_axis=0, tiled=True)
    head_rows = head_rows.reshape(chips, 2, tok, head_dim + LANES)
    sent, other_gates = project(other_place, head_rows, output_held, BF16)
    arrived = swap(sent, 1)
    kept, own_gates = project(place, head_rows, output_held, F32)
    kept = sum_nearest(kept, arrived)
    summed = kept.at[:tok].add(residual_held.astype(F32)).astype(BF16)
    bit = chips
    units = gate_weight.shape[0]
    part = units // LANES // 2 * LANES
    third = units // LANES // 3 * LANES
    up_held, first_held, low_held, gain_held = fetch(
        up_weight, (gate_weight, 0, part), (down_weight, 0, third), after=(summed,), carry=gain_held
    )
    middle, own = norm(summed, swap(summed, bit), gain_held)
    own = own.reshape(2 * tok, -1)
    bit //= 2
    while bit > 4:
        own = jnp.concatenate([own, swap(own, bit)], axis=0)
        bit //= 2
    others = [swap(own, bits) for bits in (4, 2, 6)]
    second_held, middle_held, own = fetch(
        (gate_weight, part, units - part), (down_weight, third, third), carry=own
    )
    pieces = [own] + others
    pieces = pieces + [swap(piece, 1) for piece in pieces]
    held = (first_held, second_held, up_held, low_held, middle_held)
    kept, sent = experts(pieces, (own_gates, other_gates), held, down_weight)
    kept = sum_nearest(kept, swap(sent, 1))
    combined = kept[:tok] + swap(kept[tok:].astype(BF16), chips).astype(F32)
    return (middle + combined).astype(BF16)


def solution(mesh):
    in_specs = (
        P("groups", "ep"),
        P(("groups", "ep"), None, None),
        P(("groups", "ep")),
        P(("groups", "ep"), None),
        P(("groups", "ep"), None),
        P(("groups", "ep"), None),
        P("ep", None),
        P(),
        P("ep", None),
        P("ep", None),
        P("ep", None),
    )
    out_specs = P(("groups", "ep"), None)
    return jax.shard_map(local, mesh=mesh, in_specs=in_specs, out_specs=out_specs, check_vma=False)
```

```python
import functools
import math

import jax
import jax.numpy as jnp
from jax import lax
from jax.experimental import pallas as pl
from jax.experimental.pallas import tpu as pltpu
from jax.sharding import PartitionSpec as P

EXPERTS = 8
EPSILON = 1e-05
LANES = 128
F32 = jnp.float32
BF16 = jnp.bfloat16
VMEM_SPEC = pl.BlockSpec(memory_space=pltpu.VMEM)
HBM_SPEC = pl.BlockSpec(memory_space=pltpu.HBM)
SMEM_SPEC = pl.BlockSpec(memory_space=pltpu.SMEM)


def tile_of(extent, most):
    return max(t for t in range(LANES, most + 1, LANES) if extent % t == 0)


def fetch_kernel(count, carried, ranges, *refs):
    sources, held, sems = refs[:count], refs[-count - 1 - carried : -1 - carried], refs[-1]
    copies = [
        pltpu.make_async_copy(source if rows is None else source.at[pl.ds(*rows)], target, sems.at[at])
        for at, (source, target, rows) in enumerate(zip(sources, held, ranges))
    ]
    for copy in copies:
        copy.start()
    if carried:
        refs[-2][...] = refs[count][...]
    for copy in copies:
        copy.wait()


def fetch(*arrays, after=(), carry=None):
    count, carried = len(arrays), int(carry is not None)
    carries = (carry,) * carried
    ranges = [a[1:] if isinstance(a, tuple) else None for a in arrays]
    arrays = [a[0] if isinstance(a, tuple) else a for a in arrays]
    shapes = [
        a.shape if rows is None else (rows[1],) + a.shape[1:] for a, rows in zip(arrays, ranges)
    ]
    return pl.pallas_call(
        functools.partial(fetch_kernel, count, carried, ranges),
        out_shape=tuple(pltpu.VMEM(s, a.dtype) for s, a in zip(shapes, arrays))
        + tuple(jax.ShapeDtypeStruct(c.shape, c.dtype) for c in carries),
        in_specs=[HBM_SPEC] * count
        + [VMEM_SPEC] * carried
        + [pl.BlockSpec(memory_space=pl.ANY)] * len(after),
        out_specs=(VMEM_SPEC,) * (count + carried),
        scratch_shapes=[pltpu.SemaphoreType.DMA((count,))],
        compiler_params=pltpu.CompilerParams(vmem_limit_bytes=4 << 20),
        cost_estimate=pl.CostEstimate(
            flops=0, bytes_accessed=sum(2 * a.size for a in arrays), transcendentals=0
        ),
    )(*[pltpu.with_memory_space_constraint(a, pltpu.HBM) for a in arrays], *carries, *after)


def attend_kernel(lengths_ref, routes_ref, shares_ref, query_ref, cache_ref, out_ref):
    heads, tok, head_dim = query_ref.shape
    context = cache_ref.shape[1]
    span = heads // EXPERTS
    rows = heads * tok
    turned = query_ref[...].reshape(rows, head_dim).T
    lane_row = lax.rem(lax.broadcasted_iota(jnp.int32, (1, rows), 1), tok)
    position = lax.broadcasted_iota(jnp.int32, (context, rows), 0)
    scores = jnp.zeros((context, rows), F32)
    live = jnp.zeros((1, rows), jnp.int32)
    for row in range(tok):
        found = jnp.dot(cache_ref[row, :, :head_dim], turned, preferred_element_type=F32)
        scores = jnp.where(lane_row == row, found, scores)
        live = jnp.where(lane_row == row, lengths_ref[row], live)
    scores = jnp.where(position < live, scores * head_dim ** (-0.5), -1e30)
    weights = jnp.exp(scores - jnp.max(scores, axis=0, keepdims=True))
    prob = (weights / jnp.sum(weights, axis=0, keepdims=True)).T.astype(BF16)
    place = lax.broadcasted_iota(jnp.int32, (rows, 1), 0)
    place_row = lax.rem(place, tok)
    attended = jnp.zeros((rows, head_dim), F32)
    for row in range(tok):
        found = jnp.dot(prob, cache_ref[row, :, head_dim:], preferred_element_type=F32)
        attended = jnp.where(place_row == row, found, attended)
    out_ref[:, :, :head_dim] = attended.astype(BF16).reshape(heads, tok, head_dim)
    expert = place // (tok * span)
    gates = jnp.zeros((rows, 1), F32)
    for row in range(tok):
        for k in range(shares_ref.shape[0]):
            named = (place_row == row) & (expert == routes_ref[k, row])
            gates = gates + jnp.where(named, shares_ref[k, row], 0.0)
    out_ref[:, :, head_dim:] = (
        jnp.broadcast_to(gates, (rows, LANES)).astype(BF16).reshape(heads, tok, LANES)
    )


def attend(lengths, routes, shares, query_rows, cache):
    heads, tok, head_dim = query_rows.shape
    return pl.pallas_call(
        attend_kernel,
        out_shape=jax.ShapeDtypeStruct((heads, tok, head_dim + LANES), BF16),
        in_specs=[SMEM_SPEC] * 3 + [VMEM_SPEC] * 2,
        out_specs=VMEM_SPEC,
        compiler_params=pltpu.CompilerParams(vmem_limit_bytes=8 << 20),
    )(lengths, routes, shares, query_rows, cache)


def relative_order(chips):
    order, bit = [0], chips // 2
    while bit:
        order = order + [o ^ bit for o in order]
        bit //= 2
    return order


def project_kernel(place_ref, rows_ref, weight_ref, terms_ref, gates_ref, ordered):
    chips, _, tok, _ = rows_ref.shape
    head_dim = weight_ref.shape[0]
    for at, bits in enumerate(relative_order(chips)):
        ordered[at] = rows_ref[place_ref[0] ^ bits, place_ref[1]]
    block = ordered[...].reshape(chips * tok, head_dim + LANES)
    terms_ref[...] = jnp.dot(
        block[:, :head_dim], weight_ref[...], preferred_element_type=F32
    ).astype(terms_ref.dtype)
    gates_ref[...] = block[:, head_dim:]


def project(place, rows, weight, dtype):
    chips, _, tok, width = rows.shape
    half = chips * tok
    feature = weight.shape[1]
    return pl.pallas_call(
        project_kernel,
        out_shape=(
            jax.ShapeDtypeStruct((half, feature), dtype),
            jax.ShapeDtypeStruct((half, LANES), BF16),
        ),
        in_specs=[SMEM_SPEC, VMEM_SPEC, VMEM_SPEC],
        out_specs=(VMEM_SPEC, VMEM_SPEC),
        scratch_shapes=[pltpu.VMEM((chips, tok, width), BF16)],
        compiler_params=pltpu.CompilerParams(vmem_limit_bytes=8 << 20),
        cost_estimate=pl.CostEstimate(
            flops=2 * half * feature * weight.shape[0],
            bytes_accessed=2 * weight.size,
            transcendentals=0,
        ),
    )(place, rows, weight)


def norm_kernel(kept_ref, arrived_ref, gain_ref, middle_ref, normed_ref):
    tok = kept_ref.shape[0] // 2
    for block in range(2):
        mine = pl.ds(block * tok, tok)
        total = kept_ref[mine, :].astype(F32) + arrived_ref[1 - block].astype(F32)
        if block == 0:
            middle_ref[...] = total
        scale = lax.rsqrt(jnp.mean(total * total, axis=1, keepdims=True) + EPSILON)
        normed_ref[block] = (total * scale * gain_ref[...].reshape(1, -1)).astype(BF16)


def norm(kept, arrived, gain):
    rows, feature = kept.shape
    tok = rows // 2
    return pl.pallas_call(
        norm_kernel,
        out_shape=(
            jax.ShapeDtypeStruct((tok, feature), F32),
            jax.ShapeDtypeStruct((2, tok, feature), BF16),
        ),
        in_specs=[VMEM_SPEC] * 3,
        out_specs=(VMEM_SPEC, VMEM_SPEC),
        compiler_params=pltpu.CompilerParams(vmem_limit_bytes=4 << 20),
    )(kept, arrived.reshape(2, tok, feature), gain)


def expert_kernel(own_gates_ref, other_gates_ref, first_ref, second_ref, up_ref, low_ref, middle_ref, down_source, *refs):
    pieces, results, (turned, hidden, down_ref, sems) = refs[:-8], refs[-8:-4], refs[-4:]
    half = turned.shape[1] // 2
    units, feature = up_ref.shape
    wide = feature // 2

    first_unit = units - down_ref.shape[0]
    deep = tile_of(down_ref.shape[0], 128)
    copies = [
        pltpu.make_async_copy(
            down_source.at[pl.ds(first_unit + at, deep)], down_ref.at[pl.ds(at, deep)], sems.at[at // deep]
        )
        for at in range(0, down_ref.shape[0], deep)
    ]
    for copy in copies:
        copy.start()
    turned[...] = jnp.concatenate([piece[...] for piece in pieces], axis=0).T
    gates = jnp.concatenate([own_gates_ref[...], other_gates_ref[...]], axis=0)
    gates = gates.astype(F32).T[:1]
    part = first_ref.shape[0]
    step = tile_of(math.gcd(part, units - part), 384)
    for at in range(0, units, step):
        gate_ref, low = (first_ref, at) if at < part else (second_ref, at - part)
        rows = pl.ds(at, step)
        gate_pre = jnp.dot(
            gate_ref[pl.ds(low, step), :], turned[...], preferred_element_type=F32
        )
        up_pre = jnp.dot(up_ref[rows, :], turned[...], preferred_element_type=F32)
        product = gate_pre / (1.0 + jnp.exp(-gate_pre)) * up_pre * gates
        hidden[:, rows] = product.astype(BF16).T
    for copy in copies:
        copy.wait()
    for at in range(0, feature, wide):
        columns = pl.ds(at, wide)
        total, low = None, 0
        for ref in (low_ref, middle_ref, down_ref):
            units_here = pl.ds(low, ref.shape[0])
            term = jnp.dot(hidden[:, units_here], ref[:, columns], preferred_element_type=F32)
            total = term if total is None else total + term
            low += ref.shape[0]
        kept_ref, sent_ref = results[2 * (at // wide) : 2 * (at // wide) + 2]
        kept_ref[...] = total[:half]
        sent_ref[...] = total[half:].astype(BF16)


def experts(pieces, gates, held, down_weight):
    half = gates[0].shape[0]
    units, feature = down_weight.shape
    rest = units - held[3].shape[0] - held[4].shape[0]
    return pl.pallas_call(
        expert_kernel,
        out_shape=(
            jax.ShapeDtypeStruct((half, feature // 2), F32),
            jax.ShapeDtypeStruct((half, feature // 2), BF16),
        )
        * 2,
        in_specs=[VMEM_SPEC] * 7 + [HBM_SPEC] + [VMEM_SPEC] * len(pieces),
        out_specs=(VMEM_SPEC,) * 4,
        scratch_shapes=[
            pltpu.VMEM((feature, 2 * half), BF16),
            pltpu.VMEM((2 * half, units), BF16),
            pltpu.VMEM((rest, feature), BF16),
            pltpu.SemaphoreType.DMA((8,)),
        ],
        compiler_params=pltpu.CompilerParams(vmem_limit_bytes=16 << 20),
        cost_estimate=pl.CostEstimate(
            flops=12 * half * feature * units,
            bytes_accessed=6 * units * feature,
            transcendentals=2 * half * units,
        ),
    )(
        *gates,
        *held,
        pltpu.with_memory_space_constraint(down_weight, pltpu.HBM),
        *pieces,
    )


def local(
    queries,
    key_values,
    lengths,
    residual,
    routes,
    gate_weights,
    output_weight,
    norm_gain,
    gate_weight,
    up_weight,
    down_weight,
):
    tok = key_values.shape[0]
    head_dim = key_values.shape[2] // 2
    size = lax.axis_size("ep")
    chips = size // 2
    me = lax.axis_index("ep").astype(jnp.int32)
    place = jnp.stack([me // 2, me % 2])
    other_place = jnp.stack([me // 2, 1 - me % 2])

    def swap(x, bit):
        return lax.ppermute(x, "ep", [(i, i ^ bit) for i in range(size)])

    def sum_nearest(kept, arrived):
        quarter = kept.shape[0] // 4
        parts = [
            kept[at : at + quarter] + arrived[at : at + quarter].astype(F32)
            for at in range(0, 4 * quarter, quarter)
        ]
        kept = parts[0]
        for bits, part in ((6, parts[3]), (2, parts[2]), (4, parts[1])):
            kept = kept + swap(part.astype(BF16), bits).astype(F32)
        bit = 8
        while bit < chips:
            half = kept.shape[0] // 2
            kept = kept[:half] + swap(kept[half:].astype(BF16), bit).astype(F32)
            bit *= 2
        return kept

    cache, residual_held, gain_held, lengths_held, routes_held = fetch(
        key_values, residual, norm_gain, lengths, routes.T
    )
    query_rows = lax.all_to_all(
        queries.reshape(size, tok, head_dim), "ep", split_axis=0, concat_axis=0, tiled=True
    )
    attended = attend(lengths_held, routes_held, gate_weights.astype(F32).T, query_rows, cache)
    (output_held,) = fetch(output_weight, after=(attended,))
    head_rows = lax.all_to_all(attended, "ep", split_axis=0, concat_axis=0, tiled=True)
    head_rows = head_rows.reshape(chips, 2, tok, head_dim + LANES)
    sent, other_gates = project(other_place, head_rows, output_held, BF16)
    arrived = swap(sent, 1)
    kept, own_gates = project(place, head_rows, output_held, F32)
    kept = sum_nearest(kept, arrived)
    summed = kept.at[:tok].add(residual_held.astype(F32)).astype(BF16)
    bit = chips
    units = gate_weight.shape[0]
    part = units // LANES // 2 * LANES
    third = units // LANES // 3 * LANES
    up_held, first_held, low_held, gain_held = fetch(
        up_weight, (gate_weight, 0, part), (down_weight, 0, third), after=(summed,), carry=gain_held
    )
    middle, own = norm(summed, swap(summed, bit), gain_held)
    own = own.reshape(2 * tok, -1)
    bit //= 2
    while bit > 4:
        own = jnp.concatenate([own, swap(own, bit)], axis=0)
        bit //= 2
    others = [swap(own, bits) for bits in (4, 2, 6)]
    second_held, middle_held, own = fetch(
        (gate_weight, part, units - part), (down_weight, third, third), carry=own
    )
    pieces = [own] + others
    pieces = pieces + [swap(piece, 1) for piece in pieces]
    held = (first_held, second_held, up_held, low_held, middle_held)
    results = experts(pieces, (own_gates, other_gates), held, down_weight)
    combined = []
    for kept, sent in (results[:2], results[2:]):
        kept = sum_nearest(kept, swap(sent, 1))
        combined.append(kept[:tok] + swap(kept[tok:].astype(BF16), chips).astype(F32))
    return (middle + jnp.concatenate(combined, axis=1)).astype(BF16)


def solution(mesh):
    in_specs = (
        P("groups", "ep"),
        P(("groups", "ep"), None, None),
        P(("groups", "ep")),
        P(("groups", "ep"), None),
        P(("groups", "ep"), None),
        P(("groups", "ep"), None),
        P("ep", None),
        P(),
        P("ep", None),
        P("ep", None),
        P("ep", None),
    )
    out_specs = P(("groups", "ep"), None)
    return jax.shard_map(local, mesh=mesh, in_specs=in_specs, out_specs=out_specs, check_vma=False)
```

```python
import functools
import math

import jax
import jax.numpy as jnp
from jax import lax
from jax.experimental import pallas as pl
from jax.experimental.pallas import tpu as pltpu
from jax.sharding import PartitionSpec as P

EXPERTS = 8
EPSILON = 1e-05
LANES = 128
F32 = jnp.float32
BF16 = jnp.bfloat16
VMEM_SPEC = pl.BlockSpec(memory_space=pltpu.VMEM)
HBM_SPEC = pl.BlockSpec(memory_space=pltpu.HBM)
SMEM_SPEC = pl.BlockSpec(memory_space=pltpu.SMEM)


def tile_of(extent, most):
    return max(t for t in range(LANES, most + 1, LANES) if extent % t == 0)


def fetch_kernel(count, carried, ranges, *refs):
    sources, held, sems = refs[:count], refs[-count - 1 - carried : -1 - carried], refs[-1]
    copies = [
        pltpu.make_async_copy(source if rows is None else source.at[pl.ds(*rows)], target, sems.at[at])
        for at, (source, target, rows) in enumerate(zip(sources, held, ranges))
    ]
    for copy in copies:
        copy.start()
    if carried:
        refs[-2][...] = refs[count][...]
    for copy in copies:
        copy.wait()


def fetch(*arrays, after=(), carry=None):
    count, carried = len(arrays), int(carry is not None)
    carries = (carry,) * carried
    ranges = [a[1:] if isinstance(a, tuple) else None for a in arrays]
    arrays = [a[0] if isinstance(a, tuple) else a for a in arrays]
    shapes = [
        a.shape if rows is None else (rows[1],) + a.shape[1:] for a, rows in zip(arrays, ranges)
    ]
    return pl.pallas_call(
        functools.partial(fetch_kernel, count, carried, ranges),
        out_shape=tuple(pltpu.VMEM(s, a.dtype) for s, a in zip(shapes, arrays))
        + tuple(jax.ShapeDtypeStruct(c.shape, c.dtype) for c in carries),
        in_specs=[HBM_SPEC] * count
        + [VMEM_SPEC] * carried
        + [pl.BlockSpec(memory_space=pl.ANY)] * len(after),
        out_specs=(VMEM_SPEC,) * (count + carried),
        scratch_shapes=[pltpu.SemaphoreType.DMA((count,))],
        compiler_params=pltpu.CompilerParams(vmem_limit_bytes=4 << 20),
        cost_estimate=pl.CostEstimate(
            flops=0, bytes_accessed=sum(2 * a.size for a in arrays), transcendentals=0
        ),
    )(*[pltpu.with_memory_space_constraint(a, pltpu.HBM) for a in arrays], *carries, *after)


def attend_kernel(lengths_ref, routes_ref, shares_ref, query_ref, cache_ref, out_ref):
    heads, tok, head_dim = query_ref.shape
    context = cache_ref.shape[1]
    span = heads // EXPERTS
    rows = heads * tok
    turned = query_ref[...].reshape(rows, head_dim).T
    lane_row = lax.rem(lax.broadcasted_iota(jnp.int32, (1, rows), 1), tok)
    position = lax.broadcasted_iota(jnp.int32, (context, rows), 0)
    scores = jnp.zeros((context, rows), F32)
    live = jnp.zeros((1, rows), jnp.int32)
    for row in range(tok):
        found = jnp.dot(cache_ref[row, :, :head_dim], turned, preferred_element_type=F32)
        scores = jnp.where(lane_row == row, found, scores)
        live = jnp.where(lane_row == row, lengths_ref[row], live)
    scores = jnp.where(position < live, scores * head_dim ** (-0.5), -1e30)
    weights = jnp.exp(scores - jnp.max(scores, axis=0, keepdims=True))
    prob = (weights / jnp.sum(weights, axis=0, keepdims=True)).T.astype(BF16)
    place = lax.broadcasted_iota(jnp.int32, (rows, 1), 0)
    place_row = lax.rem(place, tok)
    attended = jnp.zeros((rows, head_dim), F32)
    for row in range(tok):
        found = jnp.dot(prob, cache_ref[row, :, head_dim:], preferred_element_type=F32)
        attended = jnp.where(place_row == row, found, attended)
    out_ref[:, :, :head_dim] = attended.astype(BF16).reshape(heads, tok, head_dim)
    expert = place // (tok * span)
    gates = jnp.zeros((rows, 1), F32)
    for row in range(tok):
        for k in range(shares_ref.shape[0]):
            named = (place_row == row) & (expert == routes_ref[k, row])
            gates = gates + jnp.where(named, shares_ref[k, row], 0.0)
    out_ref[:, :, head_dim:] = (
        jnp.broadcast_to(gates, (rows, LANES)).astype(BF16).reshape(heads, tok, LANES)
    )


def attend(lengths, routes, shares, query_rows, cache):
    heads, tok, head_dim = query_rows.shape
    return pl.pallas_call(
        attend_kernel,
        out_shape=jax.ShapeDtypeStruct((heads, tok, head_dim + LANES), BF16),
        in_specs=[SMEM_SPEC] * 3 + [VMEM_SPEC] * 2,
        out_specs=VMEM_SPEC,
        compiler_params=pltpu.CompilerParams(vmem_limit_bytes=8 << 20),
    )(lengths, routes, shares, query_rows, cache)


def relative_order(chips):
    order, bit = [0], chips // 2
    while bit:
        order = order + [o ^ bit for o in order]
        bit //= 2
    return order


def project_kernel(place_ref, rows_ref, weight_ref, terms_ref, gates_ref, ordered):
    chips, _, tok, _ = rows_ref.shape
    head_dim = weight_ref.shape[0]
    for at, bits in enumerate(relative_order(chips)):
        ordered[at] = rows_ref[place_ref[0] ^ bits, place_ref[1]]
    block = ordered[...].reshape(chips * tok, head_dim + LANES)
    terms_ref[...] = jnp.dot(
        block[:, :head_dim], weight_ref[...], preferred_element_type=F32
    ).astype(terms_ref.dtype)
    gates_ref[...] = block[:, head_dim:]


def project(place, rows, weight, dtype):
    chips, _, tok, width = rows.shape
    half = chips * tok
    feature = weight.shape[1]
    return pl.pallas_call(
        project_kernel,
        out_shape=(
            jax.ShapeDtypeStruct((half, feature), dtype),
            jax.ShapeDtypeStruct((half, LANES), BF16),
        ),
        in_specs=[SMEM_SPEC, VMEM_SPEC, VMEM_SPEC],
        out_specs=(VMEM_SPEC, VMEM_SPEC),
        scratch_shapes=[pltpu.VMEM((chips, tok, width), BF16)],
        compiler_params=pltpu.CompilerParams(vmem_limit_bytes=8 << 20),
        cost_estimate=pl.CostEstimate(
            flops=2 * half * feature * weight.shape[0],
            bytes_accessed=2 * weight.size,
            transcendentals=0,
        ),
    )(place, rows, weight)


def norm_kernel(kept_ref, arrived_ref, gain_ref, middle_ref, normed_ref):
    tok = kept_ref.shape[0] // 2
    for block in range(2):
        mine = pl.ds(block * tok, tok)
        total = kept_ref[mine, :].astype(F32) + arrived_ref[1 - block].astype(F32)
        if block == 0:
            middle_ref[...] = total
        scale = lax.rsqrt(jnp.mean(total * total, axis=1, keepdims=True) + EPSILON)
        normed_ref[block] = (total * scale * gain_ref[...].reshape(1, -1)).astype(BF16)


def norm(kept, arrived, gain):
    rows, feature = kept.shape
    tok = rows // 2
    return pl.pallas_call(
        norm_kernel,
        out_shape=(
            jax.ShapeDtypeStruct((tok, feature), F32),
            jax.ShapeDtypeStruct((2, tok, feature), BF16),
        ),
        in_specs=[VMEM_SPEC] * 3,
        out_specs=(VMEM_SPEC, VMEM_SPEC),
        compiler_params=pltpu.CompilerParams(vmem_limit_bytes=4 << 20),
    )(kept, arrived.reshape(2, tok, feature), gain)


def expert_kernel(own_gates_ref, other_gates_ref, first_ref, second_ref, up_ref, low_ref, middle_ref, down_source, *refs):
    pieces, results, (turned, hidden, down_ref, sems) = refs[:-8], refs[-8:-4], refs[-4:]
    half = turned.shape[1] // 2
    units, feature = up_ref.shape
    wide = feature // 2

    first_unit = units - down_ref.shape[0]
    deep = tile_of(down_ref.shape[0], 128)
    copies = [
        pltpu.make_async_copy(
            down_source.at[pl.ds(first_unit + at, deep)], down_ref.at[pl.ds(at, deep)], sems.at[at // deep]
        )
        for at in range(0, down_ref.shape[0], deep)
    ]
    for copy in copies:
        copy.start()
    turned[...] = jnp.concatenate([piece[...] for piece in pieces], axis=0).T
    gates = jnp.concatenate([own_gates_ref[...], other_gates_ref[...]], axis=0)
    gates = gates.astype(F32).T[:1]
    part = first_ref.shape[0]
    step = tile_of(math.gcd(part, units - part), 384)
    for at in range(0, units, step):
        gate_ref, low = (first_ref, at) if at < part else (second_ref, at - part)
        rows = pl.ds(at, step)
        gate_pre = jnp.dot(
            gate_ref[pl.ds(low, step), :], turned[...], preferred_element_type=F32
        )
        up_pre = jnp.dot(up_ref[rows, :], turned[...], preferred_element_type=F32)
        product = gate_pre / (1.0 + jnp.exp(-gate_pre)) * up_pre * gates
        hidden[:, rows] = product.astype(BF16).T
    for copy in copies:
        copy.wait()
    for at in range(0, feature, wide):
        columns = pl.ds(at, wide)
        total, low = None, 0
        for ref in (low_ref, middle_ref, down_ref):
            units_here = pl.ds(low, ref.shape[0])
            term = jnp.dot(hidden[:, units_here], ref[:, columns], preferred_element_type=F32)
            total = term if total is None else total + term
            low += ref.shape[0]
        kept_ref, sent_ref = results[2 * (at // wide) : 2 * (at // wide) + 2]
        kept_ref[...] = total[:half]
        sent_ref[...] = total[half:].astype(BF16)


def experts(pieces, gates, held, down_weight):
    half = gates[0].shape[0]
    units, feature = down_weight.shape
    rest = units - held[3].shape[0] - held[4].shape[0]
    return pl.pallas_call(
        expert_kernel,
        out_shape=(
            jax.ShapeDtypeStruct((half, feature // 2), F32),
            jax.ShapeDtypeStruct((half, feature // 2), BF16),
        )
        * 2,
        in_specs=[VMEM_SPEC] * 7 + [HBM_SPEC] + [VMEM_SPEC] * len(pieces),
        out_specs=(VMEM_SPEC,) * 4,
        scratch_shapes=[
            pltpu.VMEM((feature, 2 * half), BF16),
            pltpu.VMEM((2 * half, units), BF16),
            pltpu.VMEM((rest, feature), BF16),
            pltpu.SemaphoreType.DMA((8,)),
        ],
        compiler_params=pltpu.CompilerParams(vmem_limit_bytes=16 << 20),
        cost_estimate=pl.CostEstimate(
            flops=12 * half * feature * units,
            bytes_accessed=6 * units * feature,
            transcendentals=2 * half * units,
        ),
    )(
        *gates,
        *held,
        pltpu.with_memory_space_constraint(down_weight, pltpu.HBM),
        *pieces,
    )


def local(
    queries,
    key_values,
    lengths,
    residual,
    routes,
    gate_weights,
    output_weight,
    norm_gain,
    gate_weight,
    up_weight,
    down_weight,
):
    tok = key_values.shape[0]
    head_dim = key_values.shape[2] // 2
    size = lax.axis_size("ep")
    chips = size // 2
    me = lax.axis_index("ep").astype(jnp.int32)
    place = jnp.stack([me // 2, me % 2])
    other_place = jnp.stack([me // 2, 1 - me % 2])

    def swap(x, bit):
        return lax.ppermute(x, "ep", [(i, i ^ bit) for i in range(size)])

    def sum_nearest(kept, arrived):
        quarter = kept[0].shape[0] // 4
        parts = [
            jnp.concatenate(
                [
                    mine[at : at + quarter] + theirs[at : at + quarter].astype(F32)
                    for mine, theirs in zip(kept, arrived)
                ],
                axis=1,
            )
            for at in range(0, 4 * quarter, quarter)
        ]
        kept = parts[0]
        for bits, part in ((6, parts[3]), (2, parts[2]), (4, parts[1])):
            kept = kept + swap(part.astype(BF16), bits).astype(F32)
        bit = 8
        while bit < chips:
            half = kept.shape[0] // 2
            kept = kept[:half] + swap(kept[half:].astype(BF16), bit).astype(F32)
            bit *= 2
        return kept

    cache, residual_held, gain_held, lengths_held, routes_held = fetch(
        key_values, residual, norm_gain, lengths, routes.T
    )
    query_rows = lax.all_to_all(
        queries.reshape(size, tok, head_dim), "ep", split_axis=0, concat_axis=0, tiled=True
    )
    attended = attend(lengths_held, routes_held, gate_weights.astype(F32).T, query_rows, cache)
    (output_held,) = fetch(output_weight, after=(attended,))
    head_rows = lax.all_to_all(attended, "ep", split_axis=0, concat_axis=0, tiled=True)
    head_rows = head_rows.reshape(chips, 2, tok, head_dim + LANES)
    sent, other_gates = project(other_place, head_rows, output_held, BF16)
    arrived = swap(sent, 1)
    kept, own_gates = project(place, head_rows, output_held, F32)
    kept = sum_nearest([kept], [arrived])
    summed = kept.at[:tok].add(residual_held.astype(F32)).astype(BF16)
    bit = chips
    units = gate_weight.shape[0]
    part = units // LANES // 2 * LANES
    third = units // LANES // 3 * LANES
    up_held, first_held, low_held, gain_held = fetch(
        up_weight, (gate_weight, 0, part), (down_weight, 0, third), after=(summed,), carry=gain_held
    )
    middle, own = norm(summed, swap(summed, bit), gain_held)
    own = own.reshape(2 * tok, -1)
    bit //= 2
    while bit > 4:
        own = jnp.concatenate([own, swap(own, bit)], axis=0)
        bit //= 2
    others = [swap(own, bits) for bits in (4, 2, 6)]
    second_held, middle_held, own = fetch(
        (gate_weight, part, units - part), (down_weight, third, third), carry=own
    )
    pieces = [own] + others
    pieces = pieces + [swap(piece, 1) for piece in pieces]
    held = (first_held, second_held, up_held, low_held, middle_held)
    results = experts(pieces, (own_gates, other_gates), held, down_weight)
    kept = sum_nearest(results[::2], [swap(sent, 1) for sent in results[1::2]])
    combined = kept[:tok] + swap(kept[tok:].astype(BF16), chips).astype(F32)
    return (middle + combined).astype(BF16)


def solution(mesh):
    in_specs = (
        P("groups", "ep"),
        P(("groups", "ep"), None, None),
        P(("groups", "ep")),
        P(("groups", "ep"), None),
        P(("groups", "ep"), None),
        P(("groups", "ep"), None),
        P("ep", None),
        P(),
        P("ep", None),
        P("ep", None),
        P("ep", None),
    )
    out_specs = P(("groups", "ep"), None)
    return jax.shard_map(local, mesh=mesh, in_specs=in_specs, out_specs=out_specs, check_vma=False)
```

```python
import functools
import math

import jax
import jax.numpy as jnp
from jax import lax
from jax.experimental import pallas as pl
from jax.experimental.pallas import tpu as pltpu
from jax.sharding import PartitionSpec as P

EXPERTS = 8
EPSILON = 1e-05
LANES = 128
F32 = jnp.float32
BF16 = jnp.bfloat16
VMEM_SPEC = pl.BlockSpec(memory_space=pltpu.VMEM)
HBM_SPEC = pl.BlockSpec(memory_space=pltpu.HBM)
SMEM_SPEC = pl.BlockSpec(memory_space=pltpu.SMEM)


def tile_of(extent, most):
    return max(t for t in range(LANES, most + 1, LANES) if extent % t == 0)


def fetch_kernel(count, carried, ranges, *refs):
    sources, held, sems = refs[:count], refs[-count - 1 - carried : -1 - carried], refs[-1]
    copies = [
        pltpu.make_async_copy(source if rows is None else source.at[pl.ds(*rows)], target, sems.at[at])
        for at, (source, target, rows) in enumerate(zip(sources, held, ranges))
    ]
    for copy in copies:
        copy.start()
    if carried:
        refs[-2][...] = refs[count][...]
    for copy in copies:
        copy.wait()


def fetch(*arrays, after=(), carry=None):
    count, carried = len(arrays), int(carry is not None)
    carries = (carry,) * carried
    ranges = [a[1:] if isinstance(a, tuple) else None for a in arrays]
    arrays = [a[0] if isinstance(a, tuple) else a for a in arrays]
    shapes = [
        a.shape if rows is None else (rows[1],) + a.shape[1:] for a, rows in zip(arrays, ranges)
    ]
    return pl.pallas_call(
        functools.partial(fetch_kernel, count, carried, ranges),
        out_shape=tuple(pltpu.VMEM(s, a.dtype) for s, a in zip(shapes, arrays))
        + tuple(jax.ShapeDtypeStruct(c.shape, c.dtype) for c in carries),
        in_specs=[HBM_SPEC] * count
        + [VMEM_SPEC] * carried
        + [pl.BlockSpec(memory_space=pl.ANY)] * len(after),
        out_specs=(VMEM_SPEC,) * (count + carried),
        scratch_shapes=[pltpu.SemaphoreType.DMA((count,))],
        compiler_params=pltpu.CompilerParams(vmem_limit_bytes=4 << 20),
        cost_estimate=pl.CostEstimate(
            flops=0, bytes_accessed=sum(2 * a.size for a in arrays), transcendentals=0
        ),
    )(*[pltpu.with_memory_space_constraint(a, pltpu.HBM) for a in arrays], *carries, *after)


def attend_kernel(lengths_ref, routes_ref, shares_ref, query_ref, cache_ref, out_ref):
    heads, tok, head_dim = query_ref.shape
    context = cache_ref.shape[1]
    span = heads // EXPERTS
    rows = heads * tok
    turned = query_ref[...].reshape(rows, head_dim).T
    lane_row = lax.rem(lax.broadcasted_iota(jnp.int32, (1, rows), 1), tok)
    position = lax.broadcasted_iota(jnp.int32, (context, rows), 0)
    scores = jnp.zeros((context, rows), F32)
    live = jnp.zeros((1, rows), jnp.int32)
    for row in range(tok):
        found = jnp.dot(cache_ref[row, :, :head_dim], turned, preferred_element_type=F32)
        scores = jnp.where(lane_row == row, found, scores)
        live = jnp.where(lane_row == row, lengths_ref[row], live)
    scores = jnp.where(position < live, scores * head_dim ** (-0.5), -1e30)
    weights = jnp.exp(scores - jnp.max(scores, axis=0, keepdims=True))
    prob = (weights / jnp.sum(weights, axis=0, keepdims=True)).T.astype(BF16)
    place = lax.broadcasted_iota(jnp.int32, (rows, 1), 0)
    place_row = lax.rem(place, tok)
    attended = jnp.zeros((rows, head_dim), F32)
    for row in range(tok):
        found = jnp.dot(prob, cache_ref[row, :, head_dim:], preferred_element_type=F32)
        attended = jnp.where(place_row == row, found, attended)
    out_ref[:, :, :head_dim] = attended.astype(BF16).reshape(heads, tok, head_dim)
    expert = place // (tok * span)
    gates = jnp.zeros((rows, 1), F32)
    for row in range(tok):
        for k in range(shares_ref.shape[0]):
            named = (place_row == row) & (expert == routes_ref[k, row])
            gates = gates + jnp.where(named, shares_ref[k, row], 0.0)
    out_ref[:, :, head_dim:] = (
        jnp.broadcast_to(gates, (rows, LANES)).astype(BF16).reshape(heads, tok, LANES)
    )


def attend(lengths, routes, shares, query_rows, cache):
    heads, tok, head_dim = query_rows.shape
    return pl.pallas_call(
        attend_kernel,
        out_shape=jax.ShapeDtypeStruct((heads, tok, head_dim + LANES), BF16),
        in_specs=[SMEM_SPEC] * 3 + [VMEM_SPEC] * 2,
        out_specs=VMEM_SPEC,
        compiler_params=pltpu.CompilerParams(vmem_limit_bytes=8 << 20),
    )(lengths, routes, shares, query_rows, cache)


def relative_order(chips):
    order, bit = [0], chips // 2
    while bit:
        order = order + [o ^ bit for o in order]
        bit //= 2
    return order


def project_kernel(place_ref, rows_ref, weight_ref, terms_ref, gates_ref, ordered):
    chips, _, tok, _ = rows_ref.shape
    head_dim = weight_ref.shape[0]
    for at, bits in enumerate(relative_order(chips)):
        ordered[at] = rows_ref[place_ref[0] ^ bits, place_ref[1]]
    block = ordered[...].reshape(chips * tok, head_dim + LANES)
    terms_ref[...] = jnp.dot(
        block[:, :head_dim], weight_ref[...], preferred_element_type=F32
    ).astype(terms_ref.dtype)
    gates_ref[...] = block[:, head_dim:]


def project(place, rows, weight, dtype):
    chips, _, tok, width = rows.shape
    half = chips * tok
    feature = weight.shape[1]
    return pl.pallas_call(
        project_kernel,
        out_shape=(
            jax.ShapeDtypeStruct((half, feature), dtype),
            jax.ShapeDtypeStruct((half, LANES), BF16),
        ),
        in_specs=[SMEM_SPEC, VMEM_SPEC, VMEM_SPEC],
        out_specs=(VMEM_SPEC, VMEM_SPEC),
        scratch_shapes=[pltpu.VMEM((chips, tok, width), BF16)],
        compiler_params=pltpu.CompilerParams(vmem_limit_bytes=8 << 20),
        cost_estimate=pl.CostEstimate(
            flops=2 * half * feature * weight.shape[0],
            bytes_accessed=2 * weight.size,
            transcendentals=0,
        ),
    )(place, rows, weight)


def norm_kernel(kept_ref, arrived_ref, gain_ref, middle_ref, normed_ref):
    for block in range(2):
        total = kept_ref[block].astype(F32) + arrived_ref[1 - block].astype(F32)
        if block == 0:
            middle_ref[...] = total
        scale = lax.rsqrt(jnp.mean(total * total, axis=1, keepdims=True) + EPSILON)
        normed_ref[block] = (total * scale * gain_ref[...].reshape(1, -1)).astype(BF16)


def norm(kept, arrived, gain):
    rows, feature = kept.shape
    tok = rows // 2
    return pl.pallas_call(
        norm_kernel,
        out_shape=(
            jax.ShapeDtypeStruct((tok, feature), F32),
            jax.ShapeDtypeStruct((2, tok, feature), BF16),
        ),
        in_specs=[VMEM_SPEC] * 3,
        out_specs=(VMEM_SPEC, VMEM_SPEC),
        compiler_params=pltpu.CompilerParams(vmem_limit_bytes=4 << 20),
    )(kept.reshape(2, tok, feature), arrived.reshape(2, tok, feature), gain)


def expert_kernel(own_gates_ref, other_gates_ref, first_ref, second_ref, up_ref, low_ref, middle_ref, down_source, *refs):
    pieces, results, (turned, hidden, down_ref, sems) = refs[:-8], refs[-8:-4], refs[-4:]
    half = turned.shape[1] // 2
    units, feature = up_ref.shape
    wide = feature // 2

    first_unit = units - down_ref.shape[0]
    deep = tile_of(down_ref.shape[0], 128)
    copies = [
        pltpu.make_async_copy(
            down_source.at[pl.ds(first_unit + at, deep)], down_ref.at[pl.ds(at, deep)], sems.at[at // deep]
        )
        for at in range(0, down_ref.shape[0], deep)
    ]
    for copy in copies:
        copy.start()
    turned[...] = jnp.concatenate([piece[...] for piece in pieces], axis=0).T
    gates = jnp.concatenate([own_gates_ref[...], other_gates_ref[...]], axis=0)
    gates = gates.astype(F32).T[:1]
    part = first_ref.shape[0]
    step = tile_of(math.gcd(part, units - part), 384)
    for at in range(0, units, step):
        gate_ref, low = (first_ref, at) if at < part else (second_ref, at - part)
        rows = pl.ds(at, step)
        gate_pre = jnp.dot(
            gate_ref[pl.ds(low, step), :], turned[...], preferred_element_type=F32
        )
        up_pre = jnp.dot(up_ref[rows, :], turned[...], preferred_element_type=F32)
        product = gate_pre / (1.0 + jnp.exp(-gate_pre)) * up_pre * gates
        hidden[:, rows] = product.astype(BF16).T
    for copy in copies:
        copy.wait()
    for at in range(0, feature, wide):
        columns = pl.ds(at, wide)
        total, low = None, 0
        for ref in (low_ref, middle_ref, down_ref):
            units_here = pl.ds(low, ref.shape[0])
            term = jnp.dot(hidden[:, units_here], ref[:, columns], preferred_element_type=F32)
            total = term if total is None else total + term
            low += ref.shape[0]
        kept_ref, sent_ref = results[2 * (at // wide) : 2 * (at // wide) + 2]
        kept_ref[...] = total[:half]
        sent_ref[...] = total[half:].astype(BF16)


def experts(pieces, gates, held, down_weight):
    half = gates[0].shape[0]
    units, feature = down_weight.shape
    rest = units - held[3].shape[0] - held[4].shape[0]
    return pl.pallas_call(
        expert_kernel,
        out_shape=(
            jax.ShapeDtypeStruct((half, feature // 2), F32),
            jax.ShapeDtypeStruct((half, feature // 2), BF16),
        )
        * 2,
        in_specs=[VMEM_SPEC] * 7 + [HBM_SPEC] + [VMEM_SPEC] * len(pieces),
        out_specs=(VMEM_SPEC,) * 4,
        scratch_shapes=[
            pltpu.VMEM((feature, 2 * half), BF16),
            pltpu.VMEM((2 * half, units), BF16),
            pltpu.VMEM((rest, feature), BF16),
            pltpu.SemaphoreType.DMA((8,)),
        ],
        compiler_params=pltpu.CompilerParams(vmem_limit_bytes=16 << 20),
        cost_estimate=pl.CostEstimate(
            flops=12 * half * feature * units,
            bytes_accessed=6 * units * feature,
            transcendentals=2 * half * units,
        ),
    )(
        *gates,
        *held,
        pltpu.with_memory_space_constraint(down_weight, pltpu.HBM),
        *pieces,
    )


def local(
    queries,
    key_values,
    lengths,
    residual,
    routes,
    gate_weights,
    output_weight,
    norm_gain,
    gate_weight,
    up_weight,
    down_weight,
):
    tok = key_values.shape[0]
    head_dim = key_values.shape[2] // 2
    size = lax.axis_size("ep")
    chips = size // 2
    me = lax.axis_index("ep").astype(jnp.int32)
    place = jnp.stack([me // 2, me % 2])
    other_place = jnp.stack([me // 2, 1 - me % 2])

    def swap(x, bit):
        return lax.ppermute(x, "ep", [(i, i ^ bit) for i in range(size)])

    def sum_nearest(kept, arrived):
        quarter = kept[0].shape[0] // 4
        parts = [
            jnp.concatenate(
                [
                    mine[at : at + quarter] + theirs[at : at + quarter].astype(F32)
                    for mine, theirs in zip(kept, arrived)
                ],
                axis=1,
            )
            for at in range(0, 4 * quarter, quarter)
        ]
        kept = parts[0]
        for bits, part in ((6, parts[3]), (2, parts[2]), (4, parts[1])):
            kept = kept + swap(part.astype(BF16), bits).astype(F32)
        bit = 8
        while bit < chips:
            half = kept.shape[0] // 2
            kept = kept[:half] + swap(kept[half:].astype(BF16), bit).astype(F32)
            bit *= 2
        return kept

    cache, residual_held, gain_held, lengths_held, routes_held = fetch(
        key_values, residual, norm_gain, lengths, routes.T
    )
    query_rows = lax.all_to_all(
        queries.reshape(size, tok, head_dim), "ep", split_axis=0, concat_axis=0, tiled=True
    )
    attended = attend(lengths_held, routes_held, gate_weights.astype(F32).T, query_rows, cache)
    (output_held,) = fetch(output_weight, after=(attended,))
    head_rows = lax.all_to_all(attended, "ep", split_axis=0, concat_axis=0, tiled=True)
    head_rows = head_rows.reshape(chips, 2, tok, head_dim + LANES)
    sent, other_gates = project(other_place, head_rows, output_held, BF16)
    arrived = swap(sent, 1)
    kept, own_gates = project(place, head_rows, output_held, F32)
    kept = sum_nearest([kept], [arrived])
    summed = kept.at[:tok].add(residual_held.astype(F32)).astype(BF16)
    bit = chips
    units = gate_weight.shape[0]
    part = units // LANES // 2 * LANES
    third = units // LANES // 3 * LANES
    up_held, first_held, low_held, gain_held = fetch(
        up_weight, (gate_weight, 0, part), (down_weight, 0, third), after=(summed,), carry=gain_held
    )
    middle, own = norm(summed, swap(summed, bit), gain_held)
    own = own.reshape(2 * tok, -1)
    bit //= 2
    while bit > 4:
        own = jnp.concatenate([own, swap(own, bit)], axis=0)
        bit //= 2
    others = [swap(own, bits) for bits in (4, 2, 6)]
    second_held, middle_held, own = fetch(
        (gate_weight, part, units - part), (down_weight, third, third), carry=own
    )
    pieces = [own] + others
    pieces = pieces + [swap(piece, 1) for piece in pieces]
    held = (first_held, second_held, up_held, low_held, middle_held)
    results = experts(pieces, (own_gates, other_gates), held, down_weight)
    kept = sum_nearest(results[::2], [swap(sent, 1) for sent in results[1::2]])
    combined = kept[:tok] + swap(kept[tok:].astype(BF16), chips).astype(F32)
    return (middle + combined).astype(BF16)


def solution(mesh):
    in_specs = (
        P("groups", "ep"),
        P(("groups", "ep"), None, None),
        P(("groups", "ep")),
        P(("groups", "ep"), None),
        P(("groups", "ep"), None),
        P(("groups", "ep"), None),
        P("ep", None),
        P(),
        P("ep", None),
        P("ep", None),
        P("ep", None),
    )
    out_specs = P(("groups", "ep"), None)
    return jax.shard_map(local, mesh=mesh, in_specs=in_specs, out_specs=out_specs, check_vma=False)
```

```python
import functools
import math

import jax
import jax.numpy as jnp
from jax import lax
from jax.experimental import pallas as pl
from jax.experimental.pallas import tpu as pltpu
from jax.sharding import PartitionSpec as P

EXPERTS = 8
EPSILON = 1e-05
LANES = 128
F32 = jnp.float32
BF16 = jnp.bfloat16
VMEM_SPEC = pl.BlockSpec(memory_space=pltpu.VMEM)
HBM_SPEC = pl.BlockSpec(memory_space=pltpu.HBM)
SMEM_SPEC = pl.BlockSpec(memory_space=pltpu.SMEM)


def tile_of(extent, most):
    return max(t for t in range(LANES, most + 1, LANES) if extent % t == 0)


def fetch_kernel(count, carried, ranges, *refs):
    sources, held, sems = refs[:count], refs[-count - 1 - carried : -1 - carried], refs[-1]
    copies = [
        pltpu.make_async_copy(source if rows is None else source.at[pl.ds(*rows)], target, sems.at[at])
        for at, (source, target, rows) in enumerate(zip(sources, held, ranges))
    ]
    for copy in copies:
        copy.start()
    if carried:
        refs[-2][...] = refs[count][...]
    for copy in copies:
        copy.wait()


def fetch(*arrays, after=(), carry=None):
    count, carried = len(arrays), int(carry is not None)
    carries = (carry,) * carried
    ranges = [a[1:] if isinstance(a, tuple) else None for a in arrays]
    arrays = [a[0] if isinstance(a, tuple) else a for a in arrays]
    shapes = [
        a.shape if rows is None else (rows[1],) + a.shape[1:] for a, rows in zip(arrays, ranges)
    ]
    return pl.pallas_call(
        functools.partial(fetch_kernel, count, carried, ranges),
        out_shape=tuple(pltpu.VMEM(s, a.dtype) for s, a in zip(shapes, arrays))
        + tuple(jax.ShapeDtypeStruct(c.shape, c.dtype) for c in carries),
        in_specs=[HBM_SPEC] * count
        + [VMEM_SPEC] * carried
        + [pl.BlockSpec(memory_space=pl.ANY)] * len(after),
        out_specs=(VMEM_SPEC,) * (count + carried),
        scratch_shapes=[pltpu.SemaphoreType.DMA((count,))],
        compiler_params=pltpu.CompilerParams(vmem_limit_bytes=4 << 20),
        cost_estimate=pl.CostEstimate(
            flops=0, bytes_accessed=sum(2 * a.size for a in arrays), transcendentals=0
        ),
    )(*[pltpu.with_memory_space_constraint(a, pltpu.HBM) for a in arrays], *carries, *after)


def gate_kernel(tok, span, routes_ref, shares_ref, out_ref):
    rows = out_ref.shape[0]
    place = lax.broadcasted_iota(jnp.int32, (rows, 1), 0)
    place_row = lax.rem(place, tok)
    expert = place // (tok * span)
    gates = jnp.zeros((rows, 1), F32)
    for row in range(tok):
        for k in range(shares_ref.shape[0]):
            named = (place_row == row) & (expert == routes_ref[k, row])
            gates = gates + jnp.where(named, shares_ref[k, row], 0.0)
    out_ref[...] = jnp.broadcast_to(gates, (rows, LANES)).astype(BF16)


def gate_table(size, routes, shares):
    tok = routes.shape[1]
    return pl.pallas_call(
        functools.partial(gate_kernel, tok, size // EXPERTS),
        out_shape=jax.ShapeDtypeStruct((size * tok, LANES), BF16),
        in_specs=[SMEM_SPEC] * 2,
        out_specs=VMEM_SPEC,
        compiler_params=pltpu.CompilerParams(vmem_limit_bytes=4 << 20),
    )(routes, shares)


def attend_kernel(lengths_ref, gates_ref, query_ref, cache_ref, out_ref):
    heads, tok, head_dim = query_ref.shape
    context = cache_ref.shape[1]
    rows = heads * tok
    turned = query_ref[...].reshape(rows, head_dim).T
    lane_row = lax.rem(lax.broadcasted_iota(jnp.int32, (1, rows), 1), tok)
    position = lax.broadcasted_iota(jnp.int32, (context, rows), 0)
    scores = jnp.zeros((context, rows), F32)
    live = jnp.zeros((1, rows), jnp.int32)
    for row in range(tok):
        found = jnp.dot(cache_ref[row, :, :head_dim], turned, preferred_element_type=F32)
        scores = jnp.where(lane_row == row, found, scores)
        live = jnp.where(lane_row == row, lengths_ref[row], live)
    scores = jnp.where(position < live, scores * head_dim ** (-0.5), -1e30)
    weights = jnp.exp(scores - jnp.max(scores, axis=0, keepdims=True))
    prob = (weights / jnp.sum(weights, axis=0, keepdims=True)).T.astype(BF16)
    place = lax.broadcasted_iota(jnp.int32, (rows, 1), 0)
    place_row = lax.rem(place, tok)
    attended = jnp.zeros((rows, head_dim), F32)
    for row in range(tok):
        found = jnp.dot(prob, cache_ref[row, :, head_dim:], preferred_element_type=F32)
        attended = jnp.where(place_row == row, found, attended)
    out_ref[:, :, :head_dim] = attended.astype(BF16).reshape(heads, tok, head_dim)
    out_ref[:, :, head_dim:] = gates_ref[...].reshape(heads, tok, LANES)


def attend(lengths, gates, query_rows, cache):
    heads, tok, head_dim = query_rows.shape
    return pl.pallas_call(
        attend_kernel,
        out_shape=jax.ShapeDtypeStruct((heads, tok, head_dim + LANES), BF16),
        in_specs=[SMEM_SPEC] + [VMEM_SPEC] * 3,
        out_specs=VMEM_SPEC,
        compiler_params=pltpu.CompilerParams(vmem_limit_bytes=8 << 20),
    )(lengths, gates, query_rows, cache)


def relative_order(chips):
    order, bit = [0], chips // 2
    while bit:
        order = order + [o ^ bit for o in order]
        bit //= 2
    return order


def project_kernel(place_ref, rows_ref, weight_ref, terms_ref, gates_ref, ordered):
    chips, _, tok, _ = rows_ref.shape
    head_dim = weight_ref.shape[0]
    for at, bits in enumerate(relative_order(chips)):
        ordered[at] = rows_ref[place_ref[0] ^ bits, place_ref[1]]
    block = ordered[...].reshape(chips * tok, head_dim + LANES)
    terms_ref[...] = jnp.dot(
        block[:, :head_dim], weight_ref[...], preferred_element_type=F32
    ).astype(terms_ref.dtype)
    gates_ref[...] = block[:, head_dim:]


def project(place, rows, weight, dtype):
    chips, _, tok, width = rows.shape
    half = chips * tok
    feature = weight.shape[1]
    return pl.pallas_call(
        project_kernel,
        out_shape=(
            jax.ShapeDtypeStruct((half, feature), dtype),
            jax.ShapeDtypeStruct((half, LANES), BF16),
        ),
        in_specs=[SMEM_SPEC, VMEM_SPEC, VMEM_SPEC],
        out_specs=(VMEM_SPEC, VMEM_SPEC),
        scratch_shapes=[pltpu.VMEM((chips, tok, width), BF16)],
        compiler_params=pltpu.CompilerParams(vmem_limit_bytes=8 << 20),
        cost_estimate=pl.CostEstimate(
            flops=2 * half * feature * weight.shape[0],
            bytes_accessed=2 * weight.size,
            transcendentals=0,
        ),
    )(place, rows, weight)


def norm_kernel(kept_ref, arrived_ref, gain_ref, middle_ref, normed_ref):
    for block in range(2):
        total = kept_ref[block].astype(F32) + arrived_ref[1 - block].astype(F32)
        if block == 0:
            middle_ref[...] = total
        scale = lax.rsqrt(jnp.mean(total * total, axis=1, keepdims=True) + EPSILON)
        normed_ref[block] = (total * scale * gain_ref[...].reshape(1, -1)).astype(BF16)


def norm(kept, arrived, gain):
    rows, feature = kept.shape
    tok = rows // 2
    return pl.pallas_call(
        norm_kernel,
        out_shape=(
            jax.ShapeDtypeStruct((tok, feature), F32),
            jax.ShapeDtypeStruct((2, tok, feature), BF16),
        ),
        in_specs=[VMEM_SPEC] * 3,
        out_specs=(VMEM_SPEC, VMEM_SPEC),
        compiler_params=pltpu.CompilerParams(vmem_limit_bytes=4 << 20),
    )(kept.reshape(2, tok, feature), arrived.reshape(2, tok, feature), gain)


def expert_kernel(own_gates_ref, other_gates_ref, first_ref, second_ref, up_ref, low_ref, middle_ref, down_source, *refs):
    pieces, results, (turned, hidden, down_ref, sems) = refs[:-8], refs[-8:-4], refs[-4:]
    half = turned.shape[1] // 2
    units, feature = up_ref.shape
    wide = feature // 2

    first_unit = units - down_ref.shape[0]
    deep = tile_of(down_ref.shape[0], 128)
    copies = [
        pltpu.make_async_copy(
            down_source.at[pl.ds(first_unit + at, deep)], down_ref.at[pl.ds(at, deep)], sems.at[at // deep]
        )
        for at in range(0, down_ref.shape[0], deep)
    ]
    for copy in copies:
        copy.start()
    turned[...] = jnp.concatenate([piece[...] for piece in pieces], axis=0).T
    gates = jnp.concatenate([own_gates_ref[...], other_gates_ref[...]], axis=0)
    gates = gates.astype(F32).T[:1]
    part = first_ref.shape[0]
    step = tile_of(math.gcd(part, units - part), 384)
    for at in range(0, units, step):
        gate_ref, low = (first_ref, at) if at < part else (second_ref, at - part)
        rows = pl.ds(at, step)
        gate_pre = jnp.dot(
            gate_ref[pl.ds(low, step), :], turned[...], preferred_element_type=F32
        )
        up_pre = jnp.dot(up_ref[rows, :], turned[...], preferred_element_type=F32)
        product = gate_pre / (1.0 + jnp.exp(-gate_pre)) * up_pre * gates
        hidden[:, rows] = product.astype(BF16).T
    for copy in copies:
        copy.wait()
    for at in range(0, feature, wide):
        columns = pl.ds(at, wide)
        total, low = None, 0
        for ref in (low_ref, middle_ref, down_ref):
            units_here = pl.ds(low, ref.shape[0])
            term = jnp.dot(hidden[:, units_here], ref[:, columns], preferred_element_type=F32)
            total = term if total is None else total + term
            low += ref.shape[0]
        kept_ref, sent_ref = results[2 * (at // wide) : 2 * (at // wide) + 2]
        kept_ref[...] = total[:half]
        sent_ref[...] = total[half:].astype(BF16)


def experts(pieces, gates, held, down_weight):
    half = gates[0].shape[0]
    units, feature = down_weight.shape
    rest = units - held[3].shape[0] - held[4].shape[0]
    return pl.pallas_call(
        expert_kernel,
        out_shape=(
            jax.ShapeDtypeStruct((half, feature // 2), F32),
            jax.ShapeDtypeStruct((half, feature // 2), BF16),
        )
        * 2,
        in_specs=[VMEM_SPEC] * 7 + [HBM_SPEC] + [VMEM_SPEC] * len(pieces),
        out_specs=(VMEM_SPEC,) * 4,
        scratch_shapes=[
            pltpu.VMEM((feature, 2 * half), BF16),
            pltpu.VMEM((2 * half, units), BF16),
            pltpu.VMEM((rest, feature), BF16),
            pltpu.SemaphoreType.DMA((8,)),
        ],
        compiler_params=pltpu.CompilerParams(vmem_limit_bytes=16 << 20),
        cost_estimate=pl.CostEstimate(
            flops=12 * half * feature * units,
            bytes_accessed=6 * units * feature,
            transcendentals=2 * half * units,
        ),
    )(
        *gates,
        *held,
        pltpu.with_memory_space_constraint(down_weight, pltpu.HBM),
        *pieces,
    )


def local(
    queries,
    key_values,
    lengths,
    residual,
    routes,
    gate_weights,
    output_weight,
    norm_gain,
    gate_weight,
    up_weight,
    down_weight,
):
    tok = key_values.shape[0]
    head_dim = key_values.shape[2] // 2
    size = lax.axis_size("ep")
    chips = size // 2
    me = lax.axis_index("ep").astype(jnp.int32)
    place = jnp.stack([me // 2, me % 2])
    other_place = jnp.stack([me // 2, 1 - me % 2])

    def swap(x, bit):
        return lax.ppermute(x, "ep", [(i, i ^ bit) for i in range(size)])

    def sum_nearest(kept, arrived):
        quarter = kept[0].shape[0] // 4
        parts = [
            jnp.concatenate(
                [
                    mine[at : at + quarter] + theirs[at : at + quarter].astype(F32)
                    for mine, theirs in zip(kept, arrived)
                ],
                axis=1,
            )
            for at in range(0, 4 * quarter, quarter)
        ]
        kept = parts[0]
        for bits, part in ((6, parts[3]), (2, parts[2]), (4, parts[1])):
            kept = kept + swap(part.astype(BF16), bits).astype(F32)
        bit = 8
        while bit < chips:
            half = kept.shape[0] // 2
            kept = kept[:half] + swap(kept[half:].astype(BF16), bit).astype(F32)
            bit *= 2
        return kept

    cache, residual_held, gain_held, lengths_held, routes_held = fetch(
        key_values, residual, norm_gain, lengths, routes.T
    )
    gates = gate_table(size, routes_held, gate_weights.astype(F32).T)
    query_rows = lax.all_to_all(
        queries.reshape(size, tok, head_dim), "ep", split_axis=0, concat_axis=0, tiled=True
    )
    attended = attend(lengths_held, gates, query_rows, cache)
    (output_held,) = fetch(output_weight, after=(attended,))
    head_rows = lax.all_to_all(attended, "ep", split_axis=0, concat_axis=0, tiled=True)
    head_rows = head_rows.reshape(chips, 2, tok, head_dim + LANES)
    sent, other_gates = project(other_place, head_rows, output_held, BF16)
    arrived = swap(sent, 1)
    kept, own_gates = project(place, head_rows, output_held, F32)
    kept = sum_nearest([kept], [arrived])
    summed = kept.at[:tok].add(residual_held.astype(F32)).astype(BF16)
    bit = chips
    units = gate_weight.shape[0]
    part = units // LANES // 2 * LANES
    third = units // LANES // 3 * LANES
    up_held, first_held, low_held, gain_held = fetch(
        up_weight, (gate_weight, 0, part), (down_weight, 0, third), after=(summed,), carry=gain_held
    )
    middle, own = norm(summed, swap(summed, bit), gain_held)
    own = own.reshape(2 * tok, -1)
    bit //= 2
    while bit > 4:
        own = jnp.concatenate([own, swap(own, bit)], axis=0)
        bit //= 2
    others = [swap(own, bits) for bits in (4, 2, 6)]
    second_held, middle_held, own = fetch(
        (gate_weight, part, units - part), (down_weight, third, third), carry=own
    )
    pieces = [own] + others
    pieces = pieces + [swap(piece, 1) for piece in pieces]
    held = (first_held, second_held, up_held, low_held, middle_held)
    results = experts(pieces, (own_gates, other_gates), held, down_weight)
    kept = sum_nearest(results[::2], [swap(sent, 1) for sent in results[1::2]])
    combined = kept[:tok] + swap(kept[tok:].astype(BF16), chips).astype(F32)
    return (middle + combined).astype(BF16)


def solution(mesh):
    in_specs = (
        P("groups", "ep"),
        P(("groups", "ep"), None, None),
        P(("groups", "ep")),
        P(("groups", "ep"), None),
        P(("groups", "ep"), None),
        P(("groups", "ep"), None),
        P("ep", None),
        P(),
        P("ep", None),
        P("ep", None),
        P("ep", None),
    )
    out_specs = P(("groups", "ep"), None)
    return jax.shard_map(local, mesh=mesh, in_specs=in_specs, out_specs=out_specs, check_vma=False)
```

```python
import functools
import math

import jax
import jax.numpy as jnp
from jax import lax
from jax.experimental import pallas as pl
from jax.experimental.pallas import tpu as pltpu
from jax.sharding import PartitionSpec as P

EXPERTS = 8
EPSILON = 1e-05
LANES = 128
F32 = jnp.float32
BF16 = jnp.bfloat16
VMEM_SPEC = pl.BlockSpec(memory_space=pltpu.VMEM)
HBM_SPEC = pl.BlockSpec(memory_space=pltpu.HBM)
SMEM_SPEC = pl.BlockSpec(memory_space=pltpu.SMEM)


def tile_of(extent, most):
    return max(t for t in range(LANES, most + 1, LANES) if extent % t == 0)


def fetch_kernel(count, carried, ranges, *refs):
    sources, held, sems = refs[:count], refs[-count - 1 - carried : -1 - carried], refs[-1]
    copies = [
        pltpu.make_async_copy(source if rows is None else source.at[pl.ds(*rows)], target, sems.at[at])
        for at, (source, target, rows) in enumerate(zip(sources, held, ranges))
    ]
    for copy in copies:
        copy.start()
    if carried:
        refs[-2][...] = refs[count][...]
    for copy in copies:
        copy.wait()


def fetch(*arrays, after=(), carry=None):
    count, carried = len(arrays), int(carry is not None)
    carries = (carry,) * carried
    ranges = [a[1:] if isinstance(a, tuple) else None for a in arrays]
    arrays = [a[0] if isinstance(a, tuple) else a for a in arrays]
    shapes = [
        a.shape if rows is None else (rows[1],) + a.shape[1:] for a, rows in zip(arrays, ranges)
    ]
    return pl.pallas_call(
        functools.partial(fetch_kernel, count, carried, ranges),
        out_shape=tuple(pltpu.VMEM(s, a.dtype) for s, a in zip(shapes, arrays))
        + tuple(jax.ShapeDtypeStruct(c.shape, c.dtype) for c in carries),
        in_specs=[HBM_SPEC] * count
        + [VMEM_SPEC] * carried
        + [pl.BlockSpec(memory_space=pl.ANY)] * len(after),
        out_specs=(VMEM_SPEC,) * (count + carried),
        scratch_shapes=[pltpu.SemaphoreType.DMA((count,))],
        compiler_params=pltpu.CompilerParams(vmem_limit_bytes=4 << 20),
        cost_estimate=pl.CostEstimate(
            flops=0, bytes_accessed=sum(2 * a.size for a in arrays), transcendentals=0
        ),
    )(*[pltpu.with_memory_space_constraint(a, pltpu.HBM) for a in arrays], *carries, *after)


def attend_kernel(lengths_ref, routes_ref, shares_ref, query_ref, cache_ref, out_ref):
    heads, tok, head_dim = query_ref.shape
    context = cache_ref.shape[1]
    span = heads // EXPERTS
    rows = heads * tok
    turned = query_ref[...].reshape(rows, head_dim).T
    lane_row = lax.rem(lax.broadcasted_iota(jnp.int32, (1, rows), 1), tok)
    position = lax.broadcasted_iota(jnp.int32, (context, rows), 0)
    scores = jnp.zeros((context, rows), F32)
    live = jnp.zeros((1, rows), jnp.int32)
    for row in range(tok):
        found = jnp.dot(cache_ref[row, :, :head_dim], turned, preferred_element_type=F32)
        scores = jnp.where(lane_row == row, found, scores)
        live = jnp.where(lane_row == row, lengths_ref[row], live)
    scores = jnp.where(position < live, scores * head_dim ** (-0.5), -1e30)
    weights = jnp.exp(scores - jnp.max(scores, axis=0, keepdims=True))
    prob = (weights / jnp.sum(weights, axis=0, keepdims=True)).T.astype(BF16)
    place = lax.broadcasted_iota(jnp.int32, (rows, 1), 0)
    place_row = lax.rem(place, tok)
    attended = jnp.zeros((rows, head_dim), F32)
    for row in range(tok):
        found = jnp.dot(prob, cache_ref[row, :, head_dim:], preferred_element_type=F32)
        attended = jnp.where(place_row == row, found, attended)
    out_ref[:, :, :head_dim] = attended.astype(BF16).reshape(heads, tok, head_dim)
    expert = place // (tok * span)
    gates = jnp.zeros((rows, 1), F32)
    for row in range(tok):
        for k in range(shares_ref.shape[0]):
            named = (place_row == row) & (expert == routes_ref[k, row])
            gates = gates + jnp.where(named, shares_ref[k, row], 0.0)
    out_ref[:, :, head_dim:] = (
        jnp.broadcast_to(gates, (rows, LANES)).astype(BF16).reshape(heads, tok, LANES)
    )


def attend(lengths, routes, shares, query_rows, cache):
    heads, tok, head_dim = query_rows.shape
    return pl.pallas_call(
        attend_kernel,
        out_shape=jax.ShapeDtypeStruct((heads, tok, head_dim + LANES), BF16),
        in_specs=[SMEM_SPEC] * 3 + [VMEM_SPEC] * 2,
        out_specs=VMEM_SPEC,
        compiler_params=pltpu.CompilerParams(vmem_limit_bytes=8 << 20),
    )(lengths, routes, shares, query_rows, cache)


def relative_order(chips):
    order, bit = [0], chips // 2
    while bit:
        order = order + [o ^ bit for o in order]
        bit //= 2
    return order


def project_kernel(place_ref, rows_ref, weight_ref, left_ref, right_ref, gates_ref, ordered):
    chips, _, tok, _ = rows_ref.shape
    head_dim = weight_ref.shape[0]
    for at, bits in enumerate(relative_order(chips)):
        ordered[at] = rows_ref[place_ref[0] ^ bits, place_ref[1]]
    block = ordered[...].reshape(chips * tok, head_dim + LANES)
    wide = left_ref.shape[1]
    for at, terms_ref in enumerate((left_ref, right_ref)):
        terms_ref[...] = jnp.dot(
            block[:, :head_dim],
            weight_ref[:, pl.ds(at * wide, wide)],
            preferred_element_type=F32,
        ).astype(terms_ref.dtype)
    gates_ref[...] = block[:, head_dim:]


def project(place, rows, weight, dtype):
    chips, _, tok, width = rows.shape
    half = chips * tok
    feature = weight.shape[1]
    return pl.pallas_call(
        project_kernel,
        out_shape=(
            jax.ShapeDtypeStruct((half, feature // 2), dtype),
            jax.ShapeDtypeStruct((half, feature // 2), dtype),
            jax.ShapeDtypeStruct((half, LANES), BF16),
        ),
        in_specs=[SMEM_SPEC, VMEM_SPEC, VMEM_SPEC],
        out_specs=(VMEM_SPEC,) * 3,
        scratch_shapes=[pltpu.VMEM((chips, tok, width), BF16)],
        compiler_params=pltpu.CompilerParams(vmem_limit_bytes=8 << 20),
        cost_estimate=pl.CostEstimate(
            flops=2 * half * feature * weight.shape[0],
            bytes_accessed=2 * weight.size,
            transcendentals=0,
        ),
    )(place, rows, weight)


def norm_kernel(kept_ref, arrived_ref, gain_ref, middle_ref, normed_ref):
    for block in range(2):
        total = kept_ref[block].astype(F32) + arrived_ref[1 - block].astype(F32)
        if block == 0:
            middle_ref[...] = total
        scale = lax.rsqrt(jnp.mean(total * total, axis=1, keepdims=True) + EPSILON)
        normed_ref[block] = (total * scale * gain_ref[...].reshape(1, -1)).astype(BF16)


def norm(kept, arrived, gain):
    rows, feature = kept.shape
    tok = rows // 2
    return pl.pallas_call(
        norm_kernel,
        out_shape=(
            jax.ShapeDtypeStruct((tok, feature), F32),
            jax.ShapeDtypeStruct((2, tok, feature), BF16),
        ),
        in_specs=[VMEM_SPEC] * 3,
        out_specs=(VMEM_SPEC, VMEM_SPEC),
        compiler_params=pltpu.CompilerParams(vmem_limit_bytes=4 << 20),
    )(kept.reshape(2, tok, feature), arrived.reshape(2, tok, feature), gain)


def expert_kernel(own_gates_ref, other_gates_ref, first_ref, second_ref, up_ref, low_ref, middle_ref, down_source, *refs):
    pieces, results, (turned, hidden, down_ref, sems) = refs[:-8], refs[-8:-4], refs[-4:]
    half = turned.shape[1] // 2
    units, feature = up_ref.shape
    wide = feature // 2

    first_unit = units - down_ref.shape[0]
    deep = tile_of(down_ref.shape[0], 128)
    copies = [
        pltpu.make_async_copy(
            down_source.at[pl.ds(first_unit + at, deep)], down_ref.at[pl.ds(at, deep)], sems.at[at // deep]
        )
        for at in range(0, down_ref.shape[0], deep)
    ]
    for copy in copies:
        copy.start()
    turned[...] = jnp.concatenate([piece[...] for piece in pieces], axis=0).T
    gates = jnp.concatenate([own_gates_ref[...], other_gates_ref[...]], axis=0)
    gates = gates.astype(F32).T[:1]
    part = first_ref.shape[0]
    step = tile_of(math.gcd(part, units - part), 384)
    for at in range(0, units, step):
        gate_ref, low = (first_ref, at) if at < part else (second_ref, at - part)
        rows = pl.ds(at, step)
        gate_pre = jnp.dot(
            gate_ref[pl.ds(low, step), :], turned[...], preferred_element_type=F32
        )
        up_pre = jnp.dot(up_ref[rows, :], turned[...], preferred_element_type=F32)
        product = gate_pre / (1.0 + jnp.exp(-gate_pre)) * up_pre * gates
        hidden[:, rows] = product.astype(BF16).T
    for copy in copies:
        copy.wait()
    for at in range(0, feature, wide):
        columns = pl.ds(at, wide)
        total, low = None, 0
        for ref in (low_ref, middle_ref, down_ref):
            units_here = pl.ds(low, ref.shape[0])
            term = jnp.dot(hidden[:, units_here], ref[:, columns], preferred_element_type=F32)
            total = term if total is None else total + term
            low += ref.shape[0]
        kept_ref, sent_ref = results[2 * (at // wide) : 2 * (at // wide) + 2]
        kept_ref[...] = total[:half]
        sent_ref[...] = total[half:].astype(BF16)


def experts(pieces, gates, held, down_weight):
    half = gates[0].shape[0]
    units, feature = down_weight.shape
    rest = units - held[3].shape[0] - held[4].shape[0]
    return pl.pallas_call(
        expert_kernel,
        out_shape=(
            jax.ShapeDtypeStruct((half, feature // 2), F32),
            jax.ShapeDtypeStruct((half, feature // 2), BF16),
        )
        * 2,
        in_specs=[VMEM_SPEC] * 7 + [HBM_SPEC] + [VMEM_SPEC] * len(pieces),
        out_specs=(VMEM_SPEC,) * 4,
        scratch_shapes=[
            pltpu.VMEM((feature, 2 * half), BF16),
            pltpu.VMEM((2 * half, units), BF16),
            pltpu.VMEM((rest, feature), BF16),
            pltpu.SemaphoreType.DMA((8,)),
        ],
        compiler_params=pltpu.CompilerParams(vmem_limit_bytes=16 << 20),
        cost_estimate=pl.CostEstimate(
            flops=12 * half * feature * units,
            bytes_accessed=6 * units * feature,
            transcendentals=2 * half * units,
        ),
    )(
        *gates,
        *held,
        pltpu.with_memory_space_constraint(down_weight, pltpu.HBM),
        *pieces,
    )


def local(
    queries,
    key_values,
    lengths,
    residual,
    routes,
    gate_weights,
    output_weight,
    norm_gain,
    gate_weight,
    up_weight,
    down_weight,
):
    tok = key_values.shape[0]
    head_dim = key_values.shape[2] // 2
    size = lax.axis_size("ep")
    chips = size // 2
    me = lax.axis_index("ep").astype(jnp.int32)
    place = jnp.stack([me // 2, me % 2])
    other_place = jnp.stack([me // 2, 1 - me % 2])

    def swap(x, bit):
        return lax.ppermute(x, "ep", [(i, i ^ bit) for i in range(size)])

    def sum_nearest(kept, arrived):
        quarter = kept[0].shape[0] // 4
        parts = [
            jnp.concatenate(
                [
                    mine[at : at + quarter] + theirs[at : at + quarter].astype(F32)
                    for mine, theirs in zip(kept, arrived)
                ],
                axis=1,
            )
            for at in range(0, 4 * quarter, quarter)
        ]
        kept = parts[0]
        for bits, part in ((6, parts[3]), (2, parts[2]), (4, parts[1])):
            kept = kept + swap(part.astype(BF16), bits).astype(F32)
        bit = 8
        while bit < chips:
            half = kept.shape[0] // 2
            kept = kept[:half] + swap(kept[half:].astype(BF16), bit).astype(F32)
            bit *= 2
        return kept

    cache, residual_held, gain_held, lengths_held, routes_held = fetch(
        key_values, residual, norm_gain, lengths, routes.T
    )
    query_rows = lax.all_to_all(
        queries.reshape(size, tok, head_dim), "ep", split_axis=0, concat_axis=0, tiled=True
    )
    attended = attend(lengths_held, routes_held, gate_weights.astype(F32).T, query_rows, cache)
    (output_held,) = fetch(output_weight, after=(attended,))
    head_rows = lax.all_to_all(attended, "ep", split_axis=0, concat_axis=0, tiled=True)
    head_rows = head_rows.reshape(chips, 2, tok, head_dim + LANES)
    *sent, other_gates = project(other_place, head_rows, output_held, BF16)
    arrived = [swap(terms, 1) for terms in sent]
    *kept, own_gates = project(place, head_rows, output_held, F32)
    kept = sum_nearest(kept, arrived)
    summed = kept.at[:tok].add(residual_held.astype(F32)).astype(BF16)
    bit = chips
    units = gate_weight.shape[0]
    part = units // LANES // 2 * LANES
    third = units // LANES // 3 * LANES
    up_held, first_held, low_held, gain_held = fetch(
        up_weight, (gate_weight, 0, part), (down_weight, 0, third), after=(summed,), carry=gain_held
    )
    middle, own = norm(summed, swap(summed, bit), gain_held)
    own = own.reshape(2 * tok, -1)
    bit //= 2
    while bit > 4:
        own = jnp.concatenate([own, swap(own, bit)], axis=0)
        bit //= 2
    others = [swap(own, bits) for bits in (4, 2, 6)]
    second_held, middle_held, own = fetch(
        (gate_weight, part, units - part), (down_weight, third, third), carry=own
    )
    pieces = [own] + others
    pieces = pieces + [swap(piece, 1) for piece in pieces]
    held = (first_held, second_held, up_held, low_held, middle_held)
    results = experts(pieces, (own_gates, other_gates), held, down_weight)
    kept = sum_nearest(results[::2], [swap(sent, 1) for sent in results[1::2]])
    combined = kept[:tok] + swap(kept[tok:].astype(BF16), chips).astype(F32)
    return (middle + combined).astype(BF16)


def solution(mesh):
    in_specs = (
        P("groups", "ep"),
        P(("groups", "ep"), None, None),
        P(("groups", "ep")),
        P(("groups", "ep"), None),
        P(("groups", "ep"), None),
        P(("groups", "ep"), None),
        P("ep", None),
        P(),
        P("ep", None),
        P("ep", None),
        P("ep", None),
    )
    out_specs = P(("groups", "ep"), None)
    return jax.shard_map(local, mesh=mesh, in_specs=in_specs, out_specs=out_specs, check_vma=False)
```
